256 devices in a mesh: row: 32 (over y, z_lo, x), col: 8 (over z_hi, core).
Axes of the slice: x: 4, y: 4, z: 8 (z_hi: 4, z_lo: 2; z = z_hi * 2 + z_lo), core: 2. Of those that a mesh axis runs over, the one named last changes fastest.
Arguments:
- images: bfloat16 [20480, 1152], P(('row', 'col'))
- texts: bfloat16 [20480, 1152], P(('row', 'col'))
- image_ids: int32 [20480], replicated, may hold values from 0 to 10239, as said below
- text_ids: int32 [20480], replicated, may hold values from 0 to 10239, as said below
- temp_log: float32 [1], replicated, may hold values from 1.6 to 2.7
- bias: float32 [1], replicated, may hold values from -9 to -7
Outputs:
- image_grad: bfloat16 [20480, 1152], P(('row', 'col'))
- text_grad: bfloat16 [20480, 1152], P(('row', 'col'))
- scalars: float32 [3], replicated
The draws below stay inside these ranges and needn't reach their ends.
Inputs may be any that keep to these rules, and one draw needn't show every extreme that they name: `image_ids`: every identity names exactly two image rows and exactly two text rows. `text_ids`: the text identities are a reordering of the image identities.
All inputs are finite; a program needn't handle non-finite values.
Results may differ from the reference program's by a relative error of at most 0.0035.
Values may be sent and summed in bfloat16 or wider, within the bound.
No kernel may reach another device: no remote copies, remote signals or barrier semaphores. Data moves between devices by JAX's collectives and lax.ppermute only.
A program may use at most 64 MiB of HBM per device.

```python
import math
import jax
import jax.numpy as jnp
from jax import lax

D = 1152
BATCH = 20480


cluster_count = 16


def pair_ids(key):
    base = jax.random.permutation(jax.random.fold_in(key, 101), BATCH).astype(jnp.int32) // 2
    order = jax.random.permutation(jax.random.fold_in(key, 102), BATCH)
    return (base, base[order])


def shared_parts(key, low, high):
    table = jax.random.normal(jax.random.fold_in(key, 103), (cluster_count, D), jnp.float32)
    member = jax.random.randint(jax.random.fold_in(key, 104), (BATCH // 2,), 0, cluster_count)
    strength = jax.random.uniform(jax.random.fold_in(key, 105), (BATCH // 2,), jnp.float32, low, high)
    latent = jax.random.normal(jax.random.fold_in(key, 106), (BATCH // 2, D), jnp.float32)
    return strength[:, None] * table[member] + 0.6 * latent


def embed_rows(key, ids, pair_part, spread, ramp):
    gauss = jax.random.normal(jax.random.fold_in(key, 1), (BATCH, D), jnp.float32)
    noise = gauss
    lifts = jnp.exp(jax.random.uniform(jax.random.fold_in(key, 3), (BATCH, 1), jnp.float32, 0.0, spread))
    rows = pair_part[ids] * ramp[:, None] + 0.6 * noise
    return (rows * lifts / math.sqrt(D)).astype(jnp.bfloat16)


def draw_image_ids(key, part):
    image_ids, text_ids = pair_ids(key)
    return image_ids


def draw_text_ids(key, part):
    image_ids, text_ids = pair_ids(key)
    return text_ids


def draw_images(key, part):
    low, high, spread = (0.3, 0.8, 0.0)
    start, rise = (0.2, 1.6)
    image_ids, text_ids = pair_ids(key)
    pair_part = shared_parts(key, low, high)
    key = jax.random.fold_in(key, 5)
    ramp = start + rise * jnp.arange(BATCH, dtype=jnp.float32) / BATCH
    return embed_rows(key, image_ids, pair_part, spread, ramp)


def draw_texts(key, part):
    low, high, spread = (0.3, 0.8, 0.0)
    image_ids, text_ids = pair_ids(key)
    pair_part = shared_parts(key, low, high)
    key = jax.random.fold_in(key, 6)
    ramp = jnp.ones((BATCH,), jnp.float32)
    return embed_rows(key, text_ids, pair_part, spread, ramp)


def setup_inputs(seed: int = 0) -> dict:
    streams_of = jax.random.split(jax.random.key(seed), 7)
    return {
        "images": draw_images(jax.random.fold_in(streams_of[6], 71), 0),
        "texts": draw_texts(jax.random.fold_in(streams_of[6], 71), 0),
        "image_ids": draw_image_ids(jax.random.fold_in(streams_of[6], 71), 0),
        "text_ids": draw_text_ids(jax.random.fold_in(streams_of[6], 71), 0),
        "temp_log": jnp.clip(jax.random.uniform(streams_of[4], (1,), jnp.float32, 1.6, 2.7), 1.6, 2.7),
        "bias": jnp.clip(jax.random.uniform(streams_of[5], (1,), jnp.float32, -9.0, -7.0), -9.0, -7.0),
    }


def normalize(rows):
    return rows * lax.rsqrt(lax.optimization_barrier(jnp.sum(rows * rows, axis=1, keepdims=True)) + 1e-06)

def reference(images, texts, image_ids, text_ids, temp_log, bias):
    scale = jnp.exp(temp_log[0])
    shift = bias[0]
    ximg, img_back = jax.vjp(normalize, images.astype(jnp.float32))
    xtxt, txt_back = jax.vjp(normalize, texts.astype(jnp.float32))
    xn = ximg.astype(jnp.bfloat16)
    yn = xtxt.astype(jnp.bfloat16)
    block = math.gcd(512, BATCH)
    xs = (xn.reshape(BATCH // block, block, D), image_ids.reshape(BATCH // block, block))

    def step(carry, item):
        text_acc, stats = carry
        rows, labels = item
        logits = scale * jnp.dot(rows, yn.T, preferred_element_type=jnp.float32) + shift
        sign = jnp.where(labels[:, None] == text_ids[None, :], 1.0, -1.0).astype(jnp.float32)
        grad = -sign * jax.nn.sigmoid(-sign * logits)
        part = jnp.stack([jnp.sum(jax.nn.softplus(-sign * logits)), jnp.sum(grad * (logits - shift)), jnp.sum(grad)])
        grad_b = grad.astype(jnp.bfloat16)
        gx = scale * jnp.dot(grad_b, yn, preferred_element_type=jnp.float32)
        gy = scale * lax.dot_general(grad_b, rows, (((0,), (0,)), ((), ())), preferred_element_type=jnp.float32)
        return ((text_acc + gy, stats + part), gx)
    init = (jnp.zeros((BATCH, D), jnp.float32), jnp.zeros((3,), jnp.float32))
    (gyn, stats), gx_blocks = lax.scan(step, init, xs)
    gxn = gx_blocks.reshape(BATCH, D)
    image_grad = img_back(gxn)[0].astype(jnp.bfloat16)
    text_grad = txt_back(gyn)[0].astype(jnp.bfloat16)
    return (image_grad, text_grad, stats / BATCH)
```

```python
import itertools
import jax
import jax.numpy as jnp
from jax import lax
from jax.sharding import PartitionSpec as P

NX, NY, NZ, NC = 4, 4, 8, 2


def linear(x, y, z, c):
    return (((y * 2 + z % 2) * NX + x) * (NZ // 2) + z // 2) * NC + c


def hop(a, dx=0, dy=0, dz=0, dc=0):
    pairs = [
        (linear(x, y, z, c), linear((x + dx) % NX, (y + dy) % NY, (z + dz) % NZ, (c + dc) % NC))
        for x, y, z, c in itertools.product(range(NX), range(NY), range(NZ), range(NC))
    ]
    return lax.ppermute(a, ("row", "col"), pairs)


def normalize(rows):
    return rows * lax.rsqrt(jnp.sum(rows * rows, axis=1, keepdims=True) + 1e-06)


def dot_t(a, b):
    return lax.dot_general(a, b, (((1,), (1,)), ((), ())), preferred_element_type=jnp.float32)


def tile_grad(image_block, image_labels, text_block, text_labels, scale, shift):
    logits = scale * dot_t(image_block, text_block) + shift
    sign = jnp.where(image_labels[:, None] == text_labels[None, :], 1.0, -1.0).astype(jnp.float32)
    grad = -sign * jax.nn.sigmoid(-sign * logits)
    stats = jnp.stack(
        [jnp.sum(jax.nn.softplus(-sign * logits)), jnp.sum(grad * (logits - shift)), jnp.sum(grad)]
    )
    return grad.astype(jnp.bfloat16), stats


def gather_images(xn, half):
    by_x = [hop(xn, dx=k) for k in (1, 2, 3)]
    by_y = [hop(xn, dy=j) for j in (1, 2, 3)]
    tops = jnp.concatenate([b[:half] for b in by_x], 0)
    ends = jnp.concatenate([b[half:] for b in by_y], 0)
    tops = [hop(tops, dy=j) for j in (1, 2, 3)]
    ends = [hop(ends, dx=k) for k in (1, 2, 3)]
    return [xn] + by_x + by_y + tops + ends


def image_rows(ids, x, y, half):
    at = lambda k, j: ids[(y - j) % NY, (x - k) % NX]
    out = [at(0, 0)] + [at(k, 0) for k in (1, 2, 3)] + [at(0, j) for j in (1, 2, 3)]
    out += [at(k, j)[:half] for j in (1, 2, 3) for k in (1, 2, 3)]
    out += [at(k, j)[half:] for k in (1, 2, 3) for j in (1, 2, 3)]
    return jnp.concatenate(out, 0)


Z_ORDER = (0, 1, -1, 2, -2, 3, -3, 4)


def gather_texts(yn):
    up = down = yn
    own = [yn]
    for step in range(1, 5):
        up = hop(up, dz=1)
        own.append(up)
        if step < 4:
            down = hop(down, dz=-1)
            own.append(down)
    own = jnp.concatenate(own, 0)
    return jnp.concatenate([own, hop(own, dc=1)], 0)


def text_rows(ids, z, c):
    at = lambda dz, dc: ids[(z - dz) % NZ, (c + dc) % NC]
    return jnp.concatenate([at(dz, dc) for dc in (0, 1) for dz in Z_ORDER], 0)


def scatter_texts(gy, owned):
    mine, other = gy[: NZ * owned], gy[NZ * owned :]
    mine = mine + hop(other.astype(jnp.bfloat16), dc=1).astype(jnp.float32)
    parts = mine.astype(jnp.bfloat16).reshape(NZ, owned, -1)
    total = mine[:owned]
    for i, dz in reversed(list(enumerate(Z_ORDER))):
        if dz:
            total = total + hop(parts[i], dz=-dz).astype(jnp.float32)
    return total


def scatter_images(gx, owned, half):
    f32, bf16 = jnp.float32, jnp.bfloat16
    own = gx[:owned]
    by_x = [gx[owned * k : owned * (k + 1)] for k in (1, 2, 3)]
    by_y = [gx[owned * k : owned * (k + 1)] for k in (4, 5, 6)]
    rest = gx[owned * 7 :].reshape(6, 3 * half, -1).astype(bf16)
    tops = sum(hop(rest[j - 1], dy=-j).astype(f32) for j in (1, 2, 3))
    ends = sum(hop(rest[2 + k], dx=-k).astype(f32) for k in (1, 2, 3))
    for k in (1, 2, 3):
        i = k - 1
        top = by_x[i][:half] + tops[i * half : (i + 1) * half]
        own = own + hop(jnp.concatenate([top, by_x[i][half:]], 0).astype(bf16), dx=-k).astype(f32)
        end = by_y[i][half:] + ends[i * half : (i + 1) * half]
        own = own + hop(jnp.concatenate([by_y[i][:half], end], 0).astype(bf16), dy=-k).astype(f32)
    return own


def total_stats(s):
    s = s + hop(s, dc=1)
    s = (s + hop(s, dx=2)) + (hop(s, dx=1) + hop(s, dx=3))
    s = (s + hop(s, dy=2)) + (hop(s, dy=1) + hop(s, dy=3))
    even = (s + hop(s, dz=4)) + (hop(s, dz=2) + hop(s, dz=6))
    return even + ((hop(s, dz=1) + hop(s, dz=5)) + (hop(s, dz=3) + hop(s, dz=7)))


def shards(images, texts, image_ids, text_ids, temp_log, bias):
    owned = images.shape[0]
    half = owned // 2
    batch_all = owned * lax.axis_size("row") * lax.axis_size("col")
    scale = jnp.exp(temp_log[0])
    shift = bias[0]
    row, col = lax.axis_index("row"), lax.axis_index("col")
    x, y, z, c = row % NX, row // (2 * NX), 2 * (col // NC) + row // NX % 2, col % NC
    ximg, img_back = jax.vjp(normalize, images.astype(jnp.float32))
    xtxt, txt_back = jax.vjp(normalize, texts.astype(jnp.float32))
    image_block = jnp.concatenate(gather_images(ximg.astype(jnp.bfloat16), half), 0)
    text_block = gather_texts(xtxt.astype(jnp.bfloat16))
    split = (NY, 2, NX, NZ // 2, NC, owned)
    img_ids = image_ids.reshape(split)[:, z % 2, :, z // 2, c]
    txt_ids = text_ids.reshape(split)[y, :, x].transpose(1, 0, 2, 3).reshape(NZ, NC, owned)
    img_labels = image_rows(img_ids, x, y, half)
    txt_labels = text_rows(txt_ids, z, c)
    grad_b, stats = tile_grad(image_block, img_labels, text_block, txt_labels, scale, shift)
    gx = scale * jnp.dot(grad_b, text_block, preferred_element_type=jnp.float32)
    gy = scale * lax.dot_general(
        grad_b, image_block, (((0,), (0,)), ((), ())), preferred_element_type=jnp.float32
    )
    gxn = scatter_images(gx, owned, half)
    gyn = scatter_texts(gy, owned)
    stats = total_stats(jnp.broadcast_to(stats[:, None], (3, 128)))
    image_grad = img_back(gxn)[0].astype(jnp.bfloat16)
    text_grad = txt_back(gyn)[0].astype(jnp.bfloat16)
    return image_grad, text_grad, stats[:, 0] / batch_all


def solution(mesh):
    spread = P(("row", "col"), None)
    return jax.shard_map(
        shards,
        mesh=mesh,
        in_specs=(spread, spread, P(), P(), P(), P()),
        out_specs=(spread, spread, P()),
        check_vma=False,
    )
```

```python
import functools
import itertools
import jax
import jax.numpy as jnp
from jax import lax
from jax.experimental import pallas as pl
from jax.experimental.pallas import tpu as pltpu
from jax.sharding import PartitionSpec as P

NX, NY, NZ, NC = 4, 4, 8, 2
LOG2E = 1.4426950408889634
F32, BF16 = jnp.float32, jnp.bfloat16
ANY = pl.BlockSpec(memory_space=pl.ANY)
VMEM = pl.BlockSpec(memory_space=pltpu.VMEM)
SMEM = pl.BlockSpec(memory_space=pltpu.SMEM)
BIG = pltpu.CompilerParams(vmem_limit_bytes=56 * 2**20)
SMALL = pltpu.CompilerParams(vmem_limit_bytes=24 * 2**20)
Z_ORDER = (0, 1, -1, 2, -2, 3, -3, 4)


def linear(x, y, z, c):
    return (((y * 2 + z % 2) * NX + x) * (NZ // 2) + z // 2) * NC + c


def hop(a, move):
    pairs = []
    for x, y, z, c in itertools.product(range(NX), range(NY), range(NZ), range(NC)):
        dx, dy, dz, dc = move(c)
        to = linear((x + dx) % NX, (y + dy) % NY, (z + dz) % NZ, (c + dc) % NC)
        pairs.append((linear(x, y, z, c), to))
    return lax.ppermute(a, ("row", "col"), pairs)


def hop_first(a, k):
    return hop(a, lambda c: (0, k, 0, 0) if c else (k, 0, 0, 0))


def hop_second(a, k):
    return hop(a, lambda c: (k, 0, 0, 0) if c else (0, k, 0, 0))


def hop_z(a, k):
    return hop(a, lambda c: (0, 0, k, 0))


def hop_core(a):
    return hop(a, lambda c: (0, 0, 0, 1))


def dot_t(a, b):
    return lax.dot_general(a, b, (((1,), (1,)), ((), ())), preferred_element_type=F32)


def dot_a(a, b):
    return lax.dot_general(a, b, (((0,), (0,)), ((), ())), preferred_element_type=F32)


def inverse_norm(rows):
    return lax.rsqrt(jnp.sum(rows * rows, axis=1, keepdims=True) + 1e-06)


def norm_kernel(x_ref, y_ref, xn_ref, yn_ref):
    for src, dst in ((x_ref, xn_ref), (y_ref, yn_ref)):
        rows = src[...].astype(F32)
        dst[...] = (rows * inverse_norm(rows)).astype(BF16)


def normalize(images, texts):
    like = jax.ShapeDtypeStruct(images.shape, BF16)
    return pl.pallas_call(
        norm_kernel,
        out_shape=(like, like),
        in_specs=[VMEM, VMEM],
        out_specs=(VMEM, VMEM),
        name="normalize",
        compiler_params=SMALL,
    )(images, texts)


def join_kernel(*refs):
    parts, out, sem = refs[:-2], refs[-2], refs[-1]
    at, copies = 0, []
    for i, part in enumerate(parts):
        rows = part.shape[0]
        copies.append(pltpu.make_async_copy(part, out.at[pl.ds(at, rows)], sem.at[i]))
        at += rows
    for copy in copies:
        copy.start()
    for copy in copies:
        copy.wait()


def join(parts):
    rows = sum(p.shape[0] for p in parts)
    return pl.pallas_call(
        join_kernel,
        out_shape=jax.ShapeDtypeStruct((rows, parts[0].shape[1]), parts[0].dtype),
        in_specs=[ANY] * len(parts),
        out_specs=ANY,
        scratch_shapes=[pltpu.SemaphoreType.DMA((len(parts),))],
        name="join",
        compiler_params=SMALL,
    )(*parts)


def load(refs, dst, sem, first):
    out, at = [], 0
    for ref in refs:
        rows = ref.shape[0]
        copy = pltpu.make_async_copy(ref, dst.at[pl.ds(at, rows)], sem.at[first + len(out)])
        copy.start()
        out.append((at, copy))
        at += rows
    return out


def fold(v):
    u = jnp.sum(v.reshape(v.shape[0] // 8, 8, v.shape[1]), axis=0)
    return sum(u[:, k : k + 128] for k in range(0, u.shape[1], 128))


def tile_kernel(nx, nt, *refs):
    coef, image_ids, text_ids = refs[:3]
    images, texts = refs[3 : 3 + nx], refs[3 + nx : 3 + nx + nt]
    grad, gy, stats, xb, yb, prods, sem = refs[3 + nx + nt :]
    coming = load(texts, yb, sem, 0)
    coming_x = load(images, xb, sem, nt)
    for _, copy in coming:
        copy.wait()
    rows, cols = yb.shape[0], xb.shape[0]
    wide = 256
    steps = cols // wide
    scale, shift = coef[0] * LOG2E, coef[1] * LOG2E
    acc = [jnp.zeros((8, 128), F32)] * 3

    def multiply(k):
        while coming_x and coming_x[0][0] < (k + 1) * wide:
            coming_x.pop(0)[1].wait()
        prods[k % 2] = dot_t(yb[...], xb[k * wide : (k + 1) * wide])

    multiply(0)
    for k in range(steps):
        if k + 1 < steps:
            multiply(k + 1)
        dots = prods[k % 2]
        match = text_ids[:, :1] == image_ids[:1, k * wide : (k + 1) * wide]
        logits = dots * scale + shift
        e = jnp.exp2(jnp.where(match, -logits, logits))
        p = 1.0 + e
        s = e / p
        g = jnp.where(match, -s, s)
        grad[:, k * wide : (k + 1) * wide] = g.astype(BF16)
        acc[0] += fold(jnp.log2(p[: rows // 2] * p[rows // 2 :]))
        acc[1] += fold(g * dots)
        acc[2] += fold(g)
    for i in range(3):
        stats[i] = acc[i]
    part = rows // 2
    for r in range(0, rows, part):
        gy[r : r + part] = jnp.dot(
            grad[r : r + part], xb[...], preferred_element_type=F32
        ).astype(gy.dtype)


def tile(coef, image_ids, text_ids, images, texts, gy_dtype):
    cols, rows = image_ids.shape[1], text_ids.shape[0]
    d = images[0].shape[1]
    n = len(images) + len(texts)
    return pl.pallas_call(
        functools.partial(tile_kernel, len(images), len(texts)),
        out_shape=(
            jax.ShapeDtypeStruct((rows, cols), BF16),
            jax.ShapeDtypeStruct((rows, d), gy_dtype),
            jax.ShapeDtypeStruct((3, 8, 128), F32),
        ),
        in_specs=[SMEM, VMEM, VMEM] + [ANY] * n,
        out_specs=(VMEM, VMEM, VMEM),
        scratch_shapes=[
            pltpu.VMEM((cols, d), BF16),
            pltpu.VMEM((rows, d), BF16),
            pltpu.VMEM((2, rows, 256), F32),
            pltpu.SemaphoreType.DMA((n,)),
        ],
        name="tile",
        compiler_params=BIG,
    )(coef, image_ids, text_ids, *images, *texts)


def image_side_kernel(nt, ng, *refs):
    texts, grads = refs[:nt], refs[nt : nt + ng]
    outs, (yb, gb, sem) = refs[nt + ng : -3], refs[-3:]
    for _, copy in load(texts, yb, sem, 0) + load(grads, gb, sem, nt):
        copy.wait()
    at = 0
    for out in outs:
        rows = out.shape[0]
        out[...] = dot_a(gb[:, at : at + rows], yb[...]).astype(out.dtype)
        at += rows


def image_side(texts, grads, outs):
    rows = sum(t.shape[0] for t in texts)
    d, cols = texts[0].shape[1], grads[0].shape[1]
    n = len(texts) + len(grads)
    return pl.pallas_call(
        functools.partial(image_side_kernel, len(texts), len(grads)),
        out_shape=tuple(jax.ShapeDtypeStruct((r, d), t) for r, t in outs),
        in_specs=[ANY] * n,
        out_specs=tuple([VMEM] * len(outs)),
        scratch_shapes=[
            pltpu.VMEM((rows, d), BF16),
            pltpu.VMEM((rows, cols), BF16),
            pltpu.SemaphoreType.DMA((n,)),
        ],
        name="image_side",
        compiler_params=BIG,
    )(*texts, *grads)


def add_split_kernel(n, *refs):
    parts, outs = refs[:n], refs[n:]
    rows = outs[0].shape[0]
    for i, out in enumerate(outs):
        at = pl.ds(i * rows, rows)
        out[...] = sum(p[at].astype(F32) for p in parts).astype(out.dtype)


def add_split(parts, pieces):
    rows, d = parts[0].shape[0] // pieces, parts[0].shape[1]
    return pl.pallas_call(
        functools.partial(add_split_kernel, len(parts)),
        out_shape=tuple(
            jax.ShapeDtypeStruct((rows, d), BF16 if i else F32) for i in range(pieces)
        ),
        in_specs=[VMEM] * len(parts),
        out_specs=tuple([VMEM] * pieces),
        name="add_split",
        compiler_params=SMALL,
    )(*parts)


def finish_kernel(scale, *refs):
    raw, parts, out = refs[0], refs[1:-1], refs[-1]
    rows = raw[...].astype(F32)
    inv = inverse_norm(rows)
    unit = rows * inv
    g = scale[0] * sum(p[...].astype(F32) for p in parts)
    out[...] = (inv * (g - unit * jnp.sum(unit * g, axis=1, keepdims=True))).astype(BF16)


def finish(scale, raw, parts):
    return pl.pallas_call(
        finish_kernel,
        out_shape=jax.ShapeDtypeStruct(raw.shape, BF16),
        in_specs=[SMEM] + [VMEM] * (1 + len(parts)),
        out_specs=VMEM,
        name="finish",
        compiler_params=SMALL,
    )(scale, raw, *parts)


def total_stats(s):
    s = s + hop_core(s)
    for m in (1, 2):
        pairs = [(i, i ^ (m << 3)) for i in range(256)]
        s = s + lax.ppermute(s, ("row", "col"), pairs)
    for b in (1, 2, 5, 6, 7):
        pairs = [(i, i ^ (1 << b)) for i in range(256)]
        s = s + lax.ppermute(s, ("row", "col"), pairs)
    return s


def labels(image_ids, text_ids, x, y, z, c, owned):
    split = (NY, 2, NX, NZ // 2, NC, owned)
    img = image_ids.reshape(split)[:, z % 2, :, z // 2, c].reshape(NY * NX, owned)
    txt = text_ids.reshape(split)[y, :, x].transpose(1, 0, 2, 3).reshape(NZ * NC, owned)
    first, second = jnp.where(c, y, x), jnp.where(c, x, y)
    at = []
    for j in range(4):
        for k in range(4):
            f, s = (first - k) % 4, (second - j) % 4
            at.append(jnp.where(c, f * NX + s, s * NX + f))
    img = img[jnp.stack(at)].reshape(1, -1)
    at = [(z - dz) % NZ * NC + (c + dc) % NC for dc in (0, 1) for dz in Z_ORDER]
    txt = txt[jnp.stack(at)].reshape(-1, 1)
    return img, txt


def shards(images, texts, image_ids, text_ids, temp_log, bias):
    owned = images.shape[0]
    batch_all = owned * NX * NY * NZ * NC
    row, col = lax.axis_index("row"), lax.axis_index("col")
    x, y, z, c = row % NX, row // (2 * NX), 2 * (col // NC) + row // NX % 2, col % NC
    scale = jnp.exp(temp_log)
    coef = jnp.concatenate([scale, bias])
    img_ids, txt_ids = labels(image_ids, text_ids, x, y, z, c, owned)

    xn, yn = normalize(images, texts)
    near = [xn] + [hop_first(xn, k) for k in (1, 2, 3)]
    own = [yn] + [hop_z(yn, k) for k in Z_ORDER[1:]]
    near = join(near)
    image_blocks = [near] + [hop_second(near, k) for k in (1, 2, 3)]
    other = [hop_core(join(own[:4])), hop_core(join(own[4:]))]

    half = NZ * owned
    g_own, gy_own, stats_own = tile(coef, img_ids, txt_ids[:half], image_blocks, own, F32)
    g_other, gy_other, stats_other = tile(coef, img_ids, txt_ids[half:], image_blocks, other, BF16)

    stats = jnp.sum(stats_own + stats_other, axis=(1, 2))
    stats = total_stats(jnp.broadcast_to(stats[:, None], (3, 128)))[:, 0]
    stats = stats * jnp.stack([jnp.float32(1 / LOG2E), scale[0], jnp.float32(1)])

    text_parts = add_split([gy_own, hop_core(gy_other)], NZ)
    text_parts = [text_parts[0]] + [hop_z(p, -k) for p, k in zip(text_parts[1:], Z_ORDER[1:])]

    size = 4 * owned
    gx = image_side(own + other, [g_own, g_other], [(size, F32)] + [(size, BF16)] * 3)
    gx = [gx[0]] + [hop_second(gx[k], -k) for k in (1, 2, 3)]
    gx = add_split(gx, 4)
    image_parts = [gx[0]] + [hop_first(gx[k], -k) for k in (1, 2, 3)]

    text_grad = finish(scale, texts, text_parts)
    image_grad = finish(scale, images, image_parts)
    return image_grad, text_grad, stats / batch_all


def solution(mesh):
    spread = P(("row", "col"), None)
    return jax.shard_map(
        shards,
        mesh=mesh,
        in_specs=(spread, spread, P(), P(), P(), P()),
        out_specs=(spread, spread, P()),
        check_vma=False,
    )
```

```python
import functools
import itertools
import jax
import jax.numpy as jnp
from jax import lax
from jax.experimental import pallas as pl
from jax.experimental.pallas import tpu as pltpu
from jax.sharding import PartitionSpec as P

NX, NY, NZ, NC = 4, 4, 8, 2
LOG2E = 1.4426950408889634
F32, BF16 = jnp.float32, jnp.bfloat16
ANY = pl.BlockSpec(memory_space=pl.ANY)
VMEM = pl.BlockSpec(memory_space=pltpu.VMEM)
SMEM = pl.BlockSpec(memory_space=pltpu.SMEM)
BIG = pltpu.CompilerParams(vmem_limit_bytes=56 * 2**20)
SMALL = pltpu.CompilerParams(vmem_limit_bytes=24 * 2**20)
STAT_ROWS = 16


def linear(x, y, z, c):
    return (((y * 2 + z % 2) * NX + x) * (NZ // 2) + z // 2) * NC + c


def hop(a, move):
    pairs = []
    for x, y, z, c in itertools.product(range(NX), range(NY), range(NZ), range(NC)):
        dx, dy, dz, dc = move(c)
        to = linear((x + dx) % NX, (y + dy) % NY, (z + dz) % NZ, (c + dc) % NC)
        pairs.append((linear(x, y, z, c), to))
    return lax.ppermute(a, ("row", "col"), pairs)


def hop_first(a, k):
    return hop(a, lambda c: (0, k, 0, 0) if c else (k, 0, 0, 0))


def hop_second(a, k):
    return hop(a, lambda c: (k, 0, 0, 0) if c else (0, k, 0, 0))


def hop_z(a, k):
    return hop(a, lambda c: (0, 0, -k if c else k, 0))


def hop_core(a):
    return hop(a, lambda c: (0, 0, 0, 1))


def exchange(a, bit):
    return lax.ppermute(a, ("row", "col"), [(i, i ^ (1 << bit)) for i in range(256)])


def dot_t(a, b):
    return lax.dot_general(a, b, (((1,), (1,)), ((), ())), preferred_element_type=F32)


def dot_a(a, b):
    return lax.dot_general(a, b, (((0,), (0,)), ((), ())), preferred_element_type=F32)


def inverse_norm(rows):
    return lax.rsqrt(jnp.sum(rows * rows, axis=1, keepdims=True) + 1e-06)


def norm_kernel(x_ref, y_ref, xn_ref, yn_ref):
    for src, dst in ((x_ref, xn_ref), (y_ref, yn_ref)):
        rows = src[...].astype(F32)
        dst[...] = (rows * inverse_norm(rows)).astype(BF16)


def normalize(images, texts):
    like = jax.ShapeDtypeStruct(images.shape, BF16)
    return pl.pallas_call(
        norm_kernel,
        out_shape=(like, like),
        in_specs=[VMEM, VMEM],
        out_specs=(VMEM, VMEM),
        name="normalize",
        compiler_params=SMALL,
    )(images, texts)


def join_kernel(*refs):
    parts, out, sem = refs[:-2], refs[-2], refs[-1]
    at, copies = 0, []
    for i, part in enumerate(parts):
        rows = part.shape[0]
        copies.append(pltpu.make_async_copy(part, out.at[pl.ds(at, rows)], sem.at[i]))
        at += rows
    for copy in copies:
        copy.start()
    for copy in copies:
        copy.wait()


def join(parts):
    rows = sum(p.shape[0] for p in parts)
    return pl.pallas_call(
        join_kernel,
        out_shape=jax.ShapeDtypeStruct((rows, parts[0].shape[1]), parts[0].dtype),
        in_specs=[ANY] * len(parts),
        out_specs=ANY,
        scratch_shapes=[pltpu.SemaphoreType.DMA((len(parts),))],
        name="join",
        compiler_params=SMALL,
    )(*parts)


def load(refs, dst, sem, first):
    out, at = [], 0
    for ref in refs:
        rows = ref.shape[0]
        copy = pltpu.make_async_copy(ref, dst.at[pl.ds(at, rows)], sem.at[first + len(out)])
        copy.start()
        out.append((at, copy))
        at += rows
    return out


def fold(v):
    u = jnp.sum(v.reshape(v.shape[0] // 8, 8, v.shape[1]), axis=0)
    return sum(u[:, k : k + 128] for k in range(0, u.shape[1], 128))


def put_stats(sums, rows, width):
    row = lax.broadcasted_iota(jnp.int32, (STAT_ROWS, width), 0)
    v = jnp.where(row % 3 == 0, sums[0], jnp.where(row % 3 == 1, sums[1], sums[2]))
    high = v.astype(BF16).astype(F32)
    mid = (v - high).astype(BF16).astype(F32)
    low = v - high - mid
    v = jnp.where(row < 3, high, jnp.where(row < 6, mid, low))
    rows[...] = jnp.where(row < 9, v, 0.0).astype(BF16)


def get_stats(rows):
    v = rows[...].astype(F32)
    return (v[0:3] + v[3:6]) + v[6:9]


def tile_kernel(nx, nt, *refs):
    coef, image_ids, text_ids = refs[:3]
    images, texts = refs[3 : 3 + nx], refs[3 + nx : 3 + nx + nt]
    grad, gy, stats, xb, yb, prods, sem = refs[3 + nx + nt :]
    coming = load(texts, yb, sem, 0)
    coming_x = load(images, xb, sem, nt)
    for _, copy in coming:
        copy.wait()
    rows, cols = yb.shape[0], xb.shape[0]
    wide = 256
    steps = cols // wide
    scale, shift = coef[0] * LOG2E, coef[1] * LOG2E
    acc = [jnp.zeros((8, 128), F32)] * 3

    def multiply(k):
        while coming_x and coming_x[0][0] < (k + 1) * wide:
            coming_x.pop(0)[1].wait()
        prods[k % 2] = dot_t(yb[...], xb[k * wide : (k + 1) * wide])

    multiply(0)
    for k in range(steps):
        if k + 1 < steps:
            multiply(k + 1)
        dots = prods[k % 2]
        match = text_ids[:, :1] == image_ids[:1, k * wide : (k + 1) * wide]
        logits = dots * scale + shift
        e = jnp.exp2(jnp.where(match, -logits, logits))
        p = 1.0 + e
        s = e / p
        g = jnp.where(match, -s, s)
        grad[:, k * wide : (k + 1) * wide] = g.astype(BF16)
        acc[0] += fold(jnp.log2(p[: rows // 2] * p[rows // 2 :]))
        acc[1] += fold(g * dots)
        acc[2] += fold(g)
    for i in range(3):
        stats[i] = acc[i]
    part = rows // 2
    for r in range(0, rows, part):
        gy[r : r + part] = jnp.dot(
            grad[r : r + part], xb[...], preferred_element_type=F32
        ).astype(gy.dtype)


def tile(coef, image_ids, text_ids, images, texts, gy_dtype):
    cols, rows = image_ids.shape[1], text_ids.shape[0]
    d = images[0].shape[1]
    n = len(images) + len(texts)
    return pl.pallas_call(
        functools.partial(tile_kernel, len(images), len(texts)),
        out_shape=(
            jax.ShapeDtypeStruct((rows, cols), BF16),
            jax.ShapeDtypeStruct((rows, d), gy_dtype),
            jax.ShapeDtypeStruct((3, 8, 128), F32),
        ),
        in_specs=[SMEM, VMEM, VMEM] + [ANY] * n,
        out_specs=(VMEM, VMEM, VMEM),
        scratch_shapes=[
            pltpu.VMEM((cols, d), BF16),
            pltpu.VMEM((rows, d), BF16),
            pltpu.VMEM((2, rows, 256), F32),
            pltpu.SemaphoreType.DMA((n,)),
        ],
        name="tile",
        compiler_params=BIG,
    )(coef, image_ids, text_ids, *images, *texts)


def image_side_kernel(nt, ng, *refs):
    texts, grads = refs[:nt], refs[nt : nt + ng]
    stats_a, stats_b = refs[nt + ng : nt + ng + 2]
    outs, mine, (yb, gb, sem) = refs[nt + ng + 2 : -4], refs[-4], refs[-3:]
    coming = load(texts, yb, sem, 0) + load(grads, gb, sem, nt)
    sums = [jnp.sum(stats_a[i] + stats_b[i]) for i in range(3)]
    put_stats(sums, mine, mine.shape[1])
    for _, copy in coming:
        copy.wait()
    rows = outs[0].shape[0]
    for i, out in enumerate(outs):
        out[pl.ds(0, rows)] = dot_a(gb[:, i * rows : (i + 1) * rows], yb[...]).astype(out.dtype)
        if i:
            out[pl.ds(rows, STAT_ROWS)] = mine[...]


def image_side(texts, grads, stats):
    rows = sum(t.shape[0] for t in texts)
    d, cols = texts[0].shape[1], grads[0].shape[1]
    n = len(texts) + len(grads)
    size = cols // 4
    sent = jax.ShapeDtypeStruct((size + STAT_ROWS, d), BF16)
    return pl.pallas_call(
        functools.partial(image_side_kernel, len(texts), len(grads)),
        out_shape=(jax.ShapeDtypeStruct((size, d), F32), sent, sent, sent)
        + (jax.ShapeDtypeStruct((STAT_ROWS, d), BF16),),
        in_specs=[ANY] * n + [VMEM] * 2,
        out_specs=(VMEM,) * 5,
        scratch_shapes=[
            pltpu.VMEM((rows, d), BF16),
            pltpu.VMEM((rows, cols), BF16),
            pltpu.SemaphoreType.DMA((n,)),
        ],
        name="image_side",
        compiler_params=BIG,
    )(*texts, *grads, *stats)


def total_four(own, parts):
    return (own + parts[1]) + (parts[0] + parts[2])


def image_add_kernel(own, a, b, c, mine, keep, out1, out2, out3, sums):
    rows = keep.shape[0]
    for i, out in enumerate((keep, out1, out2, out3)):
        at = pl.ds(i * rows, rows)
        out[pl.ds(0, rows)] = (
            own[at] + a[at].astype(F32) + b[at].astype(F32) + c[at].astype(F32)
        ).astype(out.dtype)
    tail = pl.ds(4 * rows, STAT_ROWS)
    v = total_four(get_stats(mine), [get_stats(p.at[tail]) for p in (a, b, c)])
    put_stats([v[0:1], v[1:2], v[2:3]], sums, sums.shape[1])
    for out in (out1, out2, out3):
        out[pl.ds(rows, STAT_ROWS)] = sums[...]


def image_add(own, parts, mine):
    rows, d = own.shape[0] // 4, own.shape[1]
    sent = jax.ShapeDtypeStruct((rows + STAT_ROWS, d), BF16)
    return pl.pallas_call(
        image_add_kernel,
        out_shape=(jax.ShapeDtypeStruct((rows, d), F32), sent, sent, sent)
        + (jax.ShapeDtypeStruct((STAT_ROWS, d), BF16),),
        in_specs=[VMEM] * 5,
        out_specs=(VMEM,) * 5,
        name="image_add",
        compiler_params=SMALL,
    )(own, *parts, mine)


def text_add_kernel(own, other, keep, far, near, twice):
    at = 0
    for out in (keep, far, near, twice):
        rows = pl.ds(at, out.shape[0])
        out[...] = (own[rows] + other[rows].astype(F32)).astype(out.dtype)
        at += out.shape[0]


def text_add(own, other):
    rows, d = own.shape[0] // 8, own.shape[1]
    kinds = ((rows, F32), (rows, BF16), (2 * rows, F32), (4 * rows, BF16))
    return pl.pallas_call(
        text_add_kernel,
        out_shape=tuple(jax.ShapeDtypeStruct((r, d), t) for r, t in kinds),
        in_specs=[VMEM] * 2,
        out_specs=(VMEM,) * 4,
        name="text_add",
        compiler_params=SMALL,
    )(own, other)


def near_add_kernel(near, twice, out):
    rows = near.shape[0]
    out[...] = (near[...] + twice[pl.ds(rows, rows)].astype(F32)).astype(BF16)


def near_add(near, twice):
    return pl.pallas_call(
        near_add_kernel,
        out_shape=jax.ShapeDtypeStruct(near.shape, BF16),
        in_specs=[VMEM] * 2,
        out_specs=VMEM,
        name="near_add",
        compiler_params=SMALL,
    )(near, twice)


def other_add_kernel(near, twice, out):
    at = pl.ds(out.shape[0], out.shape[0])
    out[...] = near[at].astype(F32) + twice[at].astype(F32)


def other_add(near, twice):
    return pl.pallas_call(
        other_add_kernel,
        out_shape=jax.ShapeDtypeStruct((near.shape[0] // 2, near.shape[1]), F32),
        in_specs=[VMEM] * 2,
        out_specs=VMEM,
        name="other_add",
        compiler_params=SMALL,
    )(near, twice)


def finish_kernel(scale, *refs):
    raw, parts, out = refs[0], refs[1:-1], refs[-1]
    rows = raw[...].astype(F32)
    inv = inverse_norm(rows)
    unit = rows * inv
    owned = pl.ds(0, raw.shape[0])
    g = scale[0] * sum(p[owned].astype(F32) for p in parts)
    out[...] = (inv * (g - unit * jnp.sum(unit * g, axis=1, keepdims=True))).astype(BF16)


def finish(scale, raw, parts):
    return pl.pallas_call(
        finish_kernel,
        out_shape=jax.ShapeDtypeStruct(raw.shape, BF16),
        in_specs=[SMEM] + [VMEM] * (1 + len(parts)),
        out_specs=VMEM,
        name="finish",
        compiler_params=SMALL,
    )(scale, raw, *parts)


def stats_kernel(mine, a, b, c, out):
    tail = pl.ds(a.shape[0] - STAT_ROWS, STAT_ROWS)
    v = total_four(get_stats(mine), [get_stats(p.at[tail]) for p in (a, b, c)])
    out[...] = v[:, :128]


def stats_sum(mine, parts):
    return pl.pallas_call(
        stats_kernel,
        out_shape=jax.ShapeDtypeStruct((3, 128), F32),
        in_specs=[VMEM] * 4,
        out_specs=VMEM,
        name="stats_sum",
        compiler_params=SMALL,
    )(mine, *parts)


def labels(image_ids, text_ids, x, y, z, c, owned):
    split = (NY, 2, NX, NZ // 2, NC, owned)
    img = image_ids.reshape(split)[:, z % 2, :, z // 2, c].reshape(NY * NX, owned)
    txt = text_ids.reshape(split)[y, :, x].transpose(1, 0, 2, 3).reshape(NZ * NC, owned)
    first, second = jnp.where(c, y, x), jnp.where(c, x, y)
    at = []
    for j in range(4):
        for k in range(4):
            f, s = (first - k) % 4, (second - j) % 4
            at.append(jnp.where(c, f * NX + s, s * NX + f))
    img = img[jnp.stack(at)].reshape(1, -1)
    up = 1 - 2 * c
    at = []
    for core, sign in ((c, up), (1 - c, -up)):
        order = [(0, core), (4, core)] + [(k, d) for k in (1, 2, 3) for d in (core, 1 - core)]
        at += [(z - sign * k) % NZ * NC + d for k, d in order]
    txt = txt[jnp.stack(at)].reshape(-1, 1)
    return img, txt


def shards(images, texts, image_ids, text_ids, temp_log, bias):
    owned = images.shape[0]
    batch_all = owned * NX * NY * NZ * NC
    row, col = lax.axis_index("row"), lax.axis_index("col")
    x, y, z, c = row % NX, row // (2 * NX), 2 * (col // NC) + row // NX % 2, col % NC
    scale = jnp.exp(temp_log)
    coef = jnp.concatenate([scale, bias])
    img_ids, txt_ids = labels(image_ids, text_ids, x, y, z, c, owned)

    xn, yn = normalize(images, texts)
    sibling = hop_core(yn)
    near = [xn] + [hop_first(xn, k) for k in (1, 2, 3)]
    pair = join([yn, sibling])
    next_pair = hop_z(pair, 1)
    far = hop_z(yn, 4)
    near = join(near)
    twice = hop_z(join([pair, next_pair]), 2)
    image_blocks = [near] + [hop_second(near, k) for k in (1, 2, 3)]
    own = [yn, far, next_pair, twice]
    other = [sibling, hop_core(join(own[1:]))]

    half = NZ * owned
    g_own, gy_own, stats_own = tile(coef, img_ids, txt_ids[:half], image_blocks, own, F32)
    g_other, gy_other, stats_other = tile(coef, img_ids, txt_ids[half:], image_blocks, other, BF16)

    gy, far, near, twice = text_add(gy_own, hop_core(gy_other))
    twice, far = hop_z(twice, -2), hop_z(far, 4)
    near = hop_z(near_add(near, twice), -1)
    text_parts = [gy, twice, near, far, hop_core(other_add(near, twice))]

    keep, g1, g2, g3, stats = image_side(
        own + other, [g_own, g_other], [stats_own, stats_other]
    )
    parts = [hop_second(g, -k) for k, g in ((1, g1), (2, g2), (3, g3))]
    keep, g1, g2, g3, stats = image_add(keep, parts, stats)
    parts = [hop_first(g, -k) for k, g in ((1, g1), (2, g2), (3, g3))]

    stats = stats_sum(stats, parts)
    for bit in (5, 1, 2, 0):
        stats = stats + exchange(stats, bit)
    stats = stats[:, 0] * jnp.stack([jnp.float32(1 / LOG2E), scale[0], jnp.float32(1)])

    text_grad = finish(scale, texts, text_parts)
    image_grad = finish(scale, images, [keep] + parts)
    return image_grad, text_grad, stats / batch_all


def solution(mesh):
    spread = P(("row", "col"), None)
    return jax.shard_map(
        shards,
        mesh=mesh,
        in_specs=(spread, spread, P(), P(), P(), P()),
        out_specs=(spread, spread, P()),
        check_vma=False,
    )
```

```python
import functools
import itertools
import jax
import jax.numpy as jnp
from jax import lax
from jax.experimental import pallas as pl
from jax.experimental.pallas import tpu as pltpu
from jax.sharding import PartitionSpec as P

NX, NY, NZ, NC = 4, 4, 8, 2
LOG2E = 1.4426950408889634
F32, BF16 = jnp.float32, jnp.bfloat16
ANY = pl.BlockSpec(memory_space=pl.ANY)
VMEM = pl.BlockSpec(memory_space=pltpu.VMEM)
SMEM = pl.BlockSpec(memory_space=pltpu.SMEM)
BIG = pltpu.CompilerParams(vmem_limit_bytes=56 * 2**20)
SMALL = pltpu.CompilerParams(vmem_limit_bytes=24 * 2**20)
STAT_ROWS = 16


def linear(x, y, z, c):
    return (((y * 2 + z % 2) * NX + x) * (NZ // 2) + z // 2) * NC + c


def hop(a, move):
    pairs = []
    for x, y, z, c in itertools.product(range(NX), range(NY), range(NZ), range(NC)):
        dx, dy, dz, dc = move(c)
        to = linear((x + dx) % NX, (y + dy) % NY, (z + dz) % NZ, (c + dc) % NC)
        pairs.append((linear(x, y, z, c), to))
    return lax.ppermute(a, ("row", "col"), pairs)


def hop_first(a, k):
    return hop(a, lambda c: (0, k, 0, 0) if c else (k, 0, 0, 0))


def hop_second(a, k):
    return hop(a, lambda c: (k, 0, 0, 0) if c else (0, k, 0, 0))


def hop_z(a, k):
    return hop(a, lambda c: (0, 0, -k if c else k, 0))


def hop_core(a):
    return hop(a, lambda c: (0, 0, 0, 1))


def exchange(a, bit0, bit1):
    pairs = [(i, i ^ (1 << (bit1 if i % 2 else bit0))) for i in range(256)]
    return lax.ppermute(a, ("row", "col"), pairs)


def dot_t(a, b):
    return lax.dot_general(a, b, (((1,), (1,)), ((), ())), preferred_element_type=F32)


def dot_a(a, b):
    return lax.dot_general(a, b, (((0,), (0,)), ((), ())), preferred_element_type=F32)


def inverse_norm(rows):
    return lax.rsqrt(jnp.sum(rows * rows, axis=1, keepdims=True) + 1e-06)


def norm_kernel(x_ref, y_ref, xn_ref, yn_ref):
    for src, dst in ((x_ref, xn_ref), (y_ref, yn_ref)):
        rows = src[...].astype(F32)
        dst[...] = (rows * inverse_norm(rows)).astype(BF16)


def normalize(images, texts):
    like = jax.ShapeDtypeStruct(images.shape, BF16)
    return pl.pallas_call(
        norm_kernel,
        out_shape=(like, like),
        in_specs=[VMEM, VMEM],
        out_specs=(VMEM, VMEM),
        name="normalize",
        compiler_params=SMALL,
    )(images, texts)


def join_kernel(n, *refs):
    parts, out, sem = refs[:n], refs[-2], refs[-1]
    at, copies = 0, []
    for i, part in enumerate(parts):
        rows = part.shape[0]
        copies.append(pltpu.make_async_copy(part, out.at[pl.ds(at, rows)], sem.at[i]))
        at += rows
    for copy in copies:
        copy.start()
    for copy in copies:
        copy.wait()


def join(parts, after=()):
    rows = sum(p.shape[0] for p in parts)
    return pl.pallas_call(
        functools.partial(join_kernel, len(parts)),
        out_shape=jax.ShapeDtypeStruct((rows, parts[0].shape[1]), parts[0].dtype),
        in_specs=[ANY] * (len(parts) + len(after)),
        out_specs=ANY,
        scratch_shapes=[pltpu.SemaphoreType.DMA((len(parts),))],
        name="join",
        compiler_params=SMALL,
    )(*parts, *after)


def load(refs, dst, sem, first):
    out, at = [], 0
    for ref in refs:
        rows = ref.shape[0]
        copy = pltpu.make_async_copy(ref, dst.at[pl.ds(at, rows)], sem.at[first + len(out)])
        copy.start()
        out.append((at, copy))
        at += rows
    return out


def fold(v):
    u = jnp.sum(v.reshape(v.shape[0] // 8, 8, v.shape[1]), axis=0)
    return sum(u[:, k : k + 128] for k in range(0, u.shape[1], 128))


def put_stats(sums, rows, width):
    row = lax.broadcasted_iota(jnp.int32, (STAT_ROWS, width), 0)
    v = jnp.where(row % 3 == 0, sums[0], jnp.where(row % 3 == 1, sums[1], sums[2]))
    high = v.astype(BF16).astype(F32)
    mid = (v - high).astype(BF16).astype(F32)
    low = v - high - mid
    v = jnp.where(row < 3, high, jnp.where(row < 6, mid, low))
    rows[...] = jnp.where(row < 9, v, 0.0).astype(BF16)


def get_stats(rows):
    v = rows[...].astype(F32)
    return (v[0:3] + v[3:6]) + v[6:9]


def tile_kernel(nx, nt, last, *refs):
    coef, image_ids, text_ids, before = refs[:4]
    images, texts = refs[4 : 4 + nx], refs[4 + nx : 4 + nx + nt]
    grad, keep, send, stats, xb, yb, prods, sem = refs[4 + nx + nt :]
    coming = load(texts, yb, sem, 0)
    coming_x = load(images, xb, sem, nt)
    for _, copy in coming:
        copy.wait()
    rows, cols = yb.shape[0], xb.shape[0]
    wide = 256
    steps = cols // wide
    scale, shift = coef[0] * LOG2E, coef[1] * LOG2E
    acc = [before[i] for i in range(3)]

    def multiply(k):
        while coming_x and coming_x[0][0] < (k + 1) * wide:
            coming_x.pop(0)[1].wait()
        prods[k % 2] = dot_t(yb[...], xb[k * wide : (k + 1) * wide])

    multiply(0)
    for k in range(steps):
        if k + 1 < steps:
            multiply(k + 1)
        dots = prods[k % 2]
        match = text_ids[:, :1] == image_ids[:1, k * wide : (k + 1) * wide]
        logits = dots * scale + shift
        e = jnp.exp2(jnp.where(match, -logits, logits))
        p = 1.0 + e
        s = e / p
        g = jnp.where(match, -s, s)
        grad[:, k * wide : (k + 1) * wide] = g.astype(BF16)
        acc[0] += fold(jnp.log2(p[: rows // 2] * p[rows // 2 :]))
        acc[1] += fold(g * dots)
        acc[2] += fold(g)
    for i in range(3):
        if last:
            stats[pl.ds(i, 1)] = jnp.full((1, 128), jnp.sum(acc[i]))
        else:
            stats[i] = acc[i]
    part = rows // 2
    for r, out in ((part, send), (0, keep)):
        out[...] = jnp.dot(
            grad[r : r + part], xb[...], preferred_element_type=F32
        ).astype(out.dtype)


def tile(coef, image_ids, text_ids, before, images, texts, last):
    cols, rows = image_ids.shape[1], text_ids.shape[0]
    d = images[0].shape[1]
    n = len(images) + len(texts)
    return pl.pallas_call(
        functools.partial(tile_kernel, len(images), len(texts), last),
        out_shape=(
            jax.ShapeDtypeStruct((rows, cols), BF16),
            jax.ShapeDtypeStruct((rows // 2, d), F32),
            jax.ShapeDtypeStruct((rows // 2, d), BF16),
            jax.ShapeDtypeStruct((3, 128) if last else (3, 8, 128), F32),
        ),
        in_specs=[SMEM, VMEM, VMEM, VMEM] + [ANY] * n,
        out_specs=(VMEM,) * 4,
        scratch_shapes=[
            pltpu.VMEM((cols, d), BF16),
            pltpu.VMEM((rows, d), BF16),
            pltpu.VMEM((2, rows, 256), F32),
            pltpu.SemaphoreType.DMA((n,)),
        ],
        name="tile_late" if last else "tile_early",
        cost_estimate=pl.CostEstimate(
            flops=4 * rows * cols * d, bytes_accessed=8 * cols * d, transcendentals=3 * rows * cols
        ),
        compiler_params=BIG,
    )(coef, image_ids, text_ids, before, *images, *texts)


def image_side_kernel(nt, ng, *refs):
    texts, grads = refs[:nt], refs[nt : nt + ng]
    outs, (yb, gb, sem) = refs[-7:-3], refs[-3:]
    for _, copy in load(texts, yb, sem, 0) + load(grads, gb, sem, nt):
        copy.wait()
    rows = outs[0].shape[0]
    for i in (1, 2, 3, 0):
        at = slice(i * rows, (i + 1) * rows)
        outs[i][...] = dot_a(gb[:, at], yb[...]).astype(outs[i].dtype)


def image_side(texts, grads, after):
    rows = sum(t.shape[0] for t in texts)
    d, cols = texts[0].shape[1], grads[0].shape[1]
    n = len(texts) + len(grads)
    size = cols // 4
    sent = jax.ShapeDtypeStruct((size, d), BF16)
    return pl.pallas_call(
        functools.partial(image_side_kernel, len(texts), len(grads)),
        out_shape=(jax.ShapeDtypeStruct((size, d), F32), sent, sent, sent),
        in_specs=[ANY] * (n + len(after)),
        out_specs=(VMEM,) * 4,
        scratch_shapes=[
            pltpu.VMEM((rows, d), BF16),
            pltpu.VMEM((rows, cols), BF16),
            pltpu.SemaphoreType.DMA((n,)),
        ],
        name="image_side",
        cost_estimate=pl.CostEstimate(
            flops=2 * rows * cols * d, bytes_accessed=8 * cols * d, transcendentals=0
        ),
        compiler_params=BIG,
    )(*texts, *grads, *after)


def total_four(own, parts):
    return (own + parts[1]) + (parts[0] + parts[2])


def image_add_kernel(own, a, b, c, stats, keep, out1, out2, out3):
    rows = keep.shape[0]
    sums = [stats[pl.ds(i, 1)][:, :1] for i in range(3)]
    for i, out in enumerate((keep, out1, out2, out3)):
        at = pl.ds(i * rows, rows)
        out[pl.ds(0, rows)] = (
            own[at] + a[at].astype(F32) + b[at].astype(F32) + c[at].astype(F32)
        ).astype(out.dtype)
        if i:
            put_stats(sums, out.at[pl.ds(rows, STAT_ROWS)], out.shape[1])


def image_add(own, parts, stats):
    rows, d = own.shape[0] // 4, own.shape[1]
    sent = jax.ShapeDtypeStruct((rows + STAT_ROWS, d), BF16)
    return pl.pallas_call(
        image_add_kernel,
        out_shape=(jax.ShapeDtypeStruct((rows, d), F32), sent, sent, sent),
        in_specs=[VMEM] * 5,
        out_specs=(VMEM,) * 4,
        name="image_add",
        compiler_params=SMALL,
    )(own, *parts, stats)


def text_add_kernel(own, other, *outs):
    at = 0
    for out in outs:
        rows = pl.ds(at, out.shape[0])
        out[...] = (own[rows] + other[rows].astype(F32)).astype(out.dtype)
        at += out.shape[0]


def text_add(own, other, kinds):
    d = own.shape[1]
    return pl.pallas_call(
        text_add_kernel,
        out_shape=tuple(jax.ShapeDtypeStruct((r, d), t) for r, t in kinds),
        in_specs=[VMEM] * 2,
        out_specs=(VMEM,) * len(kinds),
        name="text_add",
        compiler_params=SMALL,
    )(own, other)


def near_add_kernel(near, twice, *refs):
    out = refs[-1]
    rows = near.shape[0]
    out[...] = (near[...] + twice[pl.ds(rows, rows)].astype(F32)).astype(BF16)


def near_add(near, twice, after):
    return pl.pallas_call(
        near_add_kernel,
        out_shape=jax.ShapeDtypeStruct(near.shape, BF16),
        in_specs=[VMEM] * 2 + [ANY] * len(after),
        out_specs=VMEM,
        name="near_add",
        compiler_params=SMALL,
    )(near, twice, *after)


def other_add_kernel(near, twice, out):
    at = pl.ds(out.shape[0], out.shape[0])
    out[...] = near[at].astype(F32) + twice[at].astype(F32)


def other_add(near, twice):
    return pl.pallas_call(
        other_add_kernel,
        out_shape=jax.ShapeDtypeStruct((near.shape[0] // 2, near.shape[1]), F32),
        in_specs=[VMEM] * 2,
        out_specs=VMEM,
        name="other_add",
        compiler_params=SMALL,
    )(near, twice)


def finish_kernel(scale, *refs):
    raw, parts, out = refs[0], refs[1:-1], refs[-1]
    rows = raw[...].astype(F32)
    inv = inverse_norm(rows)
    unit = rows * inv
    owned = pl.ds(0, raw.shape[0])
    g = scale[0] * sum(p[owned].astype(F32) for p in parts)
    out[...] = (inv * (g - unit * jnp.sum(unit * g, axis=1, keepdims=True))).astype(BF16)


def finish(scale, raw, parts):
    return pl.pallas_call(
        finish_kernel,
        out_shape=jax.ShapeDtypeStruct(raw.shape, BF16),
        in_specs=[SMEM] + [VMEM] * (1 + len(parts)),
        out_specs=VMEM,
        name="finish",
        compiler_params=SMALL,
    )(scale, raw, *parts)


def stats_kernel(mine, a, b, c, out):
    tail = pl.ds(a.shape[0] - STAT_ROWS, STAT_ROWS)
    v = total_four(mine[...], [get_stats(p.at[tail])[:, :128] for p in (a, b, c)])
    out[...] = v


def stats_sum(mine, parts):
    return pl.pallas_call(
        stats_kernel,
        out_shape=jax.ShapeDtypeStruct((3, 128), F32),
        in_specs=[VMEM] * 4,
        out_specs=VMEM,
        name="stats_sum",
        compiler_params=SMALL,
    )(mine, *parts)


def labels(image_ids, text_ids, x, y, z, c, owned):
    split = (NY, 2, NX, NZ // 2, NC, owned)
    img = image_ids.reshape(split)[:, z % 2, :, z // 2, c].reshape(NY * NX, owned)
    txt = text_ids.reshape(split)[y, :, x].transpose(1, 0, 2, 3).reshape(NZ * NC, owned)
    first, second = jnp.where(c, y, x), jnp.where(c, x, y)
    at = []
    for j in range(4):
        for k in range(4):
            f, s = (first - k) % 4, (second - j) % 4
            at.append(jnp.where(c, f * NX + s, s * NX + f))
    img = img[jnp.stack(at)].reshape(1, -1)
    up = 1 - 2 * c
    sides = ((c, up), (1 - c, -up))
    at = []
    for core, sign in sides:
        order = [(0, core), (4, core), (1, core), (1, 1 - core)]
        at += [(z - sign * k) % NZ * NC + d for k, d in order]
    for core, sign in sides:
        order = [(2, core), (2, 1 - core), (3, core), (3, 1 - core)]
        at += [(z - sign * k) % NZ * NC + d for k, d in order]
    txt = txt[jnp.stack(at)].reshape(-1, 1)
    return img, txt


def shards(images, texts, image_ids, text_ids, temp_log, bias):
    owned = images.shape[0]
    batch_all = owned * NX * NY * NZ * NC
    row, col = lax.axis_index("row"), lax.axis_index("col")
    x, y, z, c = row % NX, row // (2 * NX), 2 * (col // NC) + row // NX % 2, col % NC
    scale = jnp.exp(temp_log)
    coef = jnp.concatenate([scale, bias])
    img_ids, txt_ids = labels(image_ids, text_ids, x, y, z, c, owned)

    xn, yn = normalize(images, texts)
    sibling = hop_core(yn)
    near = [xn] + [hop_first(xn, k) for k in (1, 2, 3)]
    pair = join([yn, sibling])
    next_pair = hop_z(pair, 1)
    far = hop_z(yn, 4)
    near = join(near)
    twice = hop_z(join([pair, next_pair], [near]), 2)
    image_blocks = [near] + [hop_second(near, k) for k in (1, 2, 3)]
    early = [yn, far, next_pair, sibling, hop_core(join([far, next_pair]))]
    late = [twice, hop_core(twice)]

    half = NZ * owned
    zero = jnp.zeros((3, 8, 128), F32)
    g_early, keep_e, send_e, part = tile(
        coef, img_ids, txt_ids[:half], zero, image_blocks, early, False
    )
    g_late, keep_l, send_l, stats = tile(
        coef, img_ids, txt_ids[half:], part, image_blocks, late, True
    )

    kinds = ((owned, F32), (owned, BF16), (2 * owned, F32))
    gy, far, near_y = text_add(keep_e, hop_core(send_e), kinds)
    (twice,) = text_add(keep_l, hop_core(send_l), ((4 * owned, BF16),))
    stats = stats + exchange(stats, 5, 5)
    keep, g1, g2, g3 = image_side(early + late, [g_early, g_late], [twice, far])
    parts = [hop_second(g, -k) for k, g in ((1, g1), (2, g2), (3, g3))]

    far, twice = hop_z(far, 4), hop_z(twice, -2)
    near_y = hop_z(near_add(near_y, twice, [far]), -1)
    text_parts = [gy, twice, near_y, far, hop_core(other_add(near_y, twice))]

    for bits in ((1, 1), (2, 2), (6, 3), (7, 4)):
        stats = stats + exchange(stats, *bits)
    keep, g1, g2, g3 = image_add(keep, parts, stats)
    parts = [hop_first(g, -k) for k, g in ((1, g1), (2, g2), (3, g3))]
    stats = stats_sum(stats, parts)
    stats = stats + exchange(stats, 0, 0)
    stats = stats[:, 0] * jnp.stack([jnp.float32(1 / LOG2E), scale[0], jnp.float32(1)])

    text_grad = finish(scale, texts, text_parts)
    image_grad = finish(scale, images, [keep] + parts)
    return image_grad, text_grad, stats / batch_all


def solution(mesh):
    spread = P(("row", "col"), None)
    return jax.shard_map(
        shards,
        mesh=mesh,
        in_specs=(spread, spread, P(), P(), P(), P()),
        out_specs=(spread, spread, P()),
        check_vma=False,
    )
```

```python
import functools
import itertools
import jax
import jax.numpy as jnp
from jax import lax
from jax.experimental import pallas as pl
from jax.experimental.pallas import tpu as pltpu
from jax.sharding import PartitionSpec as P

NX, NY, NZ, NC = 4, 4, 8, 2
LOG2E = 1.4426950408889634
F32, BF16 = jnp.float32, jnp.bfloat16
ANY = pl.BlockSpec(memory_space=pl.ANY)
VMEM = pl.BlockSpec(memory_space=pltpu.VMEM)
SMEM = pl.BlockSpec(memory_space=pltpu.SMEM)
BIG = pltpu.CompilerParams(vmem_limit_bytes=24 * 2**20)
SMALL = pltpu.CompilerParams(vmem_limit_bytes=12 * 2**20)
STAT_ROWS = 16


def linear(x, y, z, c):
    return (((y * 2 + z % 2) * NX + x) * (NZ // 2) + z // 2) * NC + c


def hop(a, move):
    pairs = []
    for x, y, z, c in itertools.product(range(NX), range(NY), range(NZ), range(NC)):
        dx, dy, dz, dc = move(c)
        to = linear((x + dx) % NX, (y + dy) % NY, (z + dz) % NZ, (c + dc) % NC)
        pairs.append((linear(x, y, z, c), to))
    return lax.ppermute(a, ("row", "col"), pairs)


def hop_first(a, k):
    return hop(a, lambda c: (0, k, 0, 0) if c else (k, 0, 0, 0))


def hop_second(a, k):
    return hop(a, lambda c: (k, 0, 0, 0) if c else (0, k, 0, 0))


def hop_z(a, k):
    return hop(a, lambda c: (0, 0, -k if c else k, 0))


def hop_core(a):
    return hop(a, lambda c: (0, 0, 0, 1))


def exchange(a, bit0, bit1):
    pairs = [(i, i ^ (1 << (bit1 if i % 2 else bit0))) for i in range(256)]
    return lax.ppermute(a, ("row", "col"), pairs)


def dot_t(a, b):
    return lax.dot_general(a, b, (((1,), (1,)), ((), ())), preferred_element_type=F32)


def dot_a(a, b):
    return lax.dot_general(a, b, (((0,), (0,)), ((), ())), preferred_element_type=F32)


def inverse_norm(rows):
    return lax.rsqrt(jnp.sum(rows * rows, axis=1, keepdims=True) + 1e-06)


def norm_kernel(x_ref, y_ref, xn_ref, yn_ref):
    for src, dst in ((x_ref, xn_ref), (y_ref, yn_ref)):
        rows = src[...].astype(F32)
        dst[...] = (rows * inverse_norm(rows)).astype(BF16)


def normalize(images, texts):
    like = jax.ShapeDtypeStruct(images.shape, BF16)
    return pl.pallas_call(
        norm_kernel,
        out_shape=(like, like),
        in_specs=[VMEM, VMEM],
        out_specs=(VMEM, VMEM),
        name="normalize",
        compiler_params=SMALL,
    )(images, texts)


def join_kernel(n, *refs):
    parts, out, sem = refs[:n], refs[-2], refs[-1]
    at, copies = 0, []
    for i, part in enumerate(parts):
        rows = part.shape[0]
        copies.append(pltpu.make_async_copy(part, out.at[pl.ds(at, rows)], sem.at[i]))
        at += rows
    for copy in copies:
        copy.start()
    for copy in copies:
        copy.wait()


def join(parts, after=()):
    rows = sum(p.shape[0] for p in parts)
    return pl.pallas_call(
        functools.partial(join_kernel, len(parts)),
        out_shape=jax.ShapeDtypeStruct((rows, parts[0].shape[1]), parts[0].dtype),
        in_specs=[ANY] * (len(parts) + len(after)),
        out_specs=ANY,
        scratch_shapes=[pltpu.SemaphoreType.DMA((len(parts),))],
        name="join",
        compiler_params=SMALL,
    )(*parts, *after)


def load(refs, dst, sem, first):
    out, at = [], 0
    for ref in refs:
        rows = ref.shape[0]
        copy = pltpu.make_async_copy(ref, dst.at[pl.ds(at, rows)], sem.at[first + len(out)])
        copy.start()
        out.append((at, copy))
        at += rows
    return out


def fold(v):
    u = jnp.sum(v.reshape(v.shape[0] // 8, 8, v.shape[1]), axis=0)
    return sum(u[:, k : k + 128] for k in range(0, u.shape[1], 128))


def put_stats(sums, rows, width):
    row = lax.broadcasted_iota(jnp.int32, (STAT_ROWS, width), 0)
    v = jnp.where(row % 3 == 0, sums[0], jnp.where(row % 3 == 1, sums[1], sums[2]))
    high = v.astype(BF16).astype(F32)
    mid = (v - high).astype(BF16).astype(F32)
    low = v - high - mid
    v = jnp.where(row < 3, high, jnp.where(row < 6, mid, low))
    rows[...] = jnp.where(row < 9, v, 0.0).astype(BF16)


def get_stats(rows):
    v = rows[...].astype(F32)
    return (v[0:3] + v[3:6]) + v[6:9]


def tile_kernel(nx, nt, last, *refs):
    coef, image_ids, text_ids, before = refs[:4]
    images, texts = refs[4 : 4 + nx], refs[4 + nx : 4 + nx + nt]
    grad, keep, send, stats, xb, yb, prods, sem = refs[4 + nx + nt :]
    coming = load(texts, yb, sem, 0)
    coming_x = load(images, xb, sem, nt)
    for _, copy in coming:
        copy.wait()
    rows, cols = yb.shape[0], xb.shape[0]
    wide = 256
    steps = cols // wide
    scale, shift = coef[0] * LOG2E, coef[1] * LOG2E
    acc = [before[i] for i in range(3)]

    def multiply(k):
        while coming_x and coming_x[0][0] < (k + 1) * wide:
            coming_x.pop(0)[1].wait()
        prods[k % 2] = dot_t(yb[...], xb[k * wide : (k + 1) * wide])

    multiply(0)
    for k in range(steps):
        if k + 1 < steps:
            multiply(k + 1)
        dots = prods[k % 2]
        match = text_ids[:, :1] == image_ids[:1, k * wide : (k + 1) * wide]
        logits = dots * scale + shift
        e = jnp.exp2(jnp.where(match, -logits, logits))
        p = 1.0 + e
        s = e / p
        g = jnp.where(match, -s, s)
        grad[:, k * wide : (k + 1) * wide] = g.astype(BF16)
        acc[0] += fold(jnp.log2(p[: rows // 2] * p[rows // 2 :]))
        acc[1] += fold(g * dots)
        acc[2] += fold(g)
    for i in range(3):
        if last:
            stats[pl.ds(i, 1)] = jnp.full((1, 128), jnp.sum(acc[i]))
        else:
            stats[i] = acc[i]
    part = rows // 2
    for r, out in ((part, send), (0, keep)):
        out[...] = jnp.dot(
            grad[r : r + part], xb[...], preferred_element_type=F32
        ).astype(out.dtype)


def tile(coef, image_ids, text_ids, before, images, texts, last):
    cols, rows = image_ids.shape[1], text_ids.shape[0]
    d = images[0].shape[1]
    n = len(images) + len(texts)
    return pl.pallas_call(
        functools.partial(tile_kernel, len(images), len(texts), last),
        out_shape=(
            jax.ShapeDtypeStruct((rows, cols), BF16),
            jax.ShapeDtypeStruct((rows // 2, d), F32),
            jax.ShapeDtypeStruct((rows // 2, d), BF16),
            jax.ShapeDtypeStruct((3, 128) if last else (3, 8, 128), F32),
        ),
        in_specs=[SMEM, VMEM, VMEM, VMEM] + [ANY] * n,
        out_specs=(VMEM,) * 4,
        scratch_shapes=[
            pltpu.VMEM((cols, d), BF16),
            pltpu.VMEM((rows, d), BF16),
            pltpu.VMEM((2, rows, 256), F32),
            pltpu.SemaphoreType.DMA((n,)),
        ],
        name="tile_late" if last else "tile_early",
        cost_estimate=pl.CostEstimate(
            flops=4 * rows * cols * d, bytes_accessed=8 * cols * d, transcendentals=3 * rows * cols
        ),
        compiler_params=BIG,
    )(coef, image_ids, text_ids, before, *images, *texts)


def image_side_kernel(nt, ng, blocks, *refs):
    texts, grads = refs[:nt], refs[nt : nt + ng]
    yb, gb, sem = refs[-3:]
    for _, copy in load(texts, yb, sem, 0) + load(grads, gb, sem, nt):
        copy.wait()
    outs = refs[-3 - len(blocks) : -3]
    rows = outs[0].shape[0]
    for i, out in zip(blocks, outs):
        out[...] = dot_a(gb[:, i * rows : (i + 1) * rows], yb[...]).astype(out.dtype)


def image_side(texts, grads, blocks, after=()):
    rows = sum(t.shape[0] for t in texts)
    d, cols = texts[0].shape[1], grads[0].shape[1]
    n = len(texts) + len(grads)
    size = cols // 4
    return pl.pallas_call(
        functools.partial(image_side_kernel, len(texts), len(grads), blocks),
        out_shape=tuple(jax.ShapeDtypeStruct((size, d), BF16 if i else F32) for i in blocks),
        in_specs=[ANY] * (n + len(after)),
        out_specs=(VMEM,) * len(blocks),
        scratch_shapes=[
            pltpu.VMEM((rows, d), BF16),
            pltpu.VMEM((rows, cols), BF16),
            pltpu.SemaphoreType.DMA((n,)),
        ],
        name="image_side",
        cost_estimate=pl.CostEstimate(
            flops=2 * rows * size * len(blocks) * d, bytes_accessed=8 * cols * d, transcendentals=0
        ),
        compiler_params=BIG,
    )(*texts, *grads, *after)


def total_four(own, parts):
    return (own + parts[1]) + (parts[0] + parts[2])


def image_add_kernel(own, a, b, c, stats, s1, s2, s3, keep, out1, out2, out3, total):
    rows = keep.shape[0]
    v = total_four(stats[...], [s1[...], s2[...], s3[...]])
    total[...] = v
    sums = [v[i : i + 1, :1] for i in range(3)]
    for i, out in enumerate((keep, out1, out2, out3)):
        at = pl.ds(i * rows, rows)
        out[pl.ds(0, rows)] = (
            own[at] + a[at].astype(F32) + b[at].astype(F32) + c[at].astype(F32)
        ).astype(out.dtype)
        if i:
            put_stats(sums, out.at[pl.ds(rows, STAT_ROWS)], out.shape[1])


def image_add(own, parts, stats, came):
    rows, d = own.shape[0] // 4, own.shape[1]
    sent = jax.ShapeDtypeStruct((rows + STAT_ROWS, d), BF16)
    return pl.pallas_call(
        image_add_kernel,
        out_shape=(jax.ShapeDtypeStruct((rows, d), F32), sent, sent, sent)
        + (jax.ShapeDtypeStruct(stats.shape, F32),),
        in_specs=[VMEM] * 8,
        out_specs=(VMEM,) * 5,
        name="image_add",
        compiler_params=SMALL,
    )(own, *parts, stats, *came)


def text_add_kernel(own, other, *outs):
    at = 0
    for out in outs:
        rows = pl.ds(at, out.shape[0])
        out[...] = (own[rows] + other[rows].astype(F32)).astype(out.dtype)
        at += out.shape[0]


def text_add(own, other, kinds):
    d = own.shape[1]
    return pl.pallas_call(
        text_add_kernel,
        out_shape=tuple(jax.ShapeDtypeStruct((r, d), t) for r, t in kinds),
        in_specs=[VMEM] * 2,
        out_specs=(VMEM,) * len(kinds),
        name="text_add",
        compiler_params=SMALL,
    )(own, other)


def step_add_kernel(n, a, b, stats, *refs):
    came, (out, sums) = refs[:n], refs[-2:]
    out[...] = (a[...] + b[...].astype(F32)).astype(BF16)
    came = [p[...] for p in came]
    sums[...] = total_four(stats[...], came) if n == 3 else stats[...] + came[0]


def step_add(a, b, stats, came, after=()):
    n = len(came)
    return pl.pallas_call(
        functools.partial(step_add_kernel, n),
        out_shape=(
            jax.ShapeDtypeStruct(a.shape, BF16),
            jax.ShapeDtypeStruct(stats.shape, F32),
        ),
        in_specs=[VMEM] * (3 + n) + [ANY] * len(after),
        out_specs=(VMEM,) * 2,
        name="step_add",
        compiler_params=SMALL,
    )(a, b, stats, *came, *after)


def finish_kernel(starts, scale, *refs):
    raw, parts, out = refs[0], refs[1:-1], refs[-1]
    rows = raw[...].astype(F32)
    inv = inverse_norm(rows)
    unit = rows * inv
    owned = raw.shape[0]
    g = scale[0] * sum(p[pl.ds(at, owned)].astype(F32) for p, at in zip(parts, starts))
    out[...] = (inv * (g - unit * jnp.sum(unit * g, axis=1, keepdims=True))).astype(BF16)


def finish(scale, raw, parts):
    parts, starts = zip(*parts)
    return pl.pallas_call(
        functools.partial(finish_kernel, starts),
        out_shape=jax.ShapeDtypeStruct(raw.shape, BF16),
        in_specs=[SMEM] + [VMEM] * (1 + len(parts)),
        out_specs=VMEM,
        name="finish",
        compiler_params=SMALL,
    )(scale, raw, *parts)


def stats_kernel(mine, a, b, c, out):
    tail = pl.ds(a.shape[0] - STAT_ROWS, STAT_ROWS)
    v = total_four(mine[...], [get_stats(p.at[tail])[:, :128] for p in (a, b, c)])
    out[...] = v


def stats_sum(mine, parts):
    return pl.pallas_call(
        stats_kernel,
        out_shape=jax.ShapeDtypeStruct((3, 128), F32),
        in_specs=[VMEM] * 4,
        out_specs=VMEM,
        name="stats_sum",
        compiler_params=SMALL,
    )(mine, *parts)


def labels(image_ids, text_ids, x, y, z, c, owned):
    split = (NY, 2, NX, NZ // 2, NC, owned)
    img = image_ids.reshape(split)[:, z % 2, :, z // 2, c].reshape(NY * NX, owned)
    txt = text_ids.reshape(split)[y, :, x].transpose(1, 0, 2, 3).reshape(NZ * NC, owned)
    first, second = jnp.where(c, y, x), jnp.where(c, x, y)
    at = []
    for j in range(4):
        for k in range(4):
            f, s = (first - k) % 4, (second - j) % 4
            at.append(jnp.where(c, f * NX + s, s * NX + f))
    img = img[jnp.stack(at)].reshape(1, -1)
    up = 1 - 2 * c
    sides = ((c, up), (1 - c, -up))
    at = []
    for core, sign in sides:
        order = [(0, core), (4, core), (1, core), (1, 1 - core)]
        at += [(z - sign * k) % NZ * NC + d for k, d in order]
    for core, sign in sides:
        order = [(2, core), (2, 1 - core), (3, core), (3, 1 - core)]
        at += [(z - sign * k) % NZ * NC + d for k, d in order]
    txt = txt[jnp.stack(at)].reshape(-1, 1)
    return img, txt


def shards(images, texts, image_ids, text_ids, temp_log, bias):
    owned = images.shape[0]
    batch_all = owned * NX * NY * NZ * NC
    row, col = lax.axis_index("row"), lax.axis_index("col")
    x, y, z, c = row % NX, row // (2 * NX), 2 * (col // NC) + row // NX % 2, col % NC
    scale = jnp.exp(temp_log)
    coef = jnp.concatenate([scale, bias])
    img_ids, txt_ids = labels(image_ids, text_ids, x, y, z, c, owned)

    xn, yn = normalize(images, texts)
    sibling = hop_core(yn)
    far = hop_z(yn, 4)
    near = [xn] + [hop_first(xn, k) for k in (1, 2, 3)]
    ring = [join([yn, sibling])]
    for _ in range(3):
        ring.append(hop_z(ring[-1], 1))
    near = join(near, [far])
    image_blocks = [near] + [hop_second(near, k) for k in (1, 2, 3)]
    early = [yn, far, ring[1], sibling, hop_core(join([far, ring[1]]))]
    late = [ring[2], ring[3], hop_core(ring[2]), hop_core(ring[3])]

    half = NZ * owned
    zero = jnp.zeros((3, 8, 128), F32)
    g_early, keep_e, send_e, part = tile(
        coef, img_ids, txt_ids[:half], zero, image_blocks, early, False
    )
    g_late, keep_l, send_l, stats = tile(
        coef, img_ids, txt_ids[half:], part, image_blocks, late, True
    )

    kinds = ((owned, F32), (owned, BF16), (2 * owned, F32))
    gy, far, gy1 = text_add(keep_e, hop_core(send_e), kinds)
    gy2, gy3 = text_add(keep_l, hop_core(send_l), ((2 * owned, F32), (2 * owned, BF16)))
    texts_all, grads_all = early + late, [g_early, g_late]
    sent1, sent3 = image_side(texts_all, grads_all, (1, 3), [gy3, far])

    far = hop_z(far, 4)
    step, stats = step_add(gy2, hop_z(gy3, -1), stats, [exchange(stats, 5, 5)])
    (sent2,) = image_side(texts_all, grads_all, (2,), [step])
    parts = [hop_second(g, -k) for k, g in zip((1, 2, 3), (sent1, sent2, sent3))]
    step, stats = step_add(gy1, hop_z(step, -1), stats, [exchange(stats, 1, 1)])
    (keep,) = image_side(texts_all, grads_all, (0,), [far])
    around = hop_z(step, -1)
    stats = stats + exchange(stats, 2, 2)
    text_parts = [(gy, 0), (far, 0), (around, 0), (hop_core(around), owned)]

    came = [hop_second(stats, k) for k in (1, 2, 3)]
    keep, g1, g2, g3, stats = image_add(keep, parts, stats, came)
    parts = [hop_first(g, -k) for k, g in ((1, g1), (2, g2), (3, g3))]
    stats = stats_sum(stats, parts)
    stats = stats + exchange(stats, 0, 0)
    stats = stats[:, 0] * jnp.stack([jnp.float32(1 / LOG2E), scale[0], jnp.float32(1)])

    text_grad = finish(scale, texts, text_parts)
    image_grad = finish(scale, images, [(p, 0) for p in [keep] + parts])
    return image_grad, text_grad, stats / batch_all


def solution(mesh):
    spread = P(("row", "col"), None)
    return jax.shard_map(
        shards,
        mesh=mesh,
        in_specs=(spread, spread, P(), P(), P(), P()),
        out_specs=(spread, spread, P()),
        check_vma=False,
    )
```

```python
import functools
import itertools
import jax
import jax.numpy as jnp
from jax import lax
from jax.experimental import pallas as pl
from jax.experimental.pallas import tpu as pltpu
from jax.sharding import PartitionSpec as P

NX, NY, NZ, NC = 4, 4, 8, 2
LOG2E = 1.4426950408889634
F32, BF16 = jnp.float32, jnp.bfloat16
ANY = pl.BlockSpec(memory_space=pl.ANY)
VMEM = pl.BlockSpec(memory_space=pltpu.VMEM)
SMEM = pl.BlockSpec(memory_space=pltpu.SMEM)
BIG = pltpu.CompilerParams(vmem_limit_bytes=24 * 2**20)
SMALL = pltpu.CompilerParams(vmem_limit_bytes=12 * 2**20)
STAT_ROWS = 16


def linear(x, y, z, c):
    return (((y * 2 + z % 2) * NX + x) * (NZ // 2) + z // 2) * NC + c


def hop(a, move):
    pairs = []
    for x, y, z, c in itertools.product(range(NX), range(NY), range(NZ), range(NC)):
        dx, dy, dz, dc = move(c)
        to = linear((x + dx) % NX, (y + dy) % NY, (z + dz) % NZ, (c + dc) % NC)
        pairs.append((linear(x, y, z, c), to))
    return lax.ppermute(a, ("row", "col"), pairs)


def hop_first(a, k):
    return hop(a, lambda c: (0, k, 0, 0) if c else (k, 0, 0, 0))


def hop_second(a, k):
    return hop(a, lambda c: (k, 0, 0, 0) if c else (0, k, 0, 0))


def hop_z(a, k):
    return hop(a, lambda c: (0, 0, -k if c else k, 0))


def hop_core(a):
    return hop(a, lambda c: (0, 0, 0, 1))


def exchange(a, bit0, bit1):
    pairs = [(i, i ^ (1 << (bit1 if i % 2 else bit0))) for i in range(256)]
    return lax.ppermute(a, ("row", "col"), pairs)


def dot_t(a, b):
    return lax.dot_general(a, b, (((1,), (1,)), ((), ())), preferred_element_type=F32)


def dot_a(a, b):
    return lax.dot_general(a, b, (((0,), (0,)), ((), ())), preferred_element_type=F32)


def inverse_norm(rows):
    return lax.rsqrt(jnp.sum(rows * rows, axis=1, keepdims=True) + 1e-06)


def norm_kernel(x_ref, y_ref, xn_ref, yn_ref):
    for src, dst in ((x_ref, xn_ref), (y_ref, yn_ref)):
        rows = src[...].astype(F32)
        dst[...] = (rows * inverse_norm(rows)).astype(BF16)


def normalize(images, texts):
    like = jax.ShapeDtypeStruct(images.shape, BF16)
    return pl.pallas_call(
        norm_kernel,
        out_shape=(like, like),
        in_specs=[VMEM, VMEM],
        out_specs=(VMEM, VMEM),
        name="normalize",
        compiler_params=SMALL,
    )(images, texts)


def join_kernel(n, *refs):
    parts, out, sem = refs[:n], refs[-2], refs[-1]
    at, copies = 0, []
    for i, part in enumerate(parts):
        rows = part.shape[0]
        copies.append(pltpu.make_async_copy(part, out.at[pl.ds(at, rows)], sem.at[i]))
        at += rows
    for copy in copies:
        copy.start()
    for copy in copies:
        copy.wait()


def join(parts, after=()):
    rows = sum(p.shape[0] for p in parts)
    return pl.pallas_call(
        functools.partial(join_kernel, len(parts)),
        out_shape=jax.ShapeDtypeStruct((rows, parts[0].shape[1]), parts[0].dtype),
        in_specs=[ANY] * (len(parts) + len(after)),
        out_specs=ANY,
        scratch_shapes=[pltpu.SemaphoreType.DMA((len(parts),))],
        name="join",
        compiler_params=SMALL,
    )(*parts, *after)


def load(refs, dst, sem, first):
    out, at = [], 0
    for ref in refs:
        rows = ref.shape[0]
        copy = pltpu.make_async_copy(ref, dst.at[pl.ds(at, rows)], sem.at[first + len(out)])
        copy.start()
        out.append((at, copy))
        at += rows
    return out


def fold(v):
    u = jnp.sum(v.reshape(v.shape[0] // 8, 8, v.shape[1]), axis=0)
    return sum(u[:, k : k + 128] for k in range(0, u.shape[1], 128))


def put_stats(sums, rows, width):
    row = lax.broadcasted_iota(jnp.int32, (STAT_ROWS, width), 0)
    v = jnp.where(row % 3 == 0, sums[0], jnp.where(row % 3 == 1, sums[1], sums[2]))
    high = v.astype(BF16).astype(F32)
    mid = (v - high).astype(BF16).astype(F32)
    low = v - high - mid
    v = jnp.where(row < 3, high, jnp.where(row < 6, mid, low))
    rows[...] = jnp.where(row < 9, v, 0.0).astype(BF16)


def get_stats(rows):
    v = rows[...].astype(F32)
    return (v[0:3] + v[3:6]) + v[6:9]


def tile_kernel(nx, nt, last, *refs):
    coef, image_ids, text_ids, before = refs[:4]
    images, texts = refs[4 : 4 + nx], refs[4 + nx : 4 + nx + nt]
    grad, yb, stats = refs[4 + nx + nt : 7 + nx + nt]
    prods, sem = refs[-2:]
    coming = load(texts, yb, sem, 0)
    if nx > 1:
        xb = refs[-3]
        coming_x = load(images, xb, sem, nt)
    else:
        xb, coming_x = images[0], []
    for _, copy in coming:
        copy.wait()
    rows, cols = yb.shape[0], xb.shape[0]
    wide = 256
    steps = cols // wide
    scale, shift = coef[0] * LOG2E, coef[1] * LOG2E
    acc = [before[i] for i in range(3)]

    def multiply(k):
        while coming_x and coming_x[0][0] < (k + 1) * wide:
            coming_x.pop(0)[1].wait()
        prods[k % 2] = dot_t(yb[...], xb[k * wide : (k + 1) * wide])

    multiply(0)
    for k in range(steps):
        if k + 1 < steps:
            multiply(k + 1)
        dots = prods[k % 2]
        match = text_ids[:, :1] == image_ids[:1, k * wide : (k + 1) * wide]
        logits = dots * scale + shift
        e = jnp.exp2(jnp.where(match, -logits, logits))
        p = 1.0 + e
        s = e / p
        g = jnp.where(match, -s, s)
        grad[:, k * wide : (k + 1) * wide] = g.astype(BF16)
        acc[0] += fold(jnp.log2(p[: rows // 2] * p[rows // 2 :]))
        acc[1] += fold(g * dots)
        acc[2] += fold(g)
    for i in range(3):
        if last:
            stats[pl.ds(i, 1)] = jnp.full((1, 128), jnp.sum(acc[i]))
        else:
            stats[i] = acc[i]


def tile(coef, image_ids, text_ids, before, images, texts, last):
    cols, rows = image_ids.shape[1], text_ids.shape[0]
    d = images[0].shape[1]
    nx, nt = len(images), len(texts)
    out_shape = (
        jax.ShapeDtypeStruct((rows, cols), BF16),
        jax.ShapeDtypeStruct((rows, d), BF16),
        jax.ShapeDtypeStruct((3, 128) if last else (3, 8, 128), F32),
    )
    if nx > 1:
        out_shape += (jax.ShapeDtypeStruct((cols, d), BF16),)
    return pl.pallas_call(
        functools.partial(tile_kernel, nx, nt, last),
        out_shape=out_shape,
        in_specs=[SMEM, VMEM, VMEM, VMEM] + [ANY if nx > 1 else VMEM] * nx + [ANY] * nt,
        out_specs=(VMEM,) * len(out_shape),
        scratch_shapes=[
            pltpu.VMEM((2, rows, 256), F32),
            pltpu.SemaphoreType.DMA((nx + nt,)),
        ],
        name="tile_late" if last else "tile_early",
        cost_estimate=pl.CostEstimate(
            flops=2 * rows * cols * d, bytes_accessed=4 * cols * d, transcendentals=3 * rows * cols
        ),
        compiler_params=BIG,
    )(coef, image_ids, text_ids, before, *images, *texts)


def text_side_kernel(lower, ge, gl, xb, *refs):
    out, at = refs[-1], 0
    for g in (ge, gl):
        half = g.shape[0] // 2
        first = half if lower else 0
        out[at : at + half] = jnp.dot(
            g[first : first + half], xb[...], preferred_element_type=F32
        ).astype(out.dtype)
        at += half


def text_side(grads, xb, lower, after=()):
    rows = sum(g.shape[0] for g in grads) // 2
    d = xb.shape[1]
    return pl.pallas_call(
        functools.partial(text_side_kernel, lower),
        out_shape=jax.ShapeDtypeStruct((rows, d), BF16 if lower else F32),
        in_specs=[VMEM] * 3 + [ANY] * len(after),
        out_specs=VMEM,
        name="text_side",
        cost_estimate=pl.CostEstimate(
            flops=2 * rows * xb.shape[0] * d, bytes_accessed=8 * rows * d, transcendentals=0
        ),
        compiler_params=BIG,
    )(*grads, xb, *after)


def image_side_kernel(blocks, ge, gl, ye, yl, *refs):
    outs = refs[len(refs) - len(blocks) :]
    rows = outs[0].shape[0]
    for i, out in zip(blocks, outs):
        at = slice(i * rows, (i + 1) * rows)
        out[...] = (dot_a(ge[:, at], ye[...]) + dot_a(gl[:, at], yl[...])).astype(out.dtype)


def image_side(grads, texts, blocks, after=()):
    d, cols = texts[0].shape[1], grads[0].shape[1]
    size = cols // 4
    rows = sum(t.shape[0] for t in texts)
    return pl.pallas_call(
        functools.partial(image_side_kernel, blocks),
        out_shape=tuple(jax.ShapeDtypeStruct((size, d), BF16 if i else F32) for i in blocks),
        in_specs=[VMEM] * 4 + [ANY] * len(after),
        out_specs=(VMEM,) * len(blocks),
        name="image_side",
        cost_estimate=pl.CostEstimate(
            flops=2 * rows * size * len(blocks) * d, bytes_accessed=8 * size * d, transcendentals=0
        ),
        compiler_params=BIG,
    )(*grads, *texts, *after)


def total_four(own, parts):
    return (own + parts[1]) + (parts[0] + parts[2])


def image_add_kernel(own, a, b, c, stats, keep, out1, out2, out3):
    rows = keep.shape[0]
    sums = [stats[pl.ds(i, 1)][:, :1] for i in range(3)]
    for i, out in enumerate((keep, out1, out2, out3)):
        at = pl.ds(i * rows, rows)
        out[pl.ds(0, rows)] = (
            own[at] + a[at].astype(F32) + b[at].astype(F32) + c[at].astype(F32)
        ).astype(out.dtype)
        if i:
            put_stats(sums, out.at[pl.ds(rows, STAT_ROWS)], out.shape[1])


def image_add(own, parts, stats):
    rows, d = own.shape[0] // 4, own.shape[1]
    sent = jax.ShapeDtypeStruct((rows + STAT_ROWS, d), BF16)
    return pl.pallas_call(
        image_add_kernel,
        out_shape=(jax.ShapeDtypeStruct((rows, d), F32), sent, sent, sent),
        in_specs=[VMEM] * 5,
        out_specs=(VMEM,) * 4,
        name="image_add",
        compiler_params=SMALL,
    )(own, *parts, stats)


def text_add_kernel(own, other, *outs):
    at = 0
    for out in outs:
        rows = pl.ds(at, out.shape[0])
        out[...] = (own[rows] + other[rows].astype(F32)).astype(out.dtype)
        at += out.shape[0]


def text_add(own, other, kinds):
    d = own.shape[1]
    return pl.pallas_call(
        text_add_kernel,
        out_shape=tuple(jax.ShapeDtypeStruct((r, d), t) for r, t in kinds),
        in_specs=[VMEM] * 2,
        out_specs=(VMEM,) * len(kinds),
        name="text_add",
        compiler_params=SMALL,
    )(own, other)


def step_add_kernel(a, b, stats, other, *refs):
    out, sums = refs[-2:]
    came = b.shape[0]
    out[0:came] = (a[0:came] + b[...].astype(F32)).astype(BF16)
    if came < a.shape[0]:
        out[came:] = a[came:].astype(BF16)
    sums[...] = stats[...] + other[...]


def step_add(a, b, stats, other, after):
    return pl.pallas_call(
        step_add_kernel,
        out_shape=(
            jax.ShapeDtypeStruct(a.shape, BF16),
            jax.ShapeDtypeStruct(stats.shape, F32),
        ),
        in_specs=[VMEM] * 4 + [ANY] * len(after),
        out_specs=(VMEM,) * 2,
        name="step_add",
        compiler_params=SMALL,
    )(a, b, stats, other, *after)


def finish_kernel(starts, scale, *refs):
    refs = list(refs)
    outs = refs[-2:]
    for at_list, out in zip(starts, outs):
        raw = refs.pop(0)
        parts = [refs.pop(0) for _ in at_list]
        rows = raw[...].astype(F32)
        inv = inverse_norm(rows)
        unit = rows * inv
        owned = raw.shape[0]
        g = scale[0] * sum(p[pl.ds(at, owned)].astype(F32) for p, at in zip(parts, at_list))
        out[...] = (inv * (g - unit * jnp.sum(unit * g, axis=1, keepdims=True))).astype(BF16)


def finish(scale, *sides):
    starts = [tuple(at for _, at in parts) for _, parts in sides]
    refs = [r for raw, parts in sides for r in [raw] + [p for p, _ in parts]]
    return pl.pallas_call(
        functools.partial(finish_kernel, starts),
        out_shape=tuple(jax.ShapeDtypeStruct(raw.shape, BF16) for raw, _ in sides),
        in_specs=[SMEM] + [VMEM] * len(refs),
        out_specs=(VMEM,) * len(sides),
        name="finish",
        compiler_params=SMALL,
    )(scale, *refs)


def stats_kernel(mine, a, b, c, out):
    tail = pl.ds(a.shape[0] - STAT_ROWS, STAT_ROWS)
    v = total_four(mine[...], [get_stats(p.at[tail])[:, :128] for p in (a, b, c)])
    out[...] = v


def stats_sum(mine, parts):
    return pl.pallas_call(
        stats_kernel,
        out_shape=jax.ShapeDtypeStruct((3, 128), F32),
        in_specs=[VMEM] * 4,
        out_specs=VMEM,
        name="stats_sum",
        compiler_params=SMALL,
    )(mine, *parts)


def labels(image_ids, text_ids, x, y, z, c, owned):
    split = (NY, 2, NX, NZ // 2, NC, owned)
    img = image_ids.reshape(split)[:, z % 2, :, z // 2, c].reshape(NY * NX, owned)
    txt = text_ids.reshape(split)[y, :, x].transpose(1, 0, 2, 3).reshape(NZ * NC, owned)
    first, second = jnp.where(c, y, x), jnp.where(c, x, y)
    at = []
    for j in range(4):
        for k in range(4):
            f, s = (first - k) % 4, (second - j) % 4
            at.append(jnp.where(c, f * NX + s, s * NX + f))
    img = img[jnp.stack(at)].reshape(1, -1)
    up = 1 - 2 * c
    sides = ((c, up), (1 - c, -up))
    at = []
    for core, sign in sides:
        order = [(0, core), (1, core), (1, 1 - core)]
        at += [(z - sign * k) % NZ * NC + d for k, d in order]
    for core, sign in sides:
        order = [(4, core)] + [(k, d) for k in (2, 3) for d in (core, 1 - core)]
        at += [(z - sign * k) % NZ * NC + d for k, d in order]
    txt = txt[jnp.stack(at)].reshape(-1, 1)
    return img, txt


def shards(images, texts, image_ids, text_ids, temp_log, bias):
    owned = images.shape[0]
    batch_all = owned * NX * NY * NZ * NC
    row, col = lax.axis_index("row"), lax.axis_index("col")
    x, y, z, c = row % NX, row // (2 * NX), 2 * (col // NC) + row // NX % 2, col % NC
    scale = jnp.exp(temp_log)
    coef = jnp.concatenate([scale, bias])
    img_ids, txt_ids = labels(image_ids, text_ids, x, y, z, c, owned)

    xn, yn = normalize(images, texts)
    sibling = hop_core(yn)
    near = join([xn] + [hop_first(xn, k) for k in (1, 2, 3)])
    ring = [join([yn, sibling])]
    ring.append(join([hop_z(ring[0], 1)], [near]))
    for _ in range(3):
        ring.append(hop_z(ring[-1], 1))
    image_blocks = [near] + [hop_second(near, k) for k in (1, 2, 3)]
    far = [ring[4][:owned], ring[4][owned:]]
    early = [yn, ring[1], sibling, hop_core(ring[1])]
    late = [far[0], ring[2], ring[3], far[1], hop_core(ring[2]), hop_core(ring[3])]

    cut = 6 * owned
    zero = jnp.zeros((3, 8, 128), F32)
    g_early, t_early, part, xb = tile(
        coef, img_ids, txt_ids[:cut], zero, image_blocks, early, False
    )
    g_late, t_late, stats = tile(coef, img_ids, txt_ids[cut:], part, [xb], late, True)
    grads, rows = [g_early, g_late], [t_early, t_late]

    send = text_side(grads, xb, True)
    keep = text_side(grads, xb, False, [send])
    kinds = ((owned, F32), (2 * owned, F32), (owned, BF16), (2 * owned, F32), (2 * owned, F32))
    gy, gy1, far, gy2, gy3 = text_add(keep, hop_core(send), kinds)
    sent1, sent3 = image_side(grads, rows, (1, 3), [far])
    step, stats = step_add(gy3, hop_z(far, -1), stats, exchange(stats, 5, 5), [sent1])
    (sent2,) = image_side(grads, rows, (2,), [step])
    parts = [hop_second(g, -k) for k, g in zip((1, 2, 3), (sent1, sent2, sent3))]
    step, stats = step_add(gy2, hop_z(step, -1), stats, exchange(stats, 1, 1), [sent2])
    (own,) = image_side(grads, rows, (0,), [step])
    step, stats = step_add(gy1, hop_z(step, -1), stats, exchange(stats, 2, 2), [own])
    around = hop_z(step, -1)
    text_parts = [(gy, 0), (around, 0), (hop_core(around), owned)]
    for bits in ((6, 3), (7, 4)):
        stats = stats + exchange(stats, *bits)

    keep, g1, g2, g3 = image_add(own, parts, stats)
    parts = [hop_first(g, -k) for k, g in ((1, g1), (2, g2), (3, g3))]
    stats = stats_sum(stats, parts)
    stats = stats + exchange(stats, 0, 0)
    stats = stats[:, 0] * jnp.stack([jnp.float32(1 / LOG2E), scale[0], jnp.float32(1)])

    image_grad, text_grad = finish(
        scale, (images, [(p, 0) for p in [keep] + parts]), (texts, text_parts)
    )
    return image_grad, text_grad, stats / batch_all


def solution(mesh):
    spread = P(("row", "col"), None)
    return jax.shard_map(
        shards,
        mesh=mesh,
        in_specs=(spread, spread, P(), P(), P(), P()),
        out_specs=(spread, spread, P()),
        check_vma=False,
    )
```

```python
import functools
import itertools
import jax
import jax.numpy as jnp
from jax import lax
from jax.experimental import pallas as pl
from jax.experimental.pallas import tpu as pltpu
from jax.sharding import PartitionSpec as P

NX, NY, NZ, NC = 4, 4, 8, 2
LOG2E = 1.4426950408889634
F32, BF16 = jnp.float32, jnp.bfloat16
ANY = pl.BlockSpec(memory_space=pl.ANY)
HBM = pl.BlockSpec(memory_space=pltpu.HBM)
STAT_ROWS = 16
VMEM = pl.BlockSpec(memory_space=pltpu.VMEM)
SMEM = pl.BlockSpec(memory_space=pltpu.SMEM)
BIG = pltpu.CompilerParams(vmem_limit_bytes=24 * 2**20)
SMALL = pltpu.CompilerParams(vmem_limit_bytes=12 * 2**20)


def linear(x, y, z, c):
    return (((y * 2 + z % 2) * NX + x) * (NZ // 2) + z // 2) * NC + c


def hop(a, move):
    pairs = []
    for x, y, z, c in itertools.product(range(NX), range(NY), range(NZ), range(NC)):
        dx, dy, dz, dc = move(c)
        to = linear((x + dx) % NX, (y + dy) % NY, (z + dz) % NZ, (c + dc) % NC)
        pairs.append((linear(x, y, z, c), to))
    return lax.ppermute(a, ("row", "col"), pairs)


def hop_first(a, k):
    return hop(a, lambda c: (0, k, 0, 0) if c else (k, 0, 0, 0))


def hop_second(a, k):
    return hop(a, lambda c: (k, 0, 0, 0) if c else (0, k, 0, 0))


def hop_z(a, k):
    return hop(a, lambda c: (0, 0, -k if c else k, 0))


def hop_core(a):
    return hop(a, lambda c: (0, 0, 0, 1))


def exchange(a, bit0, bit1):
    pairs = [(i, i ^ (1 << (bit1 if i % 2 else bit0))) for i in range(256)]
    return lax.ppermute(a, ("row", "col"), pairs)


def dot_t(a, b):
    return lax.dot_general(a, b, (((1,), (1,)), ((), ())), preferred_element_type=F32)


def dot_a(a, b):
    return lax.dot_general(a, b, (((0,), (0,)), ((), ())), preferred_element_type=F32)


def inverse_norm(rows):
    return lax.rsqrt(jnp.sum(rows * rows, axis=1, keepdims=True) + 1e-06)


def norm_kernel(x_ref, y_ref, xn_ref, yn_ref, held, sem):
    copies = [
        pltpu.make_async_copy(src, held.at[i], sem.at[i]) for i, src in enumerate((x_ref, y_ref))
    ]
    for copy in copies:
        copy.start()
    for i, dst in enumerate((xn_ref, yn_ref)):
        copies[i].wait()
        rows = held[i].astype(F32)
        dst[...] = (rows * inverse_norm(rows)).astype(BF16)


def normalize(images, texts):
    like = jax.ShapeDtypeStruct(images.shape, BF16)
    return pl.pallas_call(
        norm_kernel,
        out_shape=(like, like),
        in_specs=[HBM, HBM],
        out_specs=(VMEM, VMEM),
        scratch_shapes=[pltpu.VMEM((2,) + images.shape, BF16), pltpu.SemaphoreType.DMA((2,))],
        name="normalize",
        compiler_params=SMALL,
    )(images, texts)


def join_kernel(n, *refs):
    out, at = refs[-1], 0
    for part in refs[:n]:
        rows = part.shape[0]
        out[at : at + rows] = part[...]
        at += rows


def join(parts, after=()):
    rows = sum(p.shape[0] for p in parts)
    return pl.pallas_call(
        functools.partial(join_kernel, len(parts)),
        out_shape=jax.ShapeDtypeStruct((rows, parts[0].shape[1]), parts[0].dtype),
        in_specs=[VMEM] * len(parts) + [ANY] * len(after),
        out_specs=VMEM,
        name="join",
        compiler_params=SMALL,
    )(*parts, *after)


def load(refs, dst, sem, first):
    out, at = [], 0
    for ref in refs:
        rows = ref.shape[0]
        copy = pltpu.make_async_copy(ref, dst.at[pl.ds(at, rows)], sem.at[first + len(out)])
        copy.start()
        out.append((at, copy))
        at += rows
    return out


def fold(v):
    u = jnp.sum(v.reshape(v.shape[0] // 8, 8, v.shape[1]), axis=0)
    return sum(u[:, k : k + 128] for k in range(0, u.shape[1], 128))


def put_stats(sums, rows, width):
    row = lax.broadcasted_iota(jnp.int32, (STAT_ROWS, width), 0)
    v = jnp.where(row % 3 == 0, sums[0], jnp.where(row % 3 == 1, sums[1], sums[2]))
    high = v.astype(BF16).astype(F32)
    mid = (v - high).astype(BF16).astype(F32)
    low = v - high - mid
    v = jnp.where(row < 3, high, jnp.where(row < 6, mid, low))
    rows[...] = jnp.where(row < 9, v, 0.0).astype(BF16)


def get_stats(rows):
    v = rows[...].astype(F32)
    return (v[0:3] + v[3:6]) + v[6:9]


def tile_kernel(nx, nt, last, *refs):
    coef, image_ids, text_ids, before = refs[:4]
    images, texts = refs[4 : 4 + nx], refs[4 + nx : 4 + nx + nt]
    grad, yb, stats = refs[4 + nx + nt : 7 + nx + nt]
    prods, sem = refs[-2:]
    coming = load(texts, yb, sem, 0)
    if nx > 1:
        xb = refs[-3]
        coming_x = load(images, xb, sem, nt)
    else:
        xb, coming_x = images[0], []
    for _, copy in coming:
        copy.wait()
    rows, cols = yb.shape[0], xb.shape[0]
    wide = 256
    steps = cols // wide
    scale, shift = coef[0] * LOG2E, coef[1] * LOG2E
    acc = [before[i] for i in range(3)]

    def multiply(k):
        while coming_x and coming_x[0][0] < (k + 1) * wide:
            coming_x.pop(0)[1].wait()
        prods[k % 2] = dot_t(yb[...], xb[k * wide : (k + 1) * wide])

    multiply(0)
    for k in range(steps):
        if k + 1 < steps:
            multiply(k + 1)
        dots = prods[k % 2]
        match = text_ids[:, :1] == image_ids[:1, k * wide : (k + 1) * wide]
        logits = dots * scale + shift
        e = jnp.exp2(jnp.where(match, -logits, logits))
        p = 1.0 + e
        s = e / p
        g = jnp.where(match, -s, s)
        grad[:, k * wide : (k + 1) * wide] = g.astype(BF16)
        acc[0] += fold(jnp.log2(p[: rows // 2] * p[rows // 2 :]))
        acc[1] += fold(g * dots)
        acc[2] += fold(g)
    for i in range(3):
        if last:
            stats[pl.ds(i, 1)] = jnp.full((1, 128), jnp.sum(acc[i]))
        else:
            stats[i] = acc[i]


def tile(coef, image_ids, text_ids, before, images, texts, last):
    cols, rows = image_ids.shape[1], text_ids.shape[0]
    d = images[0].shape[1]
    nx, nt = len(images), len(texts)
    out_shape = (
        jax.ShapeDtypeStruct((rows, cols), BF16),
        jax.ShapeDtypeStruct((rows, d), BF16),
        jax.ShapeDtypeStruct((3, 128) if last else (3, 8, 128), F32),
    )
    if nx > 1:
        out_shape += (jax.ShapeDtypeStruct((cols, d), BF16),)
    return pl.pallas_call(
        functools.partial(tile_kernel, nx, nt, last),
        out_shape=out_shape,
        in_specs=[SMEM, VMEM, VMEM, VMEM] + [ANY if nx > 1 else VMEM] * nx + [ANY] * nt,
        out_specs=(VMEM,) * len(out_shape),
        scratch_shapes=[
            pltpu.VMEM((2, rows, 256), F32),
            pltpu.SemaphoreType.DMA((nx + nt,)),
        ],
        name="tile_late" if last else "tile_early",
        cost_estimate=pl.CostEstimate(
            flops=2 * rows * cols * d, bytes_accessed=4 * cols * d, transcendentals=3 * rows * cols
        ),
        compiler_params=BIG,
    )(coef, image_ids, text_ids, before, *images, *texts)


def text_side_kernel(lower, ge, gl, xb, *refs):
    out, at = refs[-1], 0
    for g in (ge, gl):
        half = g.shape[0] // 2
        first = half if lower else 0
        out[at : at + half] = jnp.dot(
            g[first : first + half], xb[...], preferred_element_type=F32
        ).astype(out.dtype)
        at += half


def text_side(grads, xb, lower, after=()):
    rows = sum(g.shape[0] for g in grads) // 2
    d = xb.shape[1]
    return pl.pallas_call(
        functools.partial(text_side_kernel, lower),
        out_shape=jax.ShapeDtypeStruct((rows, d), BF16 if lower else F32),
        in_specs=[VMEM] * 3 + [ANY] * len(after),
        out_specs=VMEM,
        name="text_side",
        cost_estimate=pl.CostEstimate(
            flops=2 * rows * xb.shape[0] * d, bytes_accessed=8 * rows * d, transcendentals=0
        ),
        compiler_params=BIG,
    )(*grads, xb, *after)


def image_side_kernel(blocks, ge, gl, ye, yl, *refs):
    outs = refs[len(refs) - len(blocks) :]
    rows = outs[0].shape[0]
    for i, out in zip(blocks, outs):
        at = slice(i * rows, (i + 1) * rows)
        out[...] = (dot_a(ge[:, at], ye[...]) + dot_a(gl[:, at], yl[...])).astype(out.dtype)


def image_side(grads, texts, blocks, after=()):
    d, cols = texts[0].shape[1], grads[0].shape[1]
    size = cols // 4
    rows = sum(t.shape[0] for t in texts)
    return pl.pallas_call(
        functools.partial(image_side_kernel, blocks),
        out_shape=tuple(jax.ShapeDtypeStruct((size, d), BF16 if i else F32) for i in blocks),
        in_specs=[VMEM] * 4 + [ANY] * len(after),
        out_specs=(VMEM,) * len(blocks),
        name="image_side",
        cost_estimate=pl.CostEstimate(
            flops=2 * rows * size * len(blocks) * d, bytes_accessed=8 * size * d, transcendentals=0
        ),
        compiler_params=BIG,
    )(*grads, *texts, *after)


def total_four(own, parts):
    return (own + parts[1]) + (parts[0] + parts[2])


def image_add_kernel(own, a, b, c, stats, other, keep, out1, out2, out3, total):
    rows = keep.shape[0]
    v = stats[...] + other[...]
    total[...] = v
    sums = [v[i : i + 1, :1] for i in range(3)]
    for i, out in enumerate((keep, out1, out2, out3)):
        at = pl.ds(i * rows, rows)
        out[pl.ds(0, rows)] = (
            own[at] + a[at].astype(F32) + b[at].astype(F32) + c[at].astype(F32)
        ).astype(out.dtype)
        if i:
            put_stats(sums, out.at[pl.ds(rows, STAT_ROWS)], out.shape[1])


def image_add(own, parts, stats, other):
    rows, d = own.shape[0] // 4, own.shape[1]
    sent = jax.ShapeDtypeStruct((rows + STAT_ROWS, d), BF16)
    return pl.pallas_call(
        image_add_kernel,
        out_shape=(jax.ShapeDtypeStruct((rows, d), F32), sent, sent, sent)
        + (jax.ShapeDtypeStruct(stats.shape, F32),),
        in_specs=[VMEM] * 6,
        out_specs=(VMEM,) * 5,
        name="image_add",
        compiler_params=SMALL,
    )(own, *parts, stats, other)


def text_add_kernel(runs, own, other, stats, c1, c2, c3, *refs):
    outs, sums = refs[:-1], refs[-1]
    for (at_own, at_other, rows, _), out in zip(runs, outs):
        out[...] = (
            own[pl.ds(at_own, rows)] + other[pl.ds(at_other, rows)].astype(F32)
        ).astype(out.dtype)
    sums[...] = total_four(stats[...], [c1[...], c2[...], c3[...]])


def text_add(own, other, runs, stats, came):
    d = own.shape[1]
    return pl.pallas_call(
        functools.partial(text_add_kernel, runs),
        out_shape=tuple(jax.ShapeDtypeStruct((rows, d), t) for _, _, rows, t in runs)
        + (jax.ShapeDtypeStruct(stats.shape, F32),),
        in_specs=[VMEM] * 6,
        out_specs=(VMEM,) * (len(runs) + 1),
        name="text_add",
        compiler_params=SMALL,
    )(own, other, stats, *came)


def step_add_kernel(with_stats, a, b, *refs):
    out = refs[-2] if with_stats else refs[-1]
    came = b.shape[0]
    out[0:came] = (a[0:came] + b[...].astype(F32)).astype(BF16)
    if came < a.shape[0]:
        out[came:] = a[came:].astype(BF16)
    if with_stats:
        refs[-1][...] = refs[0][...] + refs[1][...]


def step_add(a, b, stats, after):
    return pl.pallas_call(
        functools.partial(step_add_kernel, bool(stats)),
        out_shape=(jax.ShapeDtypeStruct(a.shape, BF16),)
        + tuple(jax.ShapeDtypeStruct(s.shape, F32) for s in stats[:1]),
        in_specs=[VMEM] * (2 + len(stats)) + [ANY] * len(after),
        out_specs=(VMEM,) * (1 + len(stats[:1])),
        name="step_add",
        compiler_params=SMALL,
    )(a, b, *stats, *after)


def lower_kernel(a, *refs):
    refs[-1][...] = a[pl.ds(a.shape[0] // 2, a.shape[0] // 2)]


def lower(a, after):
    return pl.pallas_call(
        lower_kernel,
        out_shape=jax.ShapeDtypeStruct((a.shape[0] // 2, a.shape[1]), a.dtype),
        in_specs=[VMEM, ANY],
        out_specs=VMEM,
        name="lower",
        compiler_params=SMALL,
    )(a, after)


def finish_kernel(starts, scale, *refs):
    refs = list(refs)
    outs = refs[-2:]
    for at_list, out in zip(starts, outs):
        raw = refs.pop(0)
        parts = [refs.pop(0) for _ in at_list]
        rows = raw[...].astype(F32)
        inv = inverse_norm(rows)
        unit = rows * inv
        owned = raw.shape[0]
        g = scale[0] * sum(p[pl.ds(at, owned)].astype(F32) for p, at in zip(parts, at_list))
        out[...] = (inv * (g - unit * jnp.sum(unit * g, axis=1, keepdims=True))).astype(BF16)


def finish(scale, *sides):
    starts = [tuple(at for _, at in parts) for _, parts in sides]
    refs = [r for raw, parts in sides for r in [raw] + [p for p, _ in parts]]
    return pl.pallas_call(
        functools.partial(finish_kernel, starts),
        out_shape=tuple(jax.ShapeDtypeStruct(raw.shape, BF16) for raw, _ in sides),
        in_specs=[SMEM] + [VMEM] * len(refs),
        out_specs=(VMEM,) * len(sides),
        name="finish",
        compiler_params=SMALL,
    )(scale, *refs)


def stats_kernel(mine, a, b, c, out):
    tail = pl.ds(a.shape[0] - STAT_ROWS, STAT_ROWS)
    out[...] = total_four(mine[...], [get_stats(p.at[tail])[:, :128] for p in (a, b, c)])


def stats_sum(mine, parts):
    return pl.pallas_call(
        stats_kernel,
        out_shape=jax.ShapeDtypeStruct((3, 128), F32),
        in_specs=[VMEM] * 4,
        out_specs=VMEM,
        name="stats_sum",
        compiler_params=SMALL,
    )(mine, *parts)


def scalars_kernel(batch, scale, a, b, after, out):
    v = (a[...] + b[...]) * (1.0 / batch)
    row = lax.broadcasted_iota(jnp.int32, v.shape, 0)
    out[...] = v * jnp.where(row == 0, 1 / LOG2E, jnp.where(row == 1, scale[0], 1.0))


def scalars(scale, a, b, batch, after):
    return pl.pallas_call(
        functools.partial(scalars_kernel, batch),
        out_shape=jax.ShapeDtypeStruct(a.shape, F32),
        in_specs=[SMEM] + [VMEM] * 2 + [ANY],
        out_specs=VMEM,
        name="scalars",
        compiler_params=SMALL,
    )(scale, a, b, after)


def labels(image_ids, text_ids, x, y, z, c, owned):
    split = (NY, 2, NX, NZ // 2, NC, owned)
    img = image_ids.reshape(split)[:, z % 2, :, z // 2, c].reshape(NY * NX, owned)
    txt = text_ids.reshape(split)[y, :, x].transpose(1, 0, 2, 3).reshape(NZ * NC, owned)
    first, second = jnp.where(c, y, x), jnp.where(c, x, y)
    at = []
    for j in range(4):
        for k in range(4):
            f, s = (first - k) % 4, (second - j) % 4
            at.append(jnp.where(c, f * NX + s, s * NX + f))
    img = img[jnp.stack(at)].reshape(1, -1)
    up = 1 - 2 * c
    sides = ((c, up), (1 - c, -up))
    at = []
    for core, sign in sides:
        order = [(0, core), (1, core), (1, 1 - core)]
        at += [(z - sign * k) % NZ * NC + d for k, d in order]
    for core, sign in sides:
        order = [(k, d) for k in (2, 3) for d in (core, 1 - core)]
        order.insert(4 if core is c else 0, (4, core))
        at += [(z - sign * k) % NZ * NC + d for k, d in order]
    txt = txt[jnp.stack(at)].reshape(-1, 1)
    return img, txt


def shards(images, texts, image_ids, text_ids, temp_log, bias):
    owned = images.shape[0]
    batch_all = owned * NX * NY * NZ * NC
    row, col = lax.axis_index("row"), lax.axis_index("col")
    x, y, z, c = row % NX, row // (2 * NX), 2 * (col // NC) + row // NX % 2, col % NC
    scale = jnp.exp(temp_log)
    coef = jnp.concatenate([scale, bias])
    img_ids, txt_ids = labels(image_ids, text_ids, x, y, z, c, owned)

    xn, yn = normalize(images, texts)
    sibling = hop_core(yn)
    near = join([xn] + [hop_first(xn, k) for k in (1, 2, 3)])
    ring = [join([yn, sibling])]
    ring.append(join([hop_z(ring[0], 1)], [near]))
    for _ in range(3):
        ring.append(hop_z(ring[-1], 1))
    image_blocks = [near] + [hop_second(near, k) for k in (1, 2, 3)]
    early = [yn, ring[1], sibling, hop_core(ring[1])]
    late = [ring[2], ring[3], ring[4], hop_core(ring[2]), hop_core(ring[3])]

    cut = 6 * owned
    zero = jnp.zeros((3, 8, 128), F32)
    g_early, t_early, part, xb = tile(
        coef, img_ids, txt_ids[:cut], zero, image_blocks, early, False
    )
    g_late, t_late, stats = tile(coef, img_ids, txt_ids[cut:], part, [xb], late, True)
    grads, rows = [g_early, g_late], [t_early, t_late]

    send = text_side(grads, xb, True)
    keep = text_side(grads, xb, False, [send])
    runs = (
        (0, 0, owned, F32),
        (owned, owned, 2 * owned, F32),
        (3 * owned, 4 * owned, 2 * owned, F32),
        (5 * owned, 6 * owned, 2 * owned, F32),
        (7 * owned, 3 * owned, owned, BF16),
    )
    came = [hop(stats, lambda c, k=k: (0, 0, 2 * k, 0)) for k in (1, 2, 3)]
    gy, gy1, gy2, gy3, far, stats = text_add(keep, hop_core(send), runs, stats, came)
    sent1, sent3 = image_side(grads, rows, (1, 3), [far])
    (sent2,) = image_side(grads, rows, (2,), [sent1])
    parts = [hop_second(g, -k) for k, g in zip((1, 2, 3), (sent1, sent2, sent3))]
    step, stats = step_add(gy3, hop_z(far, -1), [stats, exchange(stats, 5, 5)], [sent2])
    (own,) = image_side(grads, rows, (0,), [step])
    step, stats = step_add(gy2, hop_z(step, -1), [stats, exchange(stats, 6, 3)], [own])
    keep, g1, g2, g3, stats = image_add(own, parts, stats, exchange(stats, 7, 4))
    (step,) = step_add(gy1, hop_z(step, -1), [], [keep])
    around = hop_z(step, -1)
    parts = [hop_first(g, -k) for k, g in ((1, g1), (2, g2), (3, g3))]
    text_parts = [(gy, 0), (around, 0), (hop_core(lower(around, parts[2])), 0)]

    stats = stats_sum(stats, parts)
    image_grad, text_grad = finish(
        scale, (images, [(p, 0) for p in [keep] + parts]), (texts, text_parts)
    )
    total = scalars(scale, stats, exchange(stats, 0, 0), batch_all, image_grad)
    return image_grad, text_grad, total[:, 0]


def solution(mesh):
    spread = P(("row", "col"), None)
    return jax.shard_map(
        shards,
        mesh=mesh,
        in_specs=(spread, spread, P(), P(), P(), P()),
        out_specs=(spread, spread, P()),
        check_vma=False,
    )
```

```python
import functools
import itertools
import jax
import jax.numpy as jnp
from jax import lax
from jax.experimental import pallas as pl
from jax.experimental.pallas import tpu as pltpu
from jax.sharding import PartitionSpec as P

NX, NY, NZ, NC = 4, 4, 8, 2
LOG2E = 1.4426950408889634
F32, BF16 = jnp.float32, jnp.bfloat16
ANY = pl.BlockSpec(memory_space=pl.ANY)
STAT_ROWS = 16
VMEM = pl.BlockSpec(memory_space=pltpu.VMEM)
SMEM = pl.BlockSpec(memory_space=pltpu.SMEM)
BIG = pltpu.CompilerParams(vmem_limit_bytes=24 * 2**20)
SMALL = pltpu.CompilerParams(vmem_limit_bytes=12 * 2**20)


def linear(x, y, z, c):
    return (((y * 2 + z % 2) * NX + x) * (NZ // 2) + z // 2) * NC + c


def hop(a, move):
    pairs = []
    for x, y, z, c in itertools.product(range(NX), range(NY), range(NZ), range(NC)):
        dx, dy, dz, dc = move(c)
        to = linear((x + dx) % NX, (y + dy) % NY, (z + dz) % NZ, (c + dc) % NC)
        pairs.append((linear(x, y, z, c), to))
    return lax.ppermute(a, ("row", "col"), pairs)


def hop_first(a, k):
    return hop(a, lambda c: (0, k, 0, 0) if c else (k, 0, 0, 0))


def hop_second(a, k):
    return hop(a, lambda c: (k, 0, 0, 0) if c else (0, k, 0, 0))


def hop_z(a, k):
    return hop(a, lambda c: (0, 0, -k if c else k, 0))


def hop_core(a):
    return hop(a, lambda c: (0, 0, 0, 1))


def exchange(a, bit0, bit1):
    pairs = [(i, i ^ (1 << (bit1 if i % 2 else bit0))) for i in range(256)]
    return lax.ppermute(a, ("row", "col"), pairs)


def dot_t(a, b):
    return lax.dot_general(a, b, (((1,), (1,)), ((), ())), preferred_element_type=F32)


def dot_a(a, b):
    return lax.dot_general(a, b, (((0,), (0,)), ((), ())), preferred_element_type=F32)


def inverse_norm(rows):
    return lax.rsqrt(jnp.sum(rows * rows, axis=1, keepdims=True) + 1e-06)


def norm_kernel(raw, *refs):
    rows = raw[...].astype(F32)
    refs[-1][...] = (rows * inverse_norm(rows)).astype(BF16)


def normalize(raw, after=()):
    return pl.pallas_call(
        norm_kernel,
        out_shape=jax.ShapeDtypeStruct(raw.shape, BF16),
        in_specs=[VMEM] + [ANY] * len(after),
        out_specs=VMEM,
        name="normalize",
        compiler_params=SMALL,
    )(raw, *after)


def join_kernel(n, *refs):
    out, at = refs[-1], 0
    for part in refs[:n]:
        rows = part.shape[0]
        out[at : at + rows] = part[...]
        at += rows


def join(parts, after=()):
    rows = sum(p.shape[0] for p in parts)
    return pl.pallas_call(
        functools.partial(join_kernel, len(parts)),
        out_shape=jax.ShapeDtypeStruct((rows, parts[0].shape[1]), parts[0].dtype),
        in_specs=[VMEM] * len(parts) + [ANY] * len(after),
        out_specs=VMEM,
        name="join",
        compiler_params=SMALL,
    )(*parts, *after)


def load(refs, dst, sem, first):
    out, at = [], 0
    for ref in refs:
        rows = ref.shape[0]
        copy = pltpu.make_async_copy(ref, dst.at[pl.ds(at, rows)], sem.at[first + len(out)])
        copy.start()
        out.append((at, copy))
        at += rows
    return out


def fold(v):
    u = jnp.sum(v.reshape(v.shape[0] // 8, 8, v.shape[1]), axis=0)
    return sum(u[:, k : k + 128] for k in range(0, u.shape[1], 128))


def put_stats(sums, rows, width):
    row = lax.broadcasted_iota(jnp.int32, (STAT_ROWS, width), 0)
    v = jnp.where(row % 3 == 0, sums[0], jnp.where(row % 3 == 1, sums[1], sums[2]))
    high = v.astype(BF16).astype(F32)
    mid = (v - high).astype(BF16).astype(F32)
    low = v - high - mid
    v = jnp.where(row < 3, high, jnp.where(row < 6, mid, low))
    rows[...] = jnp.where(row < 9, v, 0.0).astype(BF16)


def get_stats(rows):
    v = rows[...].astype(F32)
    return (v[0:3] + v[3:6]) + v[6:9]


def tile_kernel(nx, nt, last, *refs):
    coef, image_ids, text_ids, before = refs[:4]
    images, texts = refs[4 : 4 + nx], refs[4 + nx : 4 + nx + nt]
    grad, yb, stats = refs[4 + nx + nt : 7 + nx + nt]
    prods, sem = refs[-2:]
    coming = load(texts, yb, sem, 0)
    if nx > 1:
        xb = refs[-3]
        coming_x = load(images, xb, sem, nt)
    else:
        xb, coming_x = images[0], []
    for _, copy in coming:
        copy.wait()
    rows, cols = yb.shape[0], xb.shape[0]
    wide = 256
    steps = cols // wide
    scale, shift = coef[0] * LOG2E, coef[1] * LOG2E
    acc = [before[i] for i in range(3)]

    def multiply(k):
        while coming_x and coming_x[0][0] < (k + 1) * wide:
            coming_x.pop(0)[1].wait()
        prods[k % 2] = dot_t(yb[...], xb[k * wide : (k + 1) * wide])

    multiply(0)
    for k in range(steps):
        if k + 1 < steps:
            multiply(k + 1)
        dots = prods[k % 2]
        match = text_ids[:, :1] == image_ids[:1, k * wide : (k + 1) * wide]
        logits = dots * scale + shift
        e = jnp.exp2(jnp.where(match, -logits, logits))
        p = 1.0 + e
        s = e / p
        g = jnp.where(match, -s, s)
        grad[:, k * wide : (k + 1) * wide] = g.astype(BF16)
        acc[0] += fold(jnp.log2(p[: rows // 2] * p[rows // 2 :]))
        acc[1] += fold(g * dots)
        acc[2] += fold(g)
    for i in range(3):
        if last:
            stats[pl.ds(i, 1)] = jnp.full((1, 128), jnp.sum(acc[i]))
        else:
            stats[i] = acc[i]


def tile(coef, image_ids, text_ids, before, images, texts, last):
    cols, rows = image_ids.shape[1], text_ids.shape[0]
    d = images[0].shape[1]
    nx, nt = len(images), len(texts)
    out_shape = (
        jax.ShapeDtypeStruct((rows, cols), BF16),
        jax.ShapeDtypeStruct((rows, d), BF16),
        jax.ShapeDtypeStruct((3, 128) if last else (3, 8, 128), F32),
    )
    if nx > 1:
        out_shape += (jax.ShapeDtypeStruct((cols, d), BF16),)
    return pl.pallas_call(
        functools.partial(tile_kernel, nx, nt, last),
        out_shape=out_shape,
        in_specs=[SMEM, VMEM, VMEM, VMEM] + [ANY if nx > 1 else VMEM] * nx + [ANY] * nt,
        out_specs=(VMEM,) * len(out_shape),
        scratch_shapes=[
            pltpu.VMEM((2, rows, 256), F32),
            pltpu.SemaphoreType.DMA((nx + nt,)),
        ],
        name="tile_late" if last else "tile_early",
        cost_estimate=pl.CostEstimate(
            flops=2 * rows * cols * d, bytes_accessed=4 * cols * d, transcendentals=3 * rows * cols
        ),
        compiler_params=BIG,
    )(coef, image_ids, text_ids, before, *images, *texts)


def text_side_kernel(lower, ge, gl, xb, *refs):
    out, at = refs[-1], 0
    for g in (ge, gl):
        half = g.shape[0] // 2
        first = half if lower else 0
        out[at : at + half] = jnp.dot(
            g[first : first + half], xb[...], preferred_element_type=F32
        ).astype(out.dtype)
        at += half


def text_side(grads, xb, lower, after=()):
    rows = sum(g.shape[0] for g in grads) // 2
    d = xb.shape[1]
    return pl.pallas_call(
        functools.partial(text_side_kernel, lower),
        out_shape=jax.ShapeDtypeStruct((rows, d), BF16 if lower else F32),
        in_specs=[VMEM] * 3 + [ANY] * len(after),
        out_specs=VMEM,
        name="text_side",
        cost_estimate=pl.CostEstimate(
            flops=2 * rows * xb.shape[0] * d, bytes_accessed=8 * rows * d, transcendentals=0
        ),
        compiler_params=BIG,
    )(*grads, xb, *after)


def image_side_kernel(blocks, ge, gl, ye, yl, *refs):
    outs = refs[len(refs) - len(blocks) :]
    rows = outs[0].shape[0]
    for i, out in zip(blocks, outs):
        at = slice(i * rows, (i + 1) * rows)
        out[...] = (dot_a(ge[:, at], ye[...]) + dot_a(gl[:, at], yl[...])).astype(out.dtype)


def image_side(grads, texts, blocks, after=()):
    d, cols = texts[0].shape[1], grads[0].shape[1]
    size = cols // 4
    rows = sum(t.shape[0] for t in texts)
    return pl.pallas_call(
        functools.partial(image_side_kernel, blocks),
        out_shape=tuple(jax.ShapeDtypeStruct((size, d), BF16 if i else F32) for i in blocks),
        in_specs=[VMEM] * 4 + [ANY] * len(after),
        out_specs=(VMEM,) * len(blocks),
        name="image_side",
        cost_estimate=pl.CostEstimate(
            flops=2 * rows * size * len(blocks) * d, bytes_accessed=8 * size * d, transcendentals=0
        ),
        compiler_params=BIG,
    )(*grads, *texts, *after)


def total_four(own, parts):
    return (own + parts[1]) + (parts[0] + parts[2])


def image_add_kernel(own, a, b, c, stats, other, keep, out1, out2, out3, total):
    rows = keep.shape[0]
    v = stats[...] + other[...]
    total[...] = v
    sums = [v[i : i + 1, :1] for i in range(3)]
    for i, out in enumerate((keep, out1, out2, out3)):
        at = pl.ds(i * rows, rows)
        out[pl.ds(0, rows)] = (
            own[at] + a[at].astype(F32) + b[at].astype(F32) + c[at].astype(F32)
        ).astype(out.dtype)
        if i:
            put_stats(sums, out.at[pl.ds(rows, STAT_ROWS)], out.shape[1])


def image_add(own, parts, stats, other):
    rows, d = own.shape[0] // 4, own.shape[1]
    sent = jax.ShapeDtypeStruct((rows + STAT_ROWS, d), BF16)
    return pl.pallas_call(
        image_add_kernel,
        out_shape=(jax.ShapeDtypeStruct((rows, d), F32), sent, sent, sent)
        + (jax.ShapeDtypeStruct(stats.shape, F32),),
        in_specs=[VMEM] * 6,
        out_specs=(VMEM,) * 5,
        name="image_add",
        compiler_params=SMALL,
    )(own, *parts, stats, other)


def text_add_kernel(runs, own, other, stats, came, *refs):
    outs, sums = refs[:-1], refs[-1]
    for (at_own, at_other, rows, _), out in zip(runs, outs):
        out[...] = (
            own[pl.ds(at_own, rows)] + other[pl.ds(at_other, rows)].astype(F32)
        ).astype(out.dtype)
    sums[...] = stats[...] + came[...]


def text_add(own, other, runs, stats, came):
    d = own.shape[1]
    return pl.pallas_call(
        functools.partial(text_add_kernel, runs),
        out_shape=tuple(jax.ShapeDtypeStruct((rows, d), t) for _, _, rows, t in runs)
        + (jax.ShapeDtypeStruct(stats.shape, F32),),
        in_specs=[VMEM] * 4,
        out_specs=(VMEM,) * (len(runs) + 1),
        name="text_add",
        compiler_params=SMALL,
    )(own, other, stats, came)


def step_add_kernel(with_stats, a, b, *refs):
    out = refs[-2] if with_stats else refs[-1]
    came = b.shape[0]
    out[0:came] = (a[0:came] + b[...].astype(F32)).astype(out.dtype)
    if came < a.shape[0]:
        out[came:] = a[came:].astype(out.dtype)
    if with_stats:
        refs[-1][...] = refs[0][...] + refs[1][...]


def step_add(a, b, stats, after, dtype=BF16):
    return pl.pallas_call(
        functools.partial(step_add_kernel, bool(stats)),
        out_shape=(jax.ShapeDtypeStruct(a.shape, dtype),)
        + tuple(jax.ShapeDtypeStruct(s.shape, F32) for s in stats[:1]),
        in_specs=[VMEM] * (2 + len(stats)) + [ANY] * len(after),
        out_specs=(VMEM,) * (1 + len(stats[:1])),
        name="step_add",
        compiler_params=SMALL,
    )(a, b, *stats, *after)


def lower_kernel(a, *refs):
    refs[-1][...] = a[pl.ds(a.shape[0] // 2, a.shape[0] // 2)]


def lower(a, after):
    return pl.pallas_call(
        lower_kernel,
        out_shape=jax.ShapeDtypeStruct((a.shape[0] // 2, a.shape[1]), a.dtype),
        in_specs=[VMEM, ANY],
        out_specs=VMEM,
        name="lower",
        compiler_params=SMALL,
    )(a, after)


def finish_kernel(starts, scale, *refs):
    refs = list(refs)
    outs = refs[-2:]
    for at_list, out in zip(starts, outs):
        raw = refs.pop(0)
        parts = [refs.pop(0) for _ in at_list]
        rows = raw[...].astype(F32)
        inv = inverse_norm(rows)
        unit = rows * inv
        owned = raw.shape[0]
        g = scale[0] * sum(p[pl.ds(at, owned)].astype(F32) for p, at in zip(parts, at_list))
        out[...] = (inv * (g - unit * jnp.sum(unit * g, axis=1, keepdims=True))).astype(BF16)


def finish(scale, *sides):
    starts = [tuple(at for _, at in parts) for _, parts in sides]
    refs = [r for raw, parts in sides for r in [raw] + [p for p, _ in parts]]
    return pl.pallas_call(
        functools.partial(finish_kernel, starts),
        out_shape=tuple(jax.ShapeDtypeStruct(raw.shape, BF16) for raw, _ in sides),
        in_specs=[SMEM] + [VMEM] * len(refs),
        out_specs=(VMEM,) * len(sides),
        name="finish",
        compiler_params=SMALL,
    )(scale, *refs)


def stats_kernel(mine, a, b, c, out):
    tail = pl.ds(a.shape[0] - STAT_ROWS, STAT_ROWS)
    out[...] = total_four(mine[...], [get_stats(p.at[tail])[:, :128] for p in (a, b, c)])


def stats_sum(mine, parts):
    return pl.pallas_call(
        stats_kernel,
        out_shape=jax.ShapeDtypeStruct((3, 128), F32),
        in_specs=[VMEM] * 4,
        out_specs=VMEM,
        name="stats_sum",
        compiler_params=SMALL,
    )(mine, *parts)


def scalars_kernel(batch, scale, a, b, after, out):
    v = (a[...] + b[...]) * (1.0 / batch)
    row = lax.broadcasted_iota(jnp.int32, v.shape, 0)
    out[...] = v * jnp.where(row == 0, 1 / LOG2E, jnp.where(row == 1, scale[0], 1.0))


def scalars(scale, a, b, batch, after):
    return pl.pallas_call(
        functools.partial(scalars_kernel, batch),
        out_shape=jax.ShapeDtypeStruct(a.shape, F32),
        in_specs=[SMEM] + [VMEM] * 2 + [ANY],
        out_specs=VMEM,
        name="scalars",
        compiler_params=SMALL,
    )(scale, a, b, after)


def labels(image_ids, text_ids, x, y, z, c, owned):
    split = (NY, 2, NX, NZ // 2, NC, owned)
    img = image_ids.reshape(split)[:, z % 2, :, z // 2, c].reshape(NY * NX, owned)
    txt = text_ids.reshape(split)[y, :, x].transpose(1, 0, 2, 3).reshape(NZ * NC, owned)
    first, second = jnp.where(c, y, x), jnp.where(c, x, y)
    at = []
    for j in range(4):
        for k in range(4):
            f, s = (first - k) % 4, (second - j) % 4
            at.append(jnp.where(c, f * NX + s, s * NX + f))
    img = img[jnp.stack(at)].reshape(1, -1)
    up = 1 - 2 * c
    sides = ((c, up), (1 - c, -up))
    at = []
    for core, sign in sides:
        order = [(0, core), (1, core), (1, 1 - core)]
        at += [(z - sign * k) % NZ * NC + d for k, d in order]
    for core, sign in sides:
        order = [(k, d) for k in (2, 3) for d in (core, 1 - core)]
        order.insert(4 if core is c else 0, (4, core))
        at += [(z - sign * k) % NZ * NC + d for k, d in order]
    txt = txt[jnp.stack(at)].reshape(-1, 1)
    return img, txt


def shards(images, texts, image_ids, text_ids, temp_log, bias):
    owned = images.shape[0]
    batch_all = owned * NX * NY * NZ * NC
    row, col = lax.axis_index("row"), lax.axis_index("col")
    x, y, z, c = row % NX, row // (2 * NX), 2 * (col // NC) + row // NX % 2, col % NC
    scale = jnp.exp(temp_log)
    coef = jnp.concatenate([scale, bias])
    img_ids, txt_ids = labels(image_ids, text_ids, x, y, z, c, owned)

    xn = normalize(images)
    yn = normalize(texts, [xn])
    sibling = hop_core(yn)
    line = [hop_first(xn, k) for k in (1, 2, 3)]
    near = join([xn] + line)
    ring = [join([yn, sibling], line[:2])]
    ring.append(join([hop_z(ring[0], 1)], [near]))
    for _ in range(3):
        ring.append(hop_z(ring[-1], 1))
    image_blocks = [near] + [hop_second(near, k) for k in (1, 2, 3)]
    early = [yn, ring[1], sibling, hop_core(ring[1])]
    late = [ring[2], ring[3], ring[4], hop_core(ring[2]), hop_core(ring[3])]

    cut = 6 * owned
    zero = jnp.zeros((3, 8, 128), F32)
    g_early, t_early, part, xb = tile(
        coef, img_ids, txt_ids[:cut], zero, image_blocks, early, False
    )
    g_late, t_late, stats = tile(coef, img_ids, txt_ids[cut:], part, [xb], late, True)
    grads, rows = [g_early, g_late], [t_early, t_late]

    send = text_side(grads, xb, True)
    keep = text_side(grads, xb, False, [send])
    runs = (
        (0, 0, owned, F32),
        (owned, owned, 2 * owned, F32),
        (3 * owned, 4 * owned, 2 * owned, F32),
        (5 * owned, 6 * owned, 2 * owned, F32),
        (7 * owned, 3 * owned, owned, BF16),
    )
    gy, gy1, gy2, gy3, far, stats = text_add(
        keep, hop_core(send), runs, stats, exchange(stats, 6, 3)
    )
    sent1, sent3 = image_side(grads, rows, (1, 3), [far])
    (sent2,) = image_side(grads, rows, (2,), [sent1])
    parts = [hop_second(g, -k) for k, g in zip((1, 2, 3), (sent1, sent2, sent3))]
    step, stats = step_add(gy3, hop_z(far, -1), [stats, exchange(stats, 7, 4)], [sent2])
    (own,) = image_side(grads, rows, (0,), [step])
    step, stats = step_add(gy2, hop_z(step, -1), [stats, exchange(stats, 5, 5)], [own], F32)
    stats = stats + exchange(stats, 1, 1)
    keep, g1, g2, g3, stats = image_add(own, parts, stats, exchange(stats, 2, 2))
    (step,) = step_add(gy1, hop_z(step, -1), [], [keep])
    around = hop_z(step, -1)
    parts = [hop_first(g, -k) for k, g in ((1, g1), (2, g2), (3, g3))]
    text_parts = [(gy, 0), (around, 0), (hop_core(lower(around, parts[2])), 0)]

    stats = stats_sum(stats, parts)
    image_grad, text_grad = finish(
        scale, (images, [(p, 0) for p in [keep] + parts]), (texts, text_parts)
    )
    total = scalars(scale, stats, exchange(stats, 0, 0), batch_all, image_grad)
    return image_grad, text_grad, total[:, 0]


def solution(mesh):
    spread = P(("row", "col"), None)
    return jax.shard_map(
        shards,
        mesh=mesh,
        in_specs=(spread, spread, P(), P(), P(), P()),
        out_specs=(spread, spread, P()),
        check_vma=False,
    )
```

```python
import functools
import itertools
import jax
import jax.numpy as jnp
from jax import lax
from jax.experimental import pallas as pl
from jax.experimental.pallas import tpu as pltpu
from jax.sharding import PartitionSpec as P

NX, NY, NZ, NC = 4, 4, 8, 2
LOG2E = 1.4426950408889634
F32, BF16 = jnp.float32, jnp.bfloat16
ANY = pl.BlockSpec(memory_space=pl.ANY)
STAT_ROWS = 16
VMEM = pl.BlockSpec(memory_space=pltpu.VMEM)
SMEM = pl.BlockSpec(memory_space=pltpu.SMEM)
BIG = pltpu.CompilerParams(vmem_limit_bytes=24 * 2**20)
SMALL = pltpu.CompilerParams(vmem_limit_bytes=12 * 2**20)


def linear(x, y, z, c):
    return (((y * 2 + z % 2) * NX + x) * (NZ // 2) + z // 2) * NC + c


def hop(a, move):
    pairs = []
    for x, y, z, c in itertools.product(range(NX), range(NY), range(NZ), range(NC)):
        dx, dy, dz, dc = move(c)
        to = linear((x + dx) % NX, (y + dy) % NY, (z + dz) % NZ, (c + dc) % NC)
        pairs.append((linear(x, y, z, c), to))
    return lax.ppermute(a, ("row", "col"), pairs)


def hop_first(a, k):
    return hop(a, lambda c: (0, k, 0, 0) if c else (k, 0, 0, 0))


def hop_second(a, k):
    return hop(a, lambda c: (k, 0, 0, 0) if c else (0, k, 0, 0))


def hop_z(a, k):
    return hop(a, lambda c: (0, 0, -k if c else k, 0))


def hop_core(a):
    return hop(a, lambda c: (0, 0, 0, 1))


def exchange(a, bit0, bit1):
    pairs = [(i, i ^ (1 << (bit1 if i % 2 else bit0))) for i in range(256)]
    return lax.ppermute(a, ("row", "col"), pairs)


def dot_t(a, b):
    return lax.dot_general(a, b, (((1,), (1,)), ((), ())), preferred_element_type=F32)


def dot_a(a, b):
    return lax.dot_general(a, b, (((0,), (0,)), ((), ())), preferred_element_type=F32)


def inverse_norm(rows):
    return lax.rsqrt(jnp.sum(rows * rows, axis=1, keepdims=True) + 1e-06)


def norm_kernel(raw, *refs):
    rows = raw[...].astype(F32)
    refs[-1][...] = (rows * inverse_norm(rows)).astype(BF16)


def normalize(raw, after=()):
    return pl.pallas_call(
        norm_kernel,
        out_shape=jax.ShapeDtypeStruct(raw.shape, BF16),
        in_specs=[VMEM] + [ANY] * len(after),
        out_specs=VMEM,
        name="normalize",
        compiler_params=SMALL,
    )(raw, *after)


def join_kernel(n, *refs):
    out, at = refs[-1], 0
    for part in refs[:n]:
        rows = part.shape[0]
        out[at : at + rows] = part[...]
        at += rows


def join(parts, after=()):
    rows = sum(p.shape[0] for p in parts)
    return pl.pallas_call(
        functools.partial(join_kernel, len(parts)),
        out_shape=jax.ShapeDtypeStruct((rows, parts[0].shape[1]), parts[0].dtype),
        in_specs=[VMEM] * len(parts) + [ANY] * len(after),
        out_specs=VMEM,
        name="join",
        compiler_params=SMALL,
    )(*parts, *after)


def load(refs, dst, sem, first):
    out, at = [], 0
    for ref in refs:
        rows = ref.shape[0]
        copy = pltpu.make_async_copy(ref, dst.at[pl.ds(at, rows)], sem.at[first + len(out)])
        copy.start()
        out.append((at, copy))
        at += rows
    return out


def fold(v):
    u = jnp.sum(v.reshape(v.shape[0] // 8, 8, v.shape[1]), axis=0)
    return sum(u[:, k : k + 128] for k in range(0, u.shape[1], 128))


def put_stats(sums, rows, width):
    row = lax.broadcasted_iota(jnp.int32, (STAT_ROWS, width), 0)
    v = jnp.where(row % 3 == 0, sums[0], jnp.where(row % 3 == 1, sums[1], sums[2]))
    high = v.astype(BF16).astype(F32)
    mid = (v - high).astype(BF16).astype(F32)
    low = v - high - mid
    v = jnp.where(row < 3, high, jnp.where(row < 6, mid, low))
    rows[...] = jnp.where(row < 9, v, 0.0).astype(BF16)


def get_stats(rows):
    v = rows[...].astype(F32)
    return (v[0:3] + v[3:6]) + v[6:9]


def tile_kernel(nx, nt, last, *refs):
    coef, image_ids, text_ids, before = refs[:4]
    images, texts = refs[4 : 4 + nx], refs[4 + nx : 4 + nx + nt]
    grad, yb, stats = refs[4 + nx + nt : 7 + nx + nt]
    prods, sem = refs[-2:]
    coming = load(texts, yb, sem, 0)
    if nx > 1:
        xb = refs[-3]
        coming_x = load(images, xb, sem, nt)
    else:
        xb, coming_x = images[0], []
    for _, copy in coming:
        copy.wait()
    rows, cols = yb.shape[0], xb.shape[0]
    wide = 256
    steps = cols // wide
    scale, shift = coef[0] * LOG2E, coef[1] * LOG2E
    acc = [before[i] for i in range(3)]

    def multiply(k):
        while coming_x and coming_x[0][0] < (k + 1) * wide:
            coming_x.pop(0)[1].wait()
        prods[k % 2] = dot_t(yb[...], xb[k * wide : (k + 1) * wide])

    multiply(0)
    for k in range(steps):
        if k + 1 < steps:
            multiply(k + 1)
        dots = prods[k % 2]
        match = text_ids[:, :1] == image_ids[:1, k * wide : (k + 1) * wide]
        logits = dots * scale + shift
        e = jnp.exp2(jnp.where(match, -logits, logits))
        p = 1.0 + e
        s = e / p
        g = jnp.where(match, -s, s)
        grad[:, k * wide : (k + 1) * wide] = g.astype(BF16)
        acc[0] += fold(jnp.log2(p[: rows // 2] * p[rows // 2 :]))
        acc[1] += fold(g * dots)
        acc[2] += fold(g)
    for i in range(3):
        if last:
            stats[pl.ds(i, 1)] = jnp.full((1, 128), jnp.sum(acc[i]))
        else:
            stats[i] = acc[i]


def tile(coef, image_ids, text_ids, before, images, texts, last):
    cols, rows = image_ids.shape[1], text_ids.shape[0]
    d = images[0].shape[1]
    nx, nt = len(images), len(texts)
    out_shape = (
        jax.ShapeDtypeStruct((rows, cols), BF16),
        jax.ShapeDtypeStruct((rows, d), BF16),
        jax.ShapeDtypeStruct((3, 128) if last else (3, 8, 128), F32),
    )
    if nx > 1:
        out_shape += (jax.ShapeDtypeStruct((cols, d), BF16),)
    return pl.pallas_call(
        functools.partial(tile_kernel, nx, nt, last),
        out_shape=out_shape,
        in_specs=[SMEM, VMEM, VMEM, VMEM] + [ANY if nx > 1 else VMEM] * nx + [ANY] * nt,
        out_specs=(VMEM,) * len(out_shape),
        scratch_shapes=[
            pltpu.VMEM((2, rows, 256), F32),
            pltpu.SemaphoreType.DMA((nx + nt,)),
        ],
        name="tile_late" if last else "tile_early",
        cost_estimate=pl.CostEstimate(
            flops=2 * rows * cols * d, bytes_accessed=4 * cols * d, transcendentals=3 * rows * cols
        ),
        compiler_params=BIG,
    )(coef, image_ids, text_ids, before, *images, *texts)


def text_side_kernel(lower, ge, gl, xb, *refs):
    out, at = refs[-1], 0
    for g in (ge, gl):
        half = g.shape[0] // 2
        first = half if lower else 0
        out[at : at + half] = jnp.dot(
            g[first : first + half], xb[...], preferred_element_type=F32
        )
        at += half


def text_side(grads, xb, lower, after=()):
    rows = sum(g.shape[0] for g in grads) // 2
    d = xb.shape[1]
    return pl.pallas_call(
        functools.partial(text_side_kernel, lower),
        out_shape=jax.ShapeDtypeStruct((rows, d), F32),
        in_specs=[VMEM] * 3 + [ANY] * len(after),
        out_specs=VMEM,
        name="text_side",
        compiler_params=BIG,
    )(*grads, xb, *after)


def image_side_kernel(blocks, ge, gl, ye, yl, *refs):
    outs = refs[len(refs) - len(blocks) :]
    if 0 not in blocks:
        outs, sums = refs[len(refs) - len(blocks) - 1 : -1], refs[-1]
        sums[...] = refs[0][...] + refs[1][...]
    rows = outs[0].shape[0]
    for i, out in zip(blocks, outs):
        at = slice(i * rows, (i + 1) * rows)
        out[...] = (dot_a(ge[:, at], ye[...]) + dot_a(gl[:, at], yl[...])).astype(out.dtype)


def image_side(grads, texts, blocks, stats=(), after=()):
    d, cols = texts[0].shape[1], grads[0].shape[1]
    size = cols // 4
    return pl.pallas_call(
        functools.partial(image_side_kernel, blocks),
        out_shape=tuple(jax.ShapeDtypeStruct((size, d), BF16 if i else F32) for i in blocks)
        + tuple(jax.ShapeDtypeStruct(s.shape, F32) for s in stats[:1]),
        in_specs=[VMEM] * (4 + len(stats)) + [ANY] * len(after),
        out_specs=(VMEM,) * (len(blocks) + len(stats[:1])),
        name="image_side",
        compiler_params=BIG,
    )(*grads, *texts, *stats, *after)


def total_four(own, parts):
    return (own + parts[1]) + (parts[0] + parts[2])


def image_add_kernel(own, a, b, c, stats, other, keep, out1, out2, out3, total):
    rows = keep.shape[0]
    v = stats[...] + other[...]
    total[...] = v
    sums = [v[i : i + 1, :1] for i in range(3)]
    for i, out in enumerate((keep, out1, out2, out3)):
        at = pl.ds(i * rows, rows)
        out[pl.ds(0, rows)] = (
            own[at] + a[at].astype(F32) + b[at].astype(F32) + c[at].astype(F32)
        ).astype(out.dtype)
        if i:
            put_stats(sums, out.at[pl.ds(rows, STAT_ROWS)], out.shape[1])


def image_add(own, parts, stats, other):
    rows, d = own.shape[0] // 4, own.shape[1]
    sent = jax.ShapeDtypeStruct((rows + STAT_ROWS, d), BF16)
    return pl.pallas_call(
        image_add_kernel,
        out_shape=(jax.ShapeDtypeStruct((rows, d), F32), sent, sent, sent)
        + (jax.ShapeDtypeStruct(stats.shape, F32),),
        in_specs=[VMEM] * 6,
        out_specs=(VMEM,) * 5,
        name="image_add",
        compiler_params=SMALL,
    )(own, *parts, stats, other)


def text_add_kernel(runs, own, other, *refs):
    outs = refs[len(refs) - len(runs) :]
    for (at_own, at_other, rows, _), out in zip(runs, outs):
        out[...] = (own[pl.ds(at_own, rows)] + other[pl.ds(at_other, rows)]).astype(out.dtype)


def text_add(own, other, runs, after):
    d = own.shape[1]
    return pl.pallas_call(
        functools.partial(text_add_kernel, runs),
        out_shape=tuple(jax.ShapeDtypeStruct((rows, d), t) for _, _, rows, t in runs),
        in_specs=[VMEM] * 2 + [ANY] * len(after),
        out_specs=(VMEM,) * len(runs),
        name="text_add",
        compiler_params=SMALL,
    )(own, other, *after)


def step_add_kernel(with_stats, a, b, *refs):
    out = refs[-2] if with_stats else refs[-1]
    came = b.shape[0]
    out[0:came] = (a[0:came] + b[...].astype(F32)).astype(out.dtype)
    if came < a.shape[0]:
        out[came:] = a[came:].astype(out.dtype)
    if with_stats:
        refs[-1][...] = refs[0][...] + refs[1][...]


def step_add(a, b, stats, after, dtype=BF16):
    return pl.pallas_call(
        functools.partial(step_add_kernel, bool(stats)),
        out_shape=(jax.ShapeDtypeStruct(a.shape, dtype),)
        + tuple(jax.ShapeDtypeStruct(s.shape, F32) for s in stats[:1]),
        in_specs=[VMEM] * (2 + len(stats)) + [ANY] * len(after),
        out_specs=(VMEM,) * (1 + len(stats[:1])),
        name="step_add",
        compiler_params=SMALL,
    )(a, b, *stats, *after)


def lower_kernel(a, *refs):
    refs[-1][...] = a[pl.ds(a.shape[0] // 2, a.shape[0] // 2)]


def lower(a, after):
    return pl.pallas_call(
        lower_kernel,
        out_shape=jax.ShapeDtypeStruct((a.shape[0] // 2, a.shape[1]), a.dtype),
        in_specs=[VMEM, ANY],
        out_specs=VMEM,
        name="lower",
        compiler_params=SMALL,
    )(a, after)


def finish_kernel(starts, scale, *refs):
    refs = list(refs)
    outs = refs[-2:]
    for at_list, out in zip(starts, outs):
        raw = refs.pop(0)
        parts = [refs.pop(0) for _ in at_list]
        rows = raw[...].astype(F32)
        inv = inverse_norm(rows)
        unit = rows * inv
        owned = raw.shape[0]
        g = scale[0] * sum(p[pl.ds(at, owned)].astype(F32) for p, at in zip(parts, at_list))
        out[...] = (inv * (g - unit * jnp.sum(unit * g, axis=1, keepdims=True))).astype(BF16)


def finish(scale, *sides):
    starts = [tuple(at for _, at in parts) for _, parts in sides]
    refs = [r for raw, parts in sides for r in [raw] + [p for p, _ in parts]]
    return pl.pallas_call(
        functools.partial(finish_kernel, starts),
        out_shape=tuple(jax.ShapeDtypeStruct(raw.shape, BF16) for raw, _ in sides),
        in_specs=[SMEM] + [VMEM] * len(refs),
        out_specs=(VMEM,) * len(sides),
        name="finish",
        compiler_params=SMALL,
    )(scale, *refs)


def stats_kernel(mine, a, b, c, out):
    tail = pl.ds(a.shape[0] - STAT_ROWS, STAT_ROWS)
    out[...] = total_four(mine[...], [get_stats(p.at[tail])[:, :128] for p in (a, b, c)])


def stats_sum(mine, parts):
    return pl.pallas_call(
        stats_kernel,
        out_shape=jax.ShapeDtypeStruct((3, 128), F32),
        in_specs=[VMEM] * 4,
        out_specs=VMEM,
        name="stats_sum",
        compiler_params=SMALL,
    )(mine, *parts)


def scalars_kernel(batch, scale, a, b, after, out):
    v = (a[...] + b[...]) * (1.0 / batch)
    row = lax.broadcasted_iota(jnp.int32, v.shape, 0)
    out[...] = v * jnp.where(row == 0, 1 / LOG2E, jnp.where(row == 1, scale[0], 1.0))


def scalars(scale, a, b, batch, after):
    return pl.pallas_call(
        functools.partial(scalars_kernel, batch),
        out_shape=jax.ShapeDtypeStruct(a.shape, F32),
        in_specs=[SMEM] + [VMEM] * 2 + [ANY],
        out_specs=VMEM,
        name="scalars",
        compiler_params=SMALL,
    )(scale, a, b, after)


def labels(image_ids, text_ids, x, y, z, c, owned):
    split = (NY, 2, NX, NZ // 2, NC, owned)
    img = image_ids.reshape(split)[:, z % 2, :, z // 2, c].reshape(NY * NX, owned)
    txt = text_ids.reshape(split)[y, :, x].transpose(1, 0, 2, 3).reshape(NZ * NC, owned)
    first, second = jnp.where(c, y, x), jnp.where(c, x, y)
    at = []
    for j in range(4):
        for k in range(4):
            f, s = (first - k) % 4, (second - j) % 4
            at.append(jnp.where(c, f * NX + s, s * NX + f))
    img = img[jnp.stack(at)].reshape(1, -1)
    up = 1 - 2 * c
    sides = ((c, up), (1 - c, -up))
    at = []
    for core, sign in sides:
        order = [(0, core), (1, core), (1, 1 - core)]
        at += [(z - sign * k) % NZ * NC + d for k, d in order]
    for core, sign in sides:
        order = [(k, d) for k in (2, 3) for d in (core, 1 - core)]
        order.insert(4 if core is c else 0, (4, core))
        at += [(z - sign * k) % NZ * NC + d for k, d in order]
    txt = txt[jnp.stack(at)].reshape(-1, 1)
    return img, txt


def shards(images, texts, image_ids, text_ids, temp_log, bias):
    owned = images.shape[0]
    batch_all = owned * NX * NY * NZ * NC
    row, col = lax.axis_index("row"), lax.axis_index("col")
    x, y, z, c = row % NX, row // (2 * NX), 2 * (col // NC) + row // NX % 2, col % NC
    scale = jnp.exp(temp_log)
    coef = jnp.concatenate([scale, bias])
    img_ids, txt_ids = labels(image_ids, text_ids, x, y, z, c, owned)

    xn = normalize(images)
    yn = normalize(texts, [xn])
    sibling = hop_core(yn)
    line = [hop_first(xn, k) for k in (1, 2, 3)]
    near = join([xn] + line)
    ring = [join([yn, sibling])]
    ring.append(join([hop_z(ring[0], 1)], [near]))
    for _ in range(3):
        ring.append(hop_z(ring[-1], 1))
    image_blocks = [near] + [hop_second(near, k) for k in (1, 2, 3)]
    early = [yn, ring[1], sibling, hop_core(ring[1])]
    late = [ring[2], ring[3], ring[4], hop_core(ring[2]), hop_core(ring[3])]

    cut = 6 * owned
    zero = jnp.zeros((3, 8, 128), F32)
    g_early, t_early, part, xb = tile(
        coef, img_ids, txt_ids[:cut], zero, image_blocks, early, False
    )
    g_late, t_late, stats = tile(coef, img_ids, txt_ids[cut:], part, [xb], late, True)
    grads, rows = [g_early, g_late], [t_early, t_late]

    send = text_side(grads, xb, True)
    keep = text_side(grads, xb, False, [send])
    *sent, stats = image_side(
        grads, rows, (1, 2, 3), [stats, exchange(stats, 6, 3)], [keep]
    )
    runs = (
        (0, 0, owned, F32),
        (owned, owned, 2 * owned, F32),
        (3 * owned, 4 * owned, 2 * owned, F32),
        (5 * owned, 6 * owned, 2 * owned, F32),
        (7 * owned, 3 * owned, owned, BF16),
    )
    gy, gy1, gy2, gy3, far = text_add(keep, hop_core(send), runs, [sent[0]])
    parts = [hop_second(g, -k) for k, g in zip((1, 2, 3), sent)]
    (own,) = image_side(grads, rows, (0,), (), [far])
    step, stats = step_add(gy3, hop_z(far, -1), [stats, exchange(stats, 7, 4)], [own])
    step, stats = step_add(gy2, hop_z(step, -1), [stats, exchange(stats, 5, 5)], [])
    stats = stats + exchange(stats, 1, 1)
    keep, g1, g2, g3, stats = image_add(own, parts, stats, exchange(stats, 2, 2))
    (step,) = step_add(gy1, hop_z(step, -1), [], [keep])
    around = hop_z(step, -1)
    parts = [hop_first(g, -k) for k, g in ((1, g1), (2, g2), (3, g3))]
    text_parts = [(gy, 0), (around, 0), (hop_core(lower(around, parts[2])), 0)]

    stats = stats_sum(stats, parts)
    image_grad, text_grad = finish(
        scale, (images, [(p, 0) for p in [keep] + parts]), (texts, text_parts)
    )
    total = scalars(scale, stats, exchange(stats, 0, 0), batch_all, image_grad)
    return image_grad, text_grad, total[:, 0]


def solution(mesh):
    spread = P(("row", "col"), None)
    return jax.shard_map(
        shards,
        mesh=mesh,
        in_specs=(spread, spread, P(), P(), P(), P()),
        out_specs=(spread, spread, P()),
        check_vma=False,
    )
```

```python
import functools
import itertools
import jax
import jax.numpy as jnp
from jax import lax
from jax.experimental import pallas as pl
from jax.experimental.pallas import tpu as pltpu
from jax.sharding import PartitionSpec as P

NX, NY, NZ, NC = 4, 4, 8, 2
LOG2E = 1.4426950408889634
F32, BF16 = jnp.float32, jnp.bfloat16
ANY = pl.BlockSpec(memory_space=pl.ANY)
STAT_ROWS = 16
VMEM = pl.BlockSpec(memory_space=pltpu.VMEM)
SMEM = pl.BlockSpec(memory_space=pltpu.SMEM)
BIG = pltpu.CompilerParams(vmem_limit_bytes=24 * 2**20)
SMALL = pltpu.CompilerParams(vmem_limit_bytes=12 * 2**20)


def linear(x, y, z, c):
    return (((y * 2 + z % 2) * NX + x) * (NZ // 2) + z // 2) * NC + c


def hop(a, move):
    pairs = []
    for x, y, z, c in itertools.product(range(NX), range(NY), range(NZ), range(NC)):
        dx, dy, dz, dc = move(c)
        to = linear((x + dx) % NX, (y + dy) % NY, (z + dz) % NZ, (c + dc) % NC)
        pairs.append((linear(x, y, z, c), to))
    return lax.ppermute(a, ("row", "col"), pairs)


def hop_first(a, k):
    return hop(a, lambda c: (0, k, 0, 0) if c else (k, 0, 0, 0))


def hop_second(a, k):
    return hop(a, lambda c: (k, 0, 0, 0) if c else (0, k, 0, 0))


def hop_z(a, k):
    return hop(a, lambda c: (0, 0, -k if c else k, 0))


def hop_core(a):
    return hop(a, lambda c: (0, 0, 0, 1))


def exchange(a, bit0, bit1):
    pairs = [(i, i ^ (1 << (bit1 if i % 2 else bit0))) for i in range(256)]
    return lax.ppermute(a, ("row", "col"), pairs)


def dot_t(a, b):
    return lax.dot_general(a, b, (((1,), (1,)), ((), ())), preferred_element_type=F32)


def dot_a(a, b):
    return lax.dot_general(a, b, (((0,), (0,)), ((), ())), preferred_element_type=F32)


def inverse_norm(rows):
    return lax.rsqrt(jnp.sum(rows * rows, axis=1, keepdims=True) + 1e-06)


def norm_kernel(raw, *refs):
    rows = raw[...].astype(F32)
    refs[-1][...] = (rows * inverse_norm(rows)).astype(BF16)


def normalize(raw, after=()):
    return pl.pallas_call(
        norm_kernel,
        out_shape=jax.ShapeDtypeStruct(raw.shape, BF16),
        in_specs=[VMEM] + [ANY] * len(after),
        out_specs=VMEM,
        name="normalize",
        compiler_params=SMALL,
    )(raw, *after)


def join_kernel(n, *refs):
    out, at = refs[-1], 0
    for part in refs[:n]:
        rows = part.shape[0]
        out[at : at + rows] = part[...]
        at += rows


def join(parts, after=()):
    rows = sum(p.shape[0] for p in parts)
    return pl.pallas_call(
        functools.partial(join_kernel, len(parts)),
        out_shape=jax.ShapeDtypeStruct((rows, parts[0].shape[1]), parts[0].dtype),
        in_specs=[VMEM] * len(parts) + [ANY] * len(after),
        out_specs=VMEM,
        name="join",
        compiler_params=SMALL,
    )(*parts, *after)


def load(refs, dst, sem, first):
    out, at = [], 0
    for ref in refs:
        rows = ref.shape[0]
        copy = pltpu.make_async_copy(ref, dst.at[pl.ds(at, rows)], sem.at[first + len(out)])
        copy.start()
        out.append((at, copy))
        at += rows
    return out


def fold(v):
    u = jnp.sum(v.reshape(v.shape[0] // 8, 8, v.shape[1]), axis=0)
    return sum(u[:, k : k + 128] for k in range(0, u.shape[1], 128))


def put_stats(sums, rows, width):
    row = lax.broadcasted_iota(jnp.int32, (STAT_ROWS, width), 0)
    v = jnp.where(row % 3 == 0, sums[0], jnp.where(row % 3 == 1, sums[1], sums[2]))
    high = v.astype(BF16).astype(F32)
    mid = (v - high).astype(BF16).astype(F32)
    low = v - high - mid
    v = jnp.where(row < 3, high, jnp.where(row < 6, mid, low))
    rows[...] = jnp.where(row < 9, v, 0.0).astype(BF16)


def get_stats(rows):
    v = rows[...].astype(F32)
    return (v[0:3] + v[3:6]) + v[6:9]


def tile_kernel(nx, nt, last, *refs):
    coef, image_ids, text_ids, before = refs[:4]
    images, texts = refs[4 : 4 + nx], refs[4 + nx : 4 + nx + nt]
    grad, yb, stats = refs[4 + nx + nt : 7 + nx + nt]
    prods, sem = refs[-2:]
    coming = load(texts, yb, sem, 0)
    if nx > 1:
        xb = refs[-3]
        coming_x = load(images, xb, sem, nt)
    else:
        xb, coming_x = images[0], []
    for _, copy in coming:
        copy.wait()
    rows, cols = yb.shape[0], xb.shape[0]
    wide = 256
    steps = cols // wide
    scale, shift = coef[0] * LOG2E, coef[1] * LOG2E
    acc = [before[i] for i in range(3)]

    def multiply(k):
        while coming_x and coming_x[0][0] < (k + 1) * wide:
            coming_x.pop(0)[1].wait()
        prods[k % 2] = dot_t(yb[...], xb[k * wide : (k + 1) * wide])

    multiply(0)
    for k in range(steps):
        if k + 1 < steps:
            multiply(k + 1)
        dots = prods[k % 2]
        match = text_ids[:, :1] == image_ids[:1, k * wide : (k + 1) * wide]
        logits = dots * scale + shift
        e = jnp.exp2(jnp.where(match, -logits, logits))
        p = 1.0 + e
        s = e / p
        g = jnp.where(match, -s, s)
        grad[:, k * wide : (k + 1) * wide] = g.astype(BF16)
        acc[0] += fold(jnp.log2(p[: rows // 2] * p[rows // 2 :]))
        acc[1] += fold(g * dots)
        acc[2] += fold(g)
    for i in range(3):
        if last:
            stats[pl.ds(i, 1)] = jnp.full((1, 128), jnp.sum(acc[i]))
        else:
            stats[i] = acc[i]


def tile(coef, image_ids, text_ids, before, images, texts, last):
    cols, rows = image_ids.shape[1], text_ids.shape[0]
    d = images[0].shape[1]
    nx, nt = len(images), len(texts)
    out_shape = (
        jax.ShapeDtypeStruct((rows, cols), BF16),
        jax.ShapeDtypeStruct((rows, d), BF16),
        jax.ShapeDtypeStruct((3, 128) if last else (3, 8, 128), F32),
    )
    if nx > 1:
        out_shape += (jax.ShapeDtypeStruct((cols, d), BF16),)
    return pl.pallas_call(
        functools.partial(tile_kernel, nx, nt, last),
        out_shape=out_shape,
        in_specs=[SMEM, VMEM, VMEM, VMEM] + [ANY if nx > 1 else VMEM] * nx + [ANY] * nt,
        out_specs=(VMEM,) * len(out_shape),
        scratch_shapes=[
            pltpu.VMEM((2, rows, 256), F32),
            pltpu.SemaphoreType.DMA((nx + nt,)),
        ],
        name="tile_late" if last else "tile_early",
        cost_estimate=pl.CostEstimate(
            flops=2 * rows * cols * d, bytes_accessed=4 * cols * d, transcendentals=3 * rows * cols
        ),
        compiler_params=BIG,
    )(coef, image_ids, text_ids, before, *images, *texts)


def text_side_kernel(lower, ge, gl, xb, *refs):
    out, at = refs[-1], 0
    for g in (ge, gl):
        half = g.shape[0] // 2
        first = half if lower else 0
        out[at : at + half] = jnp.dot(
            g[first : first + half], xb[...], preferred_element_type=F32
        )
        at += half


def text_side(grads, xb, lower, after=()):
    rows = sum(g.shape[0] for g in grads) // 2
    d = xb.shape[1]
    return pl.pallas_call(
        functools.partial(text_side_kernel, lower),
        out_shape=jax.ShapeDtypeStruct((rows, d), F32),
        in_specs=[VMEM] * 3 + [ANY] * len(after),
        out_specs=VMEM,
        name="text_side",
        compiler_params=BIG,
    )(*grads, xb, *after)


def image_side_kernel(blocks, with_stats, ge, gl, ye, yl, *refs):
    outs = refs[len(refs) - len(blocks) :]
    if with_stats:
        outs, sums = refs[len(refs) - len(blocks) - 1 : -1], refs[-1]
        sums[...] = refs[0][...] + refs[1][...]
    rows = outs[0].shape[0]
    for i, out in zip(blocks, outs):
        at = slice(i * rows, (i + 1) * rows)
        out[...] = (dot_a(ge[:, at], ye[...]) + dot_a(gl[:, at], yl[...])).astype(out.dtype)


def image_side(grads, texts, blocks, stats=(), after=()):
    d, cols = texts[0].shape[1], grads[0].shape[1]
    size = cols // 4
    return pl.pallas_call(
        functools.partial(image_side_kernel, blocks, bool(stats)),
        out_shape=tuple(jax.ShapeDtypeStruct((size, d), BF16 if i else F32) for i in blocks)
        + tuple(jax.ShapeDtypeStruct(s.shape, F32) for s in stats[:1]),
        in_specs=[VMEM] * (4 + len(stats)) + [ANY] * len(after),
        out_specs=(VMEM,) * (len(blocks) + len(stats[:1])),
        name="image_side",
        compiler_params=BIG,
    )(*grads, *texts, *stats, *after)


def total_four(own, parts):
    return (own + parts[1]) + (parts[0] + parts[2])


def image_add_kernel(own, a, b, c, stats, other, keep, out1, out2, out3, total):
    rows = keep.shape[0]
    v = stats[...] + other[...]
    total[...] = v
    sums = [v[i : i + 1, :1] for i in range(3)]
    for i, out in enumerate((keep, out1, out2, out3)):
        at = pl.ds(i * rows, rows)
        out[pl.ds(0, rows)] = (
            own[at] + a[at].astype(F32) + b[at].astype(F32) + c[at].astype(F32)
        ).astype(out.dtype)
        if i:
            put_stats(sums, out.at[pl.ds(rows, STAT_ROWS)], out.shape[1])


def image_add(own, parts, stats, other):
    rows, d = own.shape[0] // 4, own.shape[1]
    sent = jax.ShapeDtypeStruct((rows + STAT_ROWS, d), BF16)
    return pl.pallas_call(
        image_add_kernel,
        out_shape=(jax.ShapeDtypeStruct((rows, d), F32), sent, sent, sent)
        + (jax.ShapeDtypeStruct(stats.shape, F32),),
        in_specs=[VMEM] * 6,
        out_specs=(VMEM,) * 5,
        name="image_add",
        compiler_params=SMALL,
    )(own, *parts, stats, other)


def text_add_kernel(runs, own, other, stats, came, *refs):
    outs, sums = refs[len(refs) - len(runs) - 1 : -1], refs[-1]
    for (at_own, at_other, rows, _), out in zip(runs, outs):
        out[...] = (own[pl.ds(at_own, rows)] + other[pl.ds(at_other, rows)]).astype(out.dtype)
    sums[...] = stats[...] + came[...]


def text_add(own, other, runs, stats, came, after):
    d = own.shape[1]
    return pl.pallas_call(
        functools.partial(text_add_kernel, runs),
        out_shape=tuple(jax.ShapeDtypeStruct((rows, d), t) for _, _, rows, t in runs)
        + (jax.ShapeDtypeStruct(stats.shape, F32),),
        in_specs=[VMEM] * 4 + [ANY] * len(after),
        out_specs=(VMEM,) * (len(runs) + 1),
        name="text_add",
        compiler_params=SMALL,
    )(own, other, stats, came, *after)


def step_add_kernel(with_stats, a, b, *refs):
    out = refs[-2] if with_stats else refs[-1]
    came = b.shape[0]
    out[0:came] = (a[0:came] + b[...].astype(F32)).astype(out.dtype)
    if came < a.shape[0]:
        out[came:] = a[came:].astype(out.dtype)
    if with_stats:
        refs[-1][...] = refs[0][...] + refs[1][...]


def step_add(a, b, stats, after, dtype=BF16):
    return pl.pallas_call(
        functools.partial(step_add_kernel, bool(stats)),
        out_shape=(jax.ShapeDtypeStruct(a.shape, dtype),)
        + tuple(jax.ShapeDtypeStruct(s.shape, F32) for s in stats[:1]),
        in_specs=[VMEM] * (2 + len(stats)) + [ANY] * len(after),
        out_specs=(VMEM,) * (1 + len(stats[:1])),
        name="step_add",
        compiler_params=SMALL,
    )(a, b, *stats, *after)


def lower_kernel(a, *refs):
    refs[-1][...] = a[pl.ds(a.shape[0] // 2, a.shape[0] // 2)]


def lower(a, after):
    return pl.pallas_call(
        lower_kernel,
        out_shape=jax.ShapeDtypeStruct((a.shape[0] // 2, a.shape[1]), a.dtype),
        in_specs=[VMEM, ANY],
        out_specs=VMEM,
        name="lower",
        compiler_params=SMALL,
    )(a, after)


def finish_kernel(starts, scale, *refs):
    refs = list(refs)
    outs, mark = refs[-3:-1], refs[-1]
    mark[...] = jnp.zeros(mark.shape, F32)
    for at_list, out in zip(starts, outs):
        raw = refs.pop(0)
        parts = [refs.pop(0) for _ in at_list]
        rows = raw[...].astype(F32)
        inv = inverse_norm(rows)
        unit = rows * inv
        owned = raw.shape[0]
        g = scale[0] * sum(p[pl.ds(at, owned)].astype(F32) for p, at in zip(parts, at_list))
        out[...] = (inv * (g - unit * jnp.sum(unit * g, axis=1, keepdims=True))).astype(BF16)


def finish(scale, *sides):
    starts = [tuple(at for _, at in parts) for _, parts in sides]
    refs = [r for raw, parts in sides for r in [raw] + [p for p, _ in parts]]
    return pl.pallas_call(
        functools.partial(finish_kernel, starts),
        out_shape=tuple(jax.ShapeDtypeStruct(raw.shape, BF16) for raw, _ in sides)
        + (jax.ShapeDtypeStruct((8, 128), F32),),
        in_specs=[SMEM] + [VMEM] * len(refs),
        out_specs=(VMEM,) * (len(sides) + 1),
        name="finish",
        compiler_params=SMALL,
    )(scale, *refs)


def stats_kernel(mine, a, b, c, out):
    tail = pl.ds(a.shape[0] - STAT_ROWS, STAT_ROWS)
    out[...] = total_four(mine[...], [get_stats(p.at[tail])[:, :128] for p in (a, b, c)])


def stats_sum(mine, parts):
    return pl.pallas_call(
        stats_kernel,
        out_shape=jax.ShapeDtypeStruct((3, 128), F32),
        in_specs=[VMEM] * 4,
        out_specs=VMEM,
        name="stats_sum",
        compiler_params=SMALL,
    )(mine, *parts)


def scalars_kernel(batch, scale, a, b, after, out):
    v = (a[...] + b[...]) * (1.0 / batch)
    for i, factor in enumerate((1 / LOG2E, scale[0], 1.0)):
        out[i] = jnp.max(v[i : i + 1]) * factor


def scalars(scale, a, b, batch, after):
    return pl.pallas_call(
        functools.partial(scalars_kernel, batch),
        out_shape=jax.ShapeDtypeStruct((3,), F32),
        in_specs=[SMEM] + [VMEM] * 2 + [ANY],
        out_specs=SMEM,
        name="scalars",
        compiler_params=SMALL,
    )(scale, a, b, after)


def labels(image_ids, text_ids, x, y, z, c, owned):
    split = (NY, 2, NX, NZ // 2, NC, owned)
    img = image_ids.reshape(split)[:, z % 2, :, z // 2, c].reshape(NY * NX, owned)
    txt = text_ids.reshape(split)[y, :, x].transpose(1, 0, 2, 3).reshape(NZ * NC, owned)
    first, second = jnp.where(c, y, x), jnp.where(c, x, y)
    at = []
    for j in range(4):
        for k in range(4):
            f, s = (first - k) % 4, (second - j) % 4
            at.append(jnp.where(c, f * NX + s, s * NX + f))
    img = img[jnp.stack(at)].reshape(1, -1)
    up = 1 - 2 * c
    sides = ((c, up), (1 - c, -up))
    at = []
    for core, sign in sides:
        order = [(0, core), (1, core), (1, 1 - core)]
        at += [(z - sign * k) % NZ * NC + d for k, d in order]
    for core, sign in sides:
        order = [(k, d) for k in (2, 3) for d in (core, 1 - core)]
        order.insert(4 if core is c else 0, (4, core))
        at += [(z - sign * k) % NZ * NC + d for k, d in order]
    txt = txt[jnp.stack(at)].reshape(-1, 1)
    return img, txt


def shards(images, texts, image_ids, text_ids, temp_log, bias):
    owned = images.shape[0]
    batch_all = owned * NX * NY * NZ * NC
    row, col = lax.axis_index("row"), lax.axis_index("col")
    x, y, z, c = row % NX, row // (2 * NX), 2 * (col // NC) + row // NX % 2, col % NC
    scale = jnp.exp(temp_log)
    coef = jnp.concatenate([scale, bias])
    img_ids, txt_ids = labels(image_ids, text_ids, x, y, z, c, owned)

    xn = normalize(images)
    yn = normalize(texts, [xn])
    sibling = hop_core(yn)
    line = [hop_first(xn, k) for k in (1, 2, 3)]
    near = join([xn] + line)
    ring = [join([yn, sibling])]
    ring.append(join([hop_z(ring[0], 1)], [near]))
    for _ in range(3):
        ring.append(hop_z(ring[-1], 1))
    image_blocks = [near] + [hop_second(near, k) for k in (1, 2, 3)]
    early = [yn, ring[1], sibling, hop_core(ring[1])]
    late = [ring[2], ring[3], ring[4], hop_core(ring[2]), hop_core(ring[3])]

    cut = 6 * owned
    zero = jnp.zeros((3, 8, 128), F32)
    g_early, t_early, part, xb = tile(
        coef, img_ids, txt_ids[:cut], zero, image_blocks, early, False
    )
    g_late, t_late, stats = tile(coef, img_ids, txt_ids[cut:], part, [xb], late, True)
    grads, rows = [g_early, g_late], [t_early, t_late]

    send = text_side(grads, xb, True)
    keep = text_side(grads, xb, False, [send])
    sent1, sent3, stats = image_side(
        grads, rows, (1, 3), [stats, exchange(stats, 6, 3)], [keep]
    )
    (sent2,) = image_side(grads, rows, (2,), (), [sent1])
    runs = (
        (0, 0, owned, F32),
        (owned, owned, 2 * owned, F32),
        (3 * owned, 4 * owned, 2 * owned, F32),
        (5 * owned, 6 * owned, 2 * owned, F32),
        (7 * owned, 3 * owned, owned, BF16),
    )
    gy, gy1, gy2, gy3, far, stats = text_add(
        keep, hop_core(send), runs, stats, exchange(stats, 7, 4), [sent2]
    )
    parts = [hop_second(g, -k) for k, g in zip((1, 2, 3), (sent1, sent2, sent3))]
    (own,) = image_side(grads, rows, (0,), (), [far])
    step, stats = step_add(gy3, hop_z(far, -1), [stats, exchange(stats, 5, 5)], [own])
    step, stats = step_add(gy2, hop_z(step, -1), [stats, exchange(stats, 1, 1)], [])
    keep, g1, g2, g3, stats = image_add(own, parts, stats, exchange(stats, 2, 2))
    (step,) = step_add(gy1, hop_z(step, -1), [], [keep])
    around = hop_z(step, -1)
    parts = [hop_first(g, -k) for k, g in ((1, g1), (2, g2), (3, g3))]
    text_parts = [(gy, 0), (around, 0), (hop_core(lower(around, parts[2])), 0)]

    stats = stats_sum(stats, parts)
    image_grad, text_grad, mark = finish(
        scale, (images, [(p, 0) for p in [keep] + parts]), (texts, text_parts)
    )
    total = scalars(scale, stats, exchange(stats, 0, 0), batch_all, mark)
    return image_grad, text_grad, total


def solution(mesh):
    spread = P(("row", "col"), None)
    return jax.shard_map(
        shards,
        mesh=mesh,
        in_specs=(spread, spread, P(), P(), P(), P()),
        out_specs=(spread, spread, P()),
        check_vma=False,
    )
```

```python
import functools
import itertools
import jax
import jax.numpy as jnp
from jax import lax
from jax.experimental import pallas as pl
from jax.experimental.pallas import tpu as pltpu
from jax.sharding import PartitionSpec as P

NX, NY, NZ, NC = 4, 4, 8, 2
LOG2E = 1.4426950408889634
F32, BF16 = jnp.float32, jnp.bfloat16
ANY = pl.BlockSpec(memory_space=pl.ANY)
STAT_ROWS = 16
VMEM = pl.BlockSpec(memory_space=pltpu.VMEM)
SMEM = pl.BlockSpec(memory_space=pltpu.SMEM)
BIG = pltpu.CompilerParams(vmem_limit_bytes=24 * 2**20)
SMALL = pltpu.CompilerParams(vmem_limit_bytes=12 * 2**20)


def linear(x, y, z, c):
    return (((y * 2 + z % 2) * NX + x) * (NZ // 2) + z // 2) * NC + c


def hop(a, move):
    pairs = []
    for x, y, z, c in itertools.product(range(NX), range(NY), range(NZ), range(NC)):
        dx, dy, dz, dc = move(c)
        to = linear((x + dx) % NX, (y + dy) % NY, (z + dz) % NZ, (c + dc) % NC)
        pairs.append((linear(x, y, z, c), to))
    return lax.ppermute(a, ("row", "col"), pairs)


def hop_first(a, k):
    return hop(a, lambda c: (0, k, 0, 0) if c else (k, 0, 0, 0))


def hop_second(a, k):
    return hop(a, lambda c: (k, 0, 0, 0) if c else (0, k, 0, 0))


def hop_z(a, k):
    return hop(a, lambda c: (0, 0, -k if c else k, 0))


def hop_core(a):
    return hop(a, lambda c: (0, 0, 0, 1))


def exchange(a, bit0, bit1):
    pairs = [(i, i ^ (1 << (bit1 if i % 2 else bit0))) for i in range(256)]
    return lax.ppermute(a, ("row", "col"), pairs)


def dot_t(a, b):
    return lax.dot_general(a, b, (((1,), (1,)), ((), ())), preferred_element_type=F32)


def dot_a(a, b):
    return lax.dot_general(a, b, (((0,), (0,)), ((), ())), preferred_element_type=F32)


def inverse_norm(rows):
    return lax.rsqrt(jnp.sum(rows * rows, axis=1, keepdims=True) + 1e-06)


def norm_kernel(raw, *refs):
    rows = raw[...].astype(F32)
    refs[-1][...] = (rows * inverse_norm(rows)).astype(BF16)


def normalize(raw, after=()):
    return pl.pallas_call(
        norm_kernel,
        out_shape=jax.ShapeDtypeStruct(raw.shape, BF16),
        in_specs=[VMEM] + [ANY] * len(after),
        out_specs=VMEM,
        name="normalize",
        compiler_params=SMALL,
    )(raw, *after)


def join_kernel(n, *refs):
    out, at = refs[-1], 0
    for part in refs[:n]:
        rows = part.shape[0]
        out[at : at + rows] = part[...]
        at += rows


def join(parts, after=()):
    rows = sum(p.shape[0] for p in parts)
    return pl.pallas_call(
        functools.partial(join_kernel, len(parts)),
        out_shape=jax.ShapeDtypeStruct((rows, parts[0].shape[1]), parts[0].dtype),
        in_specs=[VMEM] * len(parts) + [ANY] * len(after),
        out_specs=VMEM,
        name="join",
        compiler_params=SMALL,
    )(*parts, *after)


def load(refs, dst, sem, first, at=0, cuts=None):
    out = []
    for i, ref in enumerate(refs):
        start, rows = cuts[i] if cuts else (0, ref.shape[0])
        src = ref.at[pl.ds(start, rows)]
        copy = pltpu.make_async_copy(src, dst.at[pl.ds(at, rows)], sem.at[first + i])
        copy.start()
        out.append((at, copy))
        at += rows
    return out


def fold(v):
    u = jnp.sum(v.reshape(v.shape[0] // 8, 8, v.shape[1]), axis=0)
    return sum(u[:, k : k + 128] for k in range(0, u.shape[1], 128))


def put_stats(sums, rows, width):
    row = lax.broadcasted_iota(jnp.int32, (STAT_ROWS, width), 0)
    v = jnp.where(row % 3 == 0, sums[0], jnp.where(row % 3 == 1, sums[1], sums[2]))
    high = v.astype(BF16).astype(F32)
    mid = (v - high).astype(BF16).astype(F32)
    low = v - high - mid
    v = jnp.where(row < 3, high, jnp.where(row < 6, mid, low))
    rows[...] = jnp.where(row < 9, v, 0.0).astype(BF16)


def get_stats(rows):
    v = rows[...].astype(F32)
    return (v[0:3] + v[3:6]) + v[6:9]


def tile_steps(coef, image_ids, text_ids, before, xb, yb, grad, prods, steps, coming):
    rows = yb.shape[0]
    wide = 256
    scale, shift = coef[0] * LOG2E, coef[1] * LOG2E
    acc = [jnp.zeros((8, 128), F32)] * 3 if before is None else [before[i] for i in range(3)]

    def multiply(k):
        while coming and coming[0][0] < (k + 1) * wide:
            coming.pop(0)[1].wait()
        prods[k % 2] = dot_t(yb[...], xb[k * wide : (k + 1) * wide])

    multiply(steps[0])
    for k in steps:
        if k + 1 in steps:
            multiply(k + 1)
        dots = prods[k % 2]
        match = text_ids[:, :1] == image_ids[:1, k * wide : (k + 1) * wide]
        logits = dots * scale + shift
        e = jnp.exp2(jnp.where(match, -logits, logits))
        p = 1.0 + e
        s = e / p
        g = jnp.where(match, -s, s)
        grad[:, k * wide : (k + 1) * wide] = g.astype(BF16)
        acc[0] += fold(jnp.log2(p[: rows // 2] * p[rows // 2 :]))
        acc[1] += fold(g * dots)
        acc[2] += fold(g)
    while coming:
        coming.pop(0)[1].wait()
    return acc


def tile_first_kernel(cuts, coef, image_ids, text_ids, near, *refs):
    texts, (grad, yb, stats, xb, prods, sem) = refs[: len(cuts)], refs[len(cuts) :]
    coming = load(texts, yb, sem, 0, 0, cuts) + load([near], xb, sem, len(cuts))
    for _, copy in coming:
        copy.wait()
    acc = tile_steps(coef, image_ids, text_ids, None, xb, yb, grad, prods, [0], [])
    for i in range(3):
        stats[i] = acc[i]


def tile_rest_kernel(n, coef, image_ids, text_ids, before, yb, *refs):
    blocks, (grad, stats, xb, prods, sem) = refs[:n], refs[n + 2 :]
    coming = load(blocks, xb, sem, 0, xb.shape[0] - n * blocks[0].shape[0])
    steps = range(1, xb.shape[0] // 256)
    acc = tile_steps(coef, image_ids, text_ids, before, xb, yb, grad, prods, steps, coming)
    for i in range(3):
        stats[i] = acc[i]


def tile_late_kernel(cuts, coef, image_ids, text_ids, before, xb, *refs):
    texts, (grad, yb, stats, prods, sem) = refs[: len(cuts)], refs[len(cuts) :]
    for _, copy in load(texts, yb, sem, 0, 0, cuts):
        copy.wait()
    steps = range(xb.shape[0] // 256)
    acc = tile_steps(coef, image_ids, text_ids, before, xb, yb, grad, prods, steps, [])
    for i in range(3):
        stats[pl.ds(i, 1)] = jnp.full((1, 128), jnp.sum(acc[i]))


def tile_early(coef, image_ids, text_ids, images, texts, cuts):
    cols, rows = image_ids.shape[1], text_ids.shape[0]
    d = images[0].shape[1]
    n = len(texts)
    grad = jax.ShapeDtypeStruct((rows, cols), BF16)
    yb = jax.ShapeDtypeStruct((rows, d), BF16)
    stats = jax.ShapeDtypeStruct((3, 8, 128), F32)
    xb = jax.ShapeDtypeStruct((cols, d), BF16)
    prods = pltpu.VMEM((2, rows, 256), F32)
    g, y, part, x = pl.pallas_call(
        functools.partial(tile_first_kernel, cuts),
        out_shape=(grad, yb, stats, xb),
        in_specs=[SMEM, VMEM, VMEM] + [ANY] * (1 + n),
        out_specs=(VMEM,) * 4,
        scratch_shapes=[prods, pltpu.SemaphoreType.DMA((1 + n,))],
        name="tile_first",
        cost_estimate=pl.CostEstimate(
            flops=2 * rows * 256 * d, bytes_accessed=4 * rows * d, transcendentals=3 * rows * 256
        ),
        compiler_params=BIG,
    )(coef, image_ids, text_ids, images[0], *texts)
    n = len(images) - 1
    g, part, x = pl.pallas_call(
        functools.partial(tile_rest_kernel, n),
        out_shape=(grad, stats, xb),
        in_specs=[SMEM] + [VMEM] * 4 + [ANY] * n + [VMEM] * 2,
        out_specs=(VMEM,) * 3,
        scratch_shapes=[prods, pltpu.SemaphoreType.DMA((n,))],
        input_output_aliases={5 + n: 0, 6 + n: 2},
        name="tile_rest",
        cost_estimate=pl.CostEstimate(
            flops=2 * rows * cols * d, bytes_accessed=4 * cols * d, transcendentals=3 * rows * cols
        ),
        compiler_params=BIG,
    )(coef, image_ids, text_ids, part, y, *images[1:], g, x)
    return g, y, part, x


def tile_late(coef, image_ids, text_ids, before, xb, texts, cuts):
    cols, rows = image_ids.shape[1], text_ids.shape[0]
    d = xb.shape[1]
    n = len(texts)
    return pl.pallas_call(
        functools.partial(tile_late_kernel, cuts),
        out_shape=(
            jax.ShapeDtypeStruct((rows, cols), BF16),
            jax.ShapeDtypeStruct((rows, d), BF16),
            jax.ShapeDtypeStruct((3, 128), F32),
        ),
        in_specs=[SMEM] + [VMEM] * 4 + [ANY] * n,
        out_specs=(VMEM,) * 3,
        scratch_shapes=[pltpu.VMEM((2, rows, 256), F32), pltpu.SemaphoreType.DMA((n,))],
        name="tile_late",
        cost_estimate=pl.CostEstimate(
            flops=2 * rows * cols * d, bytes_accessed=4 * cols * d, transcendentals=3 * rows * cols
        ),
        compiler_params=BIG,
    )(coef, image_ids, text_ids, before, xb, *texts)


def text_side_kernel(lower, ge, gl, xb, *refs):
    out, at = refs[-1], 0
    for g in (ge, gl):
        half = g.shape[0] // 2
        first = half if lower else 0
        out[at : at + half] = jnp.dot(
            g[first : first + half], xb[...], preferred_element_type=F32
        )
        at += half


def text_side(grads, xb, lower, after=()):
    rows = sum(g.shape[0] for g in grads) // 2
    d = xb.shape[1]
    return pl.pallas_call(
        functools.partial(text_side_kernel, lower),
        out_shape=jax.ShapeDtypeStruct((rows, d), F32),
        in_specs=[VMEM] * 3 + [ANY] * len(after),
        out_specs=VMEM,
        name="text_side",
        compiler_params=BIG,
    )(*grads, xb, *after)


def image_side_kernel(blocks, with_stats, ge, gl, ye, yl, *refs):
    outs = refs[len(refs) - len(blocks) :]
    if with_stats:
        outs, sums = refs[len(refs) - len(blocks) - 1 : -1], refs[-1]
        sums[...] = refs[0][...] + refs[1][...]
    rows = outs[0].shape[0]
    for i, out in zip(blocks, outs):
        at = slice(i * rows, (i + 1) * rows)
        out[...] = (dot_a(ge[:, at], ye[...]) + dot_a(gl[:, at], yl[...])).astype(out.dtype)


def image_side(grads, texts, blocks, stats=(), after=()):
    d, cols = texts[0].shape[1], grads[0].shape[1]
    size = cols // 4
    return pl.pallas_call(
        functools.partial(image_side_kernel, blocks, bool(stats)),
        out_shape=tuple(jax.ShapeDtypeStruct((size, d), BF16 if i else F32) for i in blocks)
        + tuple(jax.ShapeDtypeStruct(s.shape, F32) for s in stats[:1]),
        in_specs=[VMEM] * (4 + len(stats)) + [ANY] * len(after),
        out_specs=(VMEM,) * (len(blocks) + len(stats[:1])),
        name="image_side",
        compiler_params=BIG,
    )(*grads, *texts, *stats, *after)


def total_four(own, parts):
    return (own + parts[1]) + (parts[0] + parts[2])


def image_add_kernel(own, a, b, c, stats, other, keep, out1, out2, out3, total):
    rows = keep.shape[0]
    v = stats[...] + other[...]
    total[...] = v
    sums = [v[i : i + 1, :1] for i in range(3)]
    for i, out in enumerate((keep, out1, out2, out3)):
        at = pl.ds(i * rows, rows)
        out[pl.ds(0, rows)] = (
            own[at] + a[at].astype(F32) + b[at].astype(F32) + c[at].astype(F32)
        ).astype(out.dtype)
        if i:
            put_stats(sums, out.at[pl.ds(rows, STAT_ROWS)], out.shape[1])


def image_add(own, parts, stats, other):
    rows, d = own.shape[0] // 4, own.shape[1]
    sent = jax.ShapeDtypeStruct((rows + STAT_ROWS, d), BF16)
    return pl.pallas_call(
        image_add_kernel,
        out_shape=(jax.ShapeDtypeStruct((rows, d), F32), sent, sent, sent)
        + (jax.ShapeDtypeStruct(stats.shape, F32),),
        in_specs=[VMEM] * 6,
        out_specs=(VMEM,) * 5,
        name="image_add",
        compiler_params=SMALL,
    )(own, *parts, stats, other)


def text_add_kernel(runs, own, other, stats, came, *refs):
    outs, sums = refs[len(refs) - len(runs) - 1 : -1], refs[-1]
    for (at_own, at_other, rows, _), out in zip(runs, outs):
        out[...] = (own[pl.ds(at_own, rows)] + other[pl.ds(at_other, rows)]).astype(out.dtype)
    sums[...] = stats[...] + came[...]


def text_add(own, other, runs, stats, came, after):
    d = own.shape[1]
    return pl.pallas_call(
        functools.partial(text_add_kernel, runs),
        out_shape=tuple(jax.ShapeDtypeStruct((rows, d), t) for _, _, rows, t in runs)
        + (jax.ShapeDtypeStruct(stats.shape, F32),),
        in_specs=[VMEM] * 4 + [ANY] * len(after),
        out_specs=(VMEM,) * (len(runs) + 1),
        name="text_add",
        compiler_params=SMALL,
    )(own, other, stats, came, *after)


def step_add_kernel(with_stats, a, b, *refs):
    out = refs[-2] if with_stats else refs[-1]
    came = b.shape[0]
    out[0:came] = (a[0:came] + b[...].astype(F32)).astype(out.dtype)
    if came < a.shape[0]:
        out[came:] = a[came:].astype(out.dtype)
    if with_stats:
        refs[-1][...] = refs[0][...] + refs[1][...]


def step_add(a, b, stats, after, dtype=BF16):
    return pl.pallas_call(
        functools.partial(step_add_kernel, bool(stats)),
        out_shape=(jax.ShapeDtypeStruct(a.shape, dtype),)
        + tuple(jax.ShapeDtypeStruct(s.shape, F32) for s in stats[:1]),
        in_specs=[VMEM] * (2 + len(stats)) + [ANY] * len(after),
        out_specs=(VMEM,) * (1 + len(stats[:1])),
        name="step_add",
        compiler_params=SMALL,
    )(a, b, *stats, *after)


def lower_kernel(a, *refs):
    refs[-1][...] = a[pl.ds(a.shape[0] // 2, a.shape[0] // 2)]


def lower(a, after):
    return pl.pallas_call(
        lower_kernel,
        out_shape=jax.ShapeDtypeStruct((a.shape[0] // 2, a.shape[1]), a.dtype),
        in_specs=[VMEM, ANY],
        out_specs=VMEM,
        name="lower",
        compiler_params=SMALL,
    )(a, after)


def finish_kernel(starts, scale, *refs):
    refs = list(refs)
    outs, mark = refs[-3:-1], refs[-1]
    mark[...] = jnp.zeros(mark.shape, F32)
    for at_list, out in zip(starts, outs):
        raw = refs.pop(0)
        parts = [refs.pop(0) for _ in at_list]
        rows = raw[...].astype(F32)
        inv = inverse_norm(rows)
        unit = rows * inv
        owned = raw.shape[0]
        g = scale[0] * sum(p[pl.ds(at, owned)].astype(F32) for p, at in zip(parts, at_list))
        out[...] = (inv * (g - unit * jnp.sum(unit * g, axis=1, keepdims=True))).astype(BF16)


def finish(scale, *sides):
    starts = [tuple(at for _, at in parts) for _, parts in sides]
    refs = [r for raw, parts in sides for r in [raw] + [p for p, _ in parts]]
    return pl.pallas_call(
        functools.partial(finish_kernel, starts),
        out_shape=tuple(jax.ShapeDtypeStruct(raw.shape, BF16) for raw, _ in sides)
        + (jax.ShapeDtypeStruct((8, 128), F32),),
        in_specs=[SMEM] + [VMEM] * len(refs),
        out_specs=(VMEM,) * (len(sides) + 1),
        name="finish",
        compiler_params=SMALL,
    )(scale, *refs)


def stats_kernel(mine, a, b, c, out):
    tail = pl.ds(a.shape[0] - STAT_ROWS, STAT_ROWS)
    out[...] = total_four(mine[...], [get_stats(p.at[tail])[:, :128] for p in (a, b, c)])


def stats_sum(mine, parts):
    return pl.pallas_call(
        stats_kernel,
        out_shape=jax.ShapeDtypeStruct((3, 128), F32),
        in_specs=[VMEM] * 4,
        out_specs=VMEM,
        name="stats_sum",
        compiler_params=SMALL,
    )(mine, *parts)


def scalars_kernel(batch, scale, a, b, after, out):
    v = (a[...] + b[...]) * (1.0 / batch)
    for i, factor in enumerate((1 / LOG2E, scale[0], 1.0)):
        out[i] = jnp.max(v[i : i + 1]) * factor


def scalars(scale, a, b, batch, after):
    return pl.pallas_call(
        functools.partial(scalars_kernel, batch),
        out_shape=jax.ShapeDtypeStruct((3,), F32),
        in_specs=[SMEM] + [VMEM] * 2 + [ANY],
        out_specs=SMEM,
        name="scalars",
        compiler_params=SMALL,
    )(scale, a, b, after)


def labels(image_ids, text_ids, x, y, z, c, owned):
    split = (NY, 2, NX, NZ // 2, NC, owned)
    img = image_ids.reshape(split)[:, z % 2, :, z // 2, c].reshape(NY * NX, owned)
    txt = text_ids.reshape(split)[y, :, x].transpose(1, 0, 2, 3).reshape(NZ * NC, owned)
    first, second = jnp.where(c, y, x), jnp.where(c, x, y)
    at = []
    for j in range(4):
        for k in range(4):
            f, s = (first - k) % 4, (second - j) % 4
            at.append(jnp.where(c, f * NX + s, s * NX + f))
    img = img[jnp.stack(at)].reshape(1, -1)
    up = 1 - 2 * c
    sides = ((c, up), (1 - c, -up))
    at = []
    for core, sign in sides:
        order = [(0, core), (1, core), (1, 1 - core)]
        at += [(z - sign * k) % NZ * NC + d for k, d in order]
    for core, sign in sides:
        order = [(k, d) for k in (2, 3) for d in (core, 1 - core)]
        order.insert(4 if core is c else 0, (4, core))
        at += [(z - sign * k) % NZ * NC + d for k, d in order]
    txt = txt[jnp.stack(at)].reshape(-1, 1)
    return img, txt


def shards(images, texts, image_ids, text_ids, temp_log, bias):
    owned = images.shape[0]
    batch_all = owned * NX * NY * NZ * NC
    row, col = lax.axis_index("row"), lax.axis_index("col")
    x, y, z, c = row % NX, row // (2 * NX), 2 * (col // NC) + row // NX % 2, col % NC
    scale = jnp.exp(temp_log)
    coef = jnp.concatenate([scale, bias])
    img_ids, txt_ids = labels(image_ids, text_ids, x, y, z, c, owned)

    xn = normalize(images)
    yn = normalize(texts, [xn])
    sibling = hop_core(yn)
    line = [hop_first(xn, k) for k in (1, 2, 3)]
    near = join([xn] + line)
    ring = [join([yn, sibling])]
    ring.append(join([hop_z(ring[0], 1)], [near]))
    for _ in range(3):
        ring.append(hop_z(ring[-1], 1))
    image_blocks = [near] + [hop_second(near, k) for k in (1, 2, 3)]
    two = 2 * owned
    early = [yn, ring[1], sibling, hop_core(ring[1])]
    late = [ring[2], ring[3], ring[4], hop_core(ring[2]), hop_core(ring[3])]
    early_cuts = ((0, owned), (0, two), (0, owned), (0, two))
    late_cuts = ((0, two),) * 5

    cut = 6 * owned
    g_early, t_early, part, xb = tile_early(
        coef, img_ids, txt_ids[:cut], image_blocks, early, early_cuts
    )
    g_late, t_late, stats = tile_late(
        coef, img_ids, txt_ids[cut:], part, xb, late, late_cuts
    )
    grads, rows = [g_early, g_late], [t_early, t_late]

    send = text_side(grads, xb, True)
    keep = text_side(grads, xb, False, [send])
    sent1, sent3, stats = image_side(
        grads, rows, (1, 3), [stats, exchange(stats, 6, 3)], [keep]
    )
    (sent2,) = image_side(grads, rows, (2,), (), [sent1])
    runs = (
        (0, 0, owned, F32),
        (owned, owned, 2 * owned, F32),
        (3 * owned, 4 * owned, 2 * owned, F32),
        (5 * owned, 6 * owned, 2 * owned, F32),
        (7 * owned, 3 * owned, owned, BF16),
    )
    gy, gy1, gy2, gy3, far, stats = text_add(
        keep, hop_core(send), runs, stats, exchange(stats, 7, 4), [sent2]
    )
    parts = [hop_second(g, -k) for k, g in zip((1, 2, 3), (sent1, sent2, sent3))]
    (own,) = image_side(grads, rows, (0,), (), [far])
    step, stats = step_add(gy3, hop_z(far, -1), [stats, exchange(stats, 5, 5)], [own])
    step, stats = step_add(gy2, hop_z(step, -1), [stats, exchange(stats, 1, 1)], [])
    keep, g1, g2, g3, stats = image_add(own, parts, stats, exchange(stats, 2, 2))
    (step,) = step_add(gy1, hop_z(step, -1), [], [keep])
    around = hop_z(step, -1)
    parts = [hop_first(g, -k) for k, g in ((1, g1), (2, g2), (3, g3))]
    text_parts = [(gy, 0), (around, 0), (hop_core(lower(around, parts[2])), 0)]

    stats = stats_sum(stats, parts)
    image_grad, text_grad, mark = finish(
        scale, (images, [(p, 0) for p in [keep] + parts]), (texts, text_parts)
    )
    total = scalars(scale, stats, exchange(stats, 0, 0), batch_all, mark)
    return image_grad, text_grad, total


def solution(mesh):
    spread = P(("row", "col"), None)
    return jax.shard_map(
        shards,
        mesh=mesh,
        in_specs=(spread, spread, P(), P(), P(), P()),
        out_specs=(spread, spread, P()),
        check_vma=False,
    )
```

```python
import functools
import itertools
import jax
import jax.numpy as jnp
from jax import lax
from jax.experimental import pallas as pl
from jax.experimental.pallas import tpu as pltpu
from jax.sharding import PartitionSpec as P

NX, NY, NZ, NC = 4, 4, 8, 2
LOG2E = 1.4426950408889634
F32, BF16 = jnp.float32, jnp.bfloat16
ANY = pl.BlockSpec(memory_space=pl.ANY)
STAT_ROWS = 16
VMEM = pl.BlockSpec(memory_space=pltpu.VMEM)
SMEM = pl.BlockSpec(memory_space=pltpu.SMEM)
BIG = pltpu.CompilerParams(vmem_limit_bytes=24 * 2**20)
SMALL = pltpu.CompilerParams(vmem_limit_bytes=12 * 2**20)


def linear(x, y, z, c):
    return (((y * 2 + z % 2) * NX + x) * (NZ // 2) + z // 2) * NC + c


def hop(a, move):
    pairs = []
    for x, y, z, c in itertools.product(range(NX), range(NY), range(NZ), range(NC)):
        dx, dy, dz, dc = move(c)
        to = linear((x + dx) % NX, (y + dy) % NY, (z + dz) % NZ, (c + dc) % NC)
        pairs.append((linear(x, y, z, c), to))
    return lax.ppermute(a, ("row", "col"), pairs)


def hop_first(a, k):
    return hop(a, lambda c: (0, k, 0, 0) if c else (k, 0, 0, 0))


def hop_second(a, k):
    return hop(a, lambda c: (k, 0, 0, 0) if c else (0, k, 0, 0))


def hop_z(a, k):
    return hop(a, lambda c: (0, 0, -k if c else k, 0))


def hop_core(a):
    return hop(a, lambda c: (0, 0, 0, 1))


def exchange(a, bit0, bit1):
    pairs = [(i, i ^ (1 << (bit1 if i % 2 else bit0))) for i in range(256)]
    return lax.ppermute(a, ("row", "col"), pairs)


def dot_t(a, b):
    return lax.dot_general(a, b, (((1,), (1,)), ((), ())), preferred_element_type=F32)


def dot_a(a, b):
    return lax.dot_general(a, b, (((0,), (0,)), ((), ())), preferred_element_type=F32)


def inverse_norm(rows):
    return lax.rsqrt(jnp.sum(rows * rows, axis=1, keepdims=True) + 1e-06)


def norm_kernel(raw, *refs):
    rows = raw[...].astype(F32)
    refs[-1][...] = (rows * inverse_norm(rows)).astype(BF16)


def normalize(raw, after=()):
    return pl.pallas_call(
        norm_kernel,
        out_shape=jax.ShapeDtypeStruct(raw.shape, BF16),
        in_specs=[VMEM] + [ANY] * len(after),
        out_specs=VMEM,
        name="normalize",
        compiler_params=SMALL,
    )(raw, *after)


def join_kernel(n, *refs):
    out, at = refs[-1], 0
    for part in refs[:n]:
        rows = part.shape[0]
        out[at : at + rows] = part[...]
        at += rows


def join(parts, after=()):
    rows = sum(p.shape[0] for p in parts)
    return pl.pallas_call(
        functools.partial(join_kernel, len(parts)),
        out_shape=jax.ShapeDtypeStruct((rows, parts[0].shape[1]), parts[0].dtype),
        in_specs=[VMEM] * len(parts) + [ANY] * len(after),
        out_specs=VMEM,
        name="join",
        compiler_params=SMALL,
    )(*parts, *after)


def load(refs, dst, sem, first, at=0, cuts=None):
    out = []
    for i, ref in enumerate(refs):
        start, rows = cuts[i] if cuts else (0, ref.shape[0])
        src = ref.at[pl.ds(start, rows)]
        copy = pltpu.make_async_copy(src, dst.at[pl.ds(at, rows)], sem.at[first + i])
        copy.start()
        out.append((at, copy))
        at += rows
    return out


def fold(v):
    u = jnp.sum(v.reshape(v.shape[0] // 8, 8, v.shape[1]), axis=0)
    return sum(u[:, k : k + 128] for k in range(0, u.shape[1], 128))


def put_stats(sums, rows, width):
    row = lax.broadcasted_iota(jnp.int32, (STAT_ROWS, width), 0)
    v = jnp.where(row % 3 == 0, sums[0], jnp.where(row % 3 == 1, sums[1], sums[2]))
    high = v.astype(BF16).astype(F32)
    mid = (v - high).astype(BF16).astype(F32)
    low = v - high - mid
    v = jnp.where(row < 3, high, jnp.where(row < 6, mid, low))
    rows[...] = jnp.where(row < 9, v, 0.0).astype(BF16)


def get_stats(rows):
    v = rows[...].astype(F32)
    return (v[0:3] + v[3:6]) + v[6:9]


def tile_steps(coef, image_ids, text_ids, before, xb, yb, grad, prods, steps, coming):
    rows = yb.shape[0]
    wide = 256
    scale, shift = coef[0] * LOG2E, coef[1] * LOG2E
    acc = [jnp.zeros((8, 128), F32)] * 3 if before is None else [before[i] for i in range(3)]

    def multiply(k):
        while coming and coming[0][0] < (k + 1) * wide:
            coming.pop(0)[1].wait()
        prods[k % 2] = dot_t(yb[...], xb[k * wide : (k + 1) * wide])

    multiply(steps[0])
    for k in steps:
        if k + 1 in steps:
            multiply(k + 1)
        dots = prods[k % 2]
        match = text_ids[:, :1] == image_ids[:1, k * wide : (k + 1) * wide]
        logits = dots * scale + shift
        e = jnp.exp2(jnp.where(match, -logits, logits))
        p = 1.0 + e
        s = e / p
        g = jnp.where(match, -s, s)
        grad[:, k * wide : (k + 1) * wide] = g.astype(BF16)
        acc[0] += fold(jnp.log2(p[: rows // 2] * p[rows // 2 :]))
        acc[1] += fold(g * dots)
        acc[2] += fold(g)
    while coming:
        coming.pop(0)[1].wait()
    return acc


def tile_first_kernel(cuts, coef, image_ids, text_ids, near, *refs):
    texts, (grad, yb, stats, xb, prods, sem) = refs[: len(cuts)], refs[len(cuts) :]
    coming = load(texts, yb, sem, 0, 0, cuts) + load([near], xb, sem, len(cuts))
    for _, copy in coming:
        copy.wait()
    acc = tile_steps(coef, image_ids, text_ids, None, xb, yb, grad, prods, [0], [])
    for i in range(3):
        stats[i] = acc[i]


def tile_rest_kernel(n, coef, image_ids, text_ids, before, yb, *refs):
    blocks, (grad, stats, xb, prods, sem) = refs[:n], refs[n + 2 :]
    coming = load(blocks, xb, sem, 0, xb.shape[0] - n * blocks[0].shape[0])
    steps = range(1, xb.shape[0] // 256)
    acc = tile_steps(coef, image_ids, text_ids, before, xb, yb, grad, prods, steps, coming)
    for i in range(3):
        stats[i] = acc[i]


def tile_late_kernel(cuts, coef, image_ids, text_ids, before, xb, *refs):
    texts, (grad, yb, stats, prods, sem) = refs[: len(cuts)], refs[len(cuts) :]
    for _, copy in load(texts, yb, sem, 0, 0, cuts):
        copy.wait()
    steps = range(xb.shape[0] // 256)
    acc = tile_steps(coef, image_ids, text_ids, before, xb, yb, grad, prods, steps, [])
    for i in range(3):
        stats[pl.ds(i, 1)] = jnp.full((1, 128), jnp.sum(acc[i]))


def tile_early(coef, image_ids, text_ids, images, texts, cuts):
    cols, rows = image_ids.shape[1], text_ids.shape[0]
    d = images[0].shape[1]
    n = len(texts)
    grad = jax.ShapeDtypeStruct((rows, cols), BF16)
    yb = jax.ShapeDtypeStruct((rows, d), BF16)
    stats = jax.ShapeDtypeStruct((3, 8, 128), F32)
    xb = jax.ShapeDtypeStruct((cols, d), BF16)
    prods = pltpu.VMEM((2, rows, 256), F32)
    g, y, part, x = pl.pallas_call(
        functools.partial(tile_first_kernel, cuts),
        out_shape=(grad, yb, stats, xb),
        in_specs=[SMEM, VMEM, VMEM] + [ANY] * (1 + n),
        out_specs=(VMEM,) * 4,
        scratch_shapes=[prods, pltpu.SemaphoreType.DMA((1 + n,))],
        name="tile_first",
        cost_estimate=pl.CostEstimate(
            flops=2 * rows * 256 * d, bytes_accessed=4 * rows * d, transcendentals=3 * rows * 256
        ),
        compiler_params=BIG,
    )(coef, image_ids, text_ids, images[0], *texts)
    n = len(images) - 1
    g, part, x = pl.pallas_call(
        functools.partial(tile_rest_kernel, n),
        out_shape=(grad, stats, xb),
        in_specs=[SMEM] + [VMEM] * 4 + [ANY] * n + [VMEM] * 2,
        out_specs=(VMEM,) * 3,
        scratch_shapes=[prods, pltpu.SemaphoreType.DMA((n,))],
        input_output_aliases={5 + n: 0, 6 + n: 2},
        name="tile_rest",
        cost_estimate=pl.CostEstimate(
            flops=2 * rows * cols * d, bytes_accessed=4 * cols * d, transcendentals=3 * rows * cols
        ),
        compiler_params=BIG,
    )(coef, image_ids, text_ids, part, y, *images[1:], g, x)
    return g, y, part, x


def tile_late(coef, image_ids, text_ids, before, xb, texts, cuts):
    cols, rows = image_ids.shape[1], text_ids.shape[0]
    d = xb.shape[1]
    n = len(texts)
    return pl.pallas_call(
        functools.partial(tile_late_kernel, cuts),
        out_shape=(
            jax.ShapeDtypeStruct((rows, cols), BF16),
            jax.ShapeDtypeStruct((rows, d), BF16),
            jax.ShapeDtypeStruct((3, 128), F32),
        ),
        in_specs=[SMEM] + [VMEM] * 4 + [ANY] * n,
        out_specs=(VMEM,) * 3,
        scratch_shapes=[pltpu.VMEM((2, rows, 256), F32), pltpu.SemaphoreType.DMA((n,))],
        name="tile_late",
        cost_estimate=pl.CostEstimate(
            flops=2 * rows * cols * d, bytes_accessed=4 * cols * d, transcendentals=3 * rows * cols
        ),
        compiler_params=BIG,
    )(coef, image_ids, text_ids, before, xb, *texts)


def text_side_kernel(lower, ge, gl, xb, *refs):
    out, at = refs[-1], 0
    for g in (ge, gl):
        half = g.shape[0] // 2
        first = half if lower else 0
        out[at : at + half] = jnp.dot(
            g[first : first + half], xb[...], preferred_element_type=F32
        )
        at += half


def text_side(grads, xb, lower, after=()):
    rows = sum(g.shape[0] for g in grads) // 2
    d = xb.shape[1]
    return pl.pallas_call(
        functools.partial(text_side_kernel, lower),
        out_shape=jax.ShapeDtypeStruct((rows, d), F32),
        in_specs=[VMEM] * 3 + [ANY] * len(after),
        out_specs=VMEM,
        name="text_side",
        compiler_params=BIG,
    )(*grads, xb, *after)


def image_side_kernel(blocks, with_stats, ge, gl, ye, yl, *refs):
    outs = refs[len(refs) - len(blocks) :]
    if with_stats:
        outs, sums = refs[len(refs) - len(blocks) - 1 : -1], refs[-1]
        sums[...] = refs[0][...] + refs[1][...]
    rows = outs[0].shape[0]
    for i, out in zip(blocks, outs):
        at = slice(i * rows, (i + 1) * rows)
        out[...] = (dot_a(ge[:, at], ye[...]) + dot_a(gl[:, at], yl[...])).astype(out.dtype)


def image_side(grads, texts, blocks, stats=(), after=()):
    d, cols = texts[0].shape[1], grads[0].shape[1]
    size = cols // 4
    return pl.pallas_call(
        functools.partial(image_side_kernel, blocks, bool(stats)),
        out_shape=tuple(jax.ShapeDtypeStruct((size, d), BF16 if i else F32) for i in blocks)
        + tuple(jax.ShapeDtypeStruct(s.shape, F32) for s in stats[:1]),
        in_specs=[VMEM] * (4 + len(stats)) + [ANY] * len(after),
        out_specs=(VMEM,) * (len(blocks) + len(stats[:1])),
        name="image_side",
        compiler_params=BIG,
    )(*grads, *texts, *stats, *after)


def total_four(own, parts):
    return (own + parts[1]) + (parts[0] + parts[2])


def image_add_kernel(own, a, b, c, stats, other, keep, out1, out2, out3, total):
    rows = keep.shape[0]
    v = stats[...] + other[...]
    total[...] = v
    sums = [v[i : i + 1, :1] for i in range(3)]
    for i, out in enumerate((keep, out1, out2, out3)):
        at = pl.ds(i * rows, rows)
        out[pl.ds(0, rows)] = (
            own[at] + a[at].astype(F32) + b[at].astype(F32) + c[at].astype(F32)
        ).astype(out.dtype)
        if i:
            put_stats(sums, out.at[pl.ds(rows, STAT_ROWS)], out.shape[1])


def image_add(own, parts, stats, other):
    rows, d = own.shape[0] // 4, own.shape[1]
    sent = jax.ShapeDtypeStruct((rows + STAT_ROWS, d), BF16)
    return pl.pallas_call(
        image_add_kernel,
        out_shape=(jax.ShapeDtypeStruct((rows, d), F32), sent, sent, sent)
        + (jax.ShapeDtypeStruct(stats.shape, F32),),
        in_specs=[VMEM] * 6,
        out_specs=(VMEM,) * 5,
        name="image_add",
        compiler_params=SMALL,
    )(own, *parts, stats, other)


def text_add_kernel(runs, own, other, stats, came, *refs):
    outs, sums = refs[len(refs) - len(runs) - 1 : -1], refs[-1]
    for (at_own, at_other, rows, _), out in zip(runs, outs):
        out[...] = (own[pl.ds(at_own, rows)] + other[pl.ds(at_other, rows)]).astype(out.dtype)
    sums[...] = stats[...] + came[...]


def text_add(own, other, runs, stats, came, after):
    d = own.shape[1]
    return pl.pallas_call(
        functools.partial(text_add_kernel, runs),
        out_shape=tuple(jax.ShapeDtypeStruct((rows, d), t) for _, _, rows, t in runs)
        + (jax.ShapeDtypeStruct(stats.shape, F32),),
        in_specs=[VMEM] * 4 + [ANY] * len(after),
        out_specs=(VMEM,) * (len(runs) + 1),
        name="text_add",
        compiler_params=SMALL,
    )(own, other, stats, came, *after)


def step_add_kernel(with_stats, a, b, *refs):
    out = refs[-2] if with_stats else refs[-1]
    came = b.shape[0]
    out[0:came] = (a[0:came] + b[...].astype(F32)).astype(out.dtype)
    if came < a.shape[0]:
        out[came:] = a[came:].astype(out.dtype)
    if with_stats:
        refs[-1][...] = refs[0][...] + refs[1][...]


def step_add(a, b, stats, after, dtype=BF16):
    return pl.pallas_call(
        functools.partial(step_add_kernel, bool(stats)),
        out_shape=(jax.ShapeDtypeStruct(a.shape, dtype),)
        + tuple(jax.ShapeDtypeStruct(s.shape, F32) for s in stats[:1]),
        in_specs=[VMEM] * (2 + len(stats)) + [ANY] * len(after),
        out_specs=(VMEM,) * (1 + len(stats[:1])),
        name="step_add",
        compiler_params=SMALL,
    )(a, b, *stats, *after)


def lower_kernel(a, *refs):
    refs[-1][...] = a[pl.ds(a.shape[0] // 2, a.shape[0] // 2)]


def lower(a, after):
    return pl.pallas_call(
        lower_kernel,
        out_shape=jax.ShapeDtypeStruct((a.shape[0] // 2, a.shape[1]), a.dtype),
        in_specs=[VMEM, ANY],
        out_specs=VMEM,
        name="lower",
        compiler_params=SMALL,
    )(a, after)


def finish_kernel(starts, scale, *refs):
    refs = list(refs)
    outs, mark = refs[-3:-1], refs[-1]
    mark[...] = jnp.zeros(mark.shape, F32)
    for at_list, out in zip(starts, outs):
        raw = refs.pop(0)
        parts = [refs.pop(0) for _ in at_list]
        rows = raw[...].astype(F32)
        inv = inverse_norm(rows)
        unit = rows * inv
        owned = raw.shape[0]
        g = scale[0] * sum(p[pl.ds(at, owned)].astype(F32) for p, at in zip(parts, at_list))
        out[...] = (inv * (g - unit * jnp.sum(unit * g, axis=1, keepdims=True))).astype(BF16)


def finish(scale, *sides):
    starts = [tuple(at for _, at in parts) for _, parts in sides]
    refs = [r for raw, parts in sides for r in [raw] + [p for p, _ in parts]]
    return pl.pallas_call(
        functools.partial(finish_kernel, starts),
        out_shape=tuple(jax.ShapeDtypeStruct(raw.shape, BF16) for raw, _ in sides)
        + (jax.ShapeDtypeStruct((8, 128), F32),),
        in_specs=[SMEM] + [VMEM] * len(refs),
        out_specs=(VMEM,) * (len(sides) + 1),
        name="finish",
        compiler_params=SMALL,
    )(scale, *refs)


def stats_kernel(mine, a, b, c, out):
    tail = pl.ds(a.shape[0] - STAT_ROWS, STAT_ROWS)
    out[...] = total_four(mine[...], [get_stats(p.at[tail])[:, :128] for p in (a, b, c)])


def stats_sum(mine, parts):
    return pl.pallas_call(
        stats_kernel,
        out_shape=jax.ShapeDtypeStruct((3, 128), F32),
        in_specs=[VMEM] * 4,
        out_specs=VMEM,
        name="stats_sum",
        compiler_params=SMALL,
    )(mine, *parts)


def scalars_kernel(batch, scale, a, b, after, out):
    v = (a[...] + b[...]) * (1.0 / batch)
    for i, factor in enumerate((1 / LOG2E, scale[0], 1.0)):
        out[i] = jnp.max(v[i : i + 1]) * factor


def scalars(scale, a, b, batch, after):
    return pl.pallas_call(
        functools.partial(scalars_kernel, batch),
        out_shape=jax.ShapeDtypeStruct((3,), F32),
        in_specs=[SMEM] + [VMEM] * 2 + [ANY],
        out_specs=SMEM,
        name="scalars",
        compiler_params=SMALL,
    )(scale, a, b, after)


def labels(image_ids, text_ids, x, y, z, c, owned):
    split = (NY, 2, NX, NZ // 2, NC, owned)
    img = image_ids.reshape(split)[:, z % 2, :, z // 2, c].reshape(NY * NX, owned)
    txt = text_ids.reshape(split)[y, :, x].transpose(1, 0, 2, 3).reshape(NZ * NC, owned)
    first, second = jnp.where(c, y, x), jnp.where(c, x, y)
    at = []
    for j in range(4):
        for k in range(4):
            f, s = (first - k) % 4, (second - j) % 4
            at.append(jnp.where(c, f * NX + s, s * NX + f))
    img = img[jnp.stack(at)].reshape(1, -1)
    up = 1 - 2 * c
    sides = ((c, up), (1 - c, -up))
    at = []
    for core, sign in sides:
        order = [(0, core), (1, core), (1, 1 - core)]
        at += [(z - sign * k) % NZ * NC + d for k, d in order]
    for core, sign in sides:
        order = [(k, d) for k in (2, 3) for d in (core, 1 - core)]
        order.insert(4 if core is c else 0, (4, core))
        at += [(z - sign * k) % NZ * NC + d for k, d in order]
    txt = txt[jnp.stack(at)].reshape(-1, 1)
    return img, txt


def shards(images, texts, image_ids, text_ids, temp_log, bias):
    owned = images.shape[0]
    batch_all = owned * NX * NY * NZ * NC
    row, col = lax.axis_index("row"), lax.axis_index("col")
    x, y, z, c = row % NX, row // (2 * NX), 2 * (col // NC) + row // NX % 2, col % NC
    scale = jnp.exp(temp_log)
    coef = jnp.concatenate([scale, bias])
    img_ids, txt_ids = labels(image_ids, text_ids, x, y, z, c, owned)

    yn = normalize(texts)
    xn = normalize(images, [yn])
    sibling = hop_core(yn)
    line = [hop_first(xn, k) for k in (1, 2, 3)]
    near = join([xn] + line)
    ring = [join([yn, sibling])]
    ring.append(join([hop_z(ring[0], 1)], [near]))
    for _ in range(3):
        ring.append(hop_z(ring[-1], 1))
    image_blocks = [near] + [hop_second(near, k) for k in (1, 2, 3)]
    two = 2 * owned
    early = [yn, ring[1], sibling, hop_core(ring[1])]
    late = [ring[2], ring[3], ring[4], hop_core(ring[2]), hop_core(ring[3])]
    early_cuts = ((0, owned), (0, two), (0, owned), (0, two))
    late_cuts = ((0, two),) * 5

    cut = 6 * owned
    g_early, t_early, part, xb = tile_early(
        coef, img_ids, txt_ids[:cut], image_blocks, early, early_cuts
    )
    g_late, t_late, stats = tile_late(
        coef, img_ids, txt_ids[cut:], part, xb, late, late_cuts
    )
    grads, rows = [g_early, g_late], [t_early, t_late]

    send = text_side(grads, xb, True)
    keep = text_side(grads, xb, False, [send])
    sent1, sent3, stats = image_side(
        grads, rows, (1, 3), [stats, exchange(stats, 6, 3)], [keep]
    )
    (sent2,) = image_side(grads, rows, (2,), (), [sent1])
    runs = (
        (0, 0, owned, F32),
        (owned, owned, 2 * owned, F32),
        (3 * owned, 4 * owned, 2 * owned, F32),
        (5 * owned, 6 * owned, 2 * owned, F32),
        (7 * owned, 3 * owned, owned, BF16),
    )
    gy, gy1, gy2, gy3, far, stats = text_add(
        keep, hop_core(send), runs, stats, exchange(stats, 5, 5), [sent2]
    )
    parts = [hop_second(g, -k) for k, g in zip((1, 2, 3), (sent1, sent2, sent3))]
    (own,) = image_side(grads, rows, (0,), (), [far])
    step, stats = step_add(gy3, hop_z(far, -1), [stats, exchange(stats, 1, 1)], [own])
    step, stats = step_add(gy2, hop_z(step, -1), [stats, exchange(stats, 2, 2)], [])
    keep, g1, g2, g3, stats = image_add(own, parts, stats, exchange(stats, 7, 4))
    (step,) = step_add(gy1, hop_z(step, -1), [], [keep])
    around = hop_z(step, -1)
    parts = [hop_first(g, -k) for k, g in ((1, g1), (2, g2), (3, g3))]
    text_parts = [(gy, 0), (around, 0), (hop_core(lower(around, parts[2])), 0)]

    stats = stats_sum(stats, parts)
    image_grad, text_grad, mark = finish(
        scale, (images, [(p, 0) for p in [keep] + parts]), (texts, text_parts)
    )
    total = scalars(scale, stats, exchange(stats, 0, 0), batch_all, mark)
    return image_grad, text_grad, total


def solution(mesh):
    spread = P(("row", "col"), None)
    return jax.shard_map(
        shards,
        mesh=mesh,
        in_specs=(spread, spread, P(), P(), P(), P()),
        out_specs=(spread, spread, P()),
        check_vma=False,
    )
```

```python
import functools
import itertools
import jax
import jax.numpy as jnp
from jax import lax
from jax.experimental import pallas as pl
from jax.experimental.pallas import tpu as pltpu
from jax.sharding import PartitionSpec as P

NX, NY, NZ, NC = 4, 4, 8, 2
LOG2E = 1.4426950408889634
F32, BF16 = jnp.float32, jnp.bfloat16
ANY = pl.BlockSpec(memory_space=pl.ANY)
STAT_ROWS = 16
VMEM = pl.BlockSpec(memory_space=pltpu.VMEM)
SMEM = pl.BlockSpec(memory_space=pltpu.SMEM)
BIG = pltpu.CompilerParams(vmem_limit_bytes=24 * 2**20)
SMALL = pltpu.CompilerParams(vmem_limit_bytes=12 * 2**20)


def linear(x, y, z, c):
    return (((y * 2 + z % 2) * NX + x) * (NZ // 2) + z // 2) * NC + c


def hop(a, move):
    pairs = []
    for x, y, z, c in itertools.product(range(NX), range(NY), range(NZ), range(NC)):
        dx, dy, dz, dc = move(c)
        to = linear((x + dx) % NX, (y + dy) % NY, (z + dz) % NZ, (c + dc) % NC)
        pairs.append((linear(x, y, z, c), to))
    return lax.ppermute(a, ("row", "col"), pairs)


def hop_first(a, k):
    return hop(a, lambda c: (0, k, 0, 0) if c else (k, 0, 0, 0))


def hop_second(a, k):
    return hop(a, lambda c: (k, 0, 0, 0) if c else (0, k, 0, 0))


def hop_z(a, k):
    return hop(a, lambda c: (0, 0, -k if c else k, 0))


def hop_core(a):
    return hop(a, lambda c: (0, 0, 0, 1))


def exchange(a, bit0, bit1):
    pairs = [(i, i ^ (1 << (bit1 if i % 2 else bit0))) for i in range(256)]
    return lax.ppermute(a, ("row", "col"), pairs)


def dot_t(a, b):
    return lax.dot_general(a, b, (((1,), (1,)), ((), ())), preferred_element_type=F32)


def dot_a(a, b):
    return lax.dot_general(a, b, (((0,), (0,)), ((), ())), preferred_element_type=F32)


def inverse_norm(rows):
    return lax.rsqrt(jnp.sum(rows * rows, axis=1, keepdims=True) + 1e-06)


def norm_kernel(raw, *refs):
    rows = raw[...].astype(F32)
    refs[-1][...] = (rows * inverse_norm(rows)).astype(BF16)


def normalize(raw, after=()):
    return pl.pallas_call(
        norm_kernel,
        out_shape=jax.ShapeDtypeStruct(raw.shape, BF16),
        in_specs=[VMEM] + [ANY] * len(after),
        out_specs=VMEM,
        name="normalize",
        compiler_params=SMALL,
    )(raw, *after)


def join_kernel(n, *refs):
    out, at = refs[-1], 0
    for part in refs[:n]:
        rows = part.shape[0]
        out[at : at + rows] = part[...]
        at += rows


def join(parts, after=()):
    rows = sum(p.shape[0] for p in parts)
    return pl.pallas_call(
        functools.partial(join_kernel, len(parts)),
        out_shape=jax.ShapeDtypeStruct((rows, parts[0].shape[1]), parts[0].dtype),
        in_specs=[VMEM] * len(parts) + [ANY] * len(after),
        out_specs=VMEM,
        name="join",
        compiler_params=SMALL,
    )(*parts, *after)


def load(refs, dst, sem, first, at=0, cuts=None):
    out = []
    for i, ref in enumerate(refs):
        start, rows = cuts[i] if cuts else (0, ref.shape[0])
        src = ref.at[pl.ds(start, rows)]
        copy = pltpu.make_async_copy(src, dst.at[pl.ds(at, rows)], sem.at[first + i])
        copy.start()
        out.append((at, copy))
        at += rows
    return out


def fold(v):
    u = jnp.sum(v.reshape(v.shape[0] // 8, 8, v.shape[1]), axis=0)
    return sum(u[:, k : k + 128] for k in range(0, u.shape[1], 128))


def put_stats(sums, rows, width):
    row = lax.broadcasted_iota(jnp.int32, (STAT_ROWS, width), 0)
    v = jnp.where(row % 3 == 0, sums[0], jnp.where(row % 3 == 1, sums[1], sums[2]))
    high = v.astype(BF16).astype(F32)
    mid = (v - high).astype(BF16).astype(F32)
    low = v - high - mid
    v = jnp.where(row < 3, high, jnp.where(row < 6, mid, low))
    rows[...] = jnp.where(row < 9, v, 0.0).astype(BF16)


def get_stats(rows):
    v = rows[...].astype(F32)
    return (v[0:3] + v[3:6]) + v[6:9]


def tile_steps(coef, image_ids, text_ids, before, xb, yb, grad, prods, steps, coming):
    rows = yb.shape[0]
    wide = 256
    scale, shift = coef[0] * LOG2E, coef[1] * LOG2E
    acc = [jnp.zeros((8, 128), F32)] * 3 if before is None else [before[i] for i in range(3)]

    def multiply(k):
        while coming and coming[0][0] < (k + 1) * wide:
            coming.pop(0)[1].wait()
        prods[k % 2] = dot_t(yb[...], xb[k * wide : (k + 1) * wide])

    multiply(steps[0])
    for k in steps:
        if k + 1 in steps:
            multiply(k + 1)
        dots = prods[k % 2]
        match = text_ids[:, :1] == image_ids[:1, k * wide : (k + 1) * wide]
        logits = dots * scale + shift
        e = jnp.exp2(jnp.where(match, -logits, logits))
        p = 1.0 + e
        s = e / p
        g = jnp.where(match, -s, s)
        grad[:, k * wide : (k + 1) * wide] = g.astype(BF16)
        acc[0] += fold(jnp.log2(p[: rows // 2] * p[rows // 2 :]))
        acc[1] += fold(g * dots)
        acc[2] += fold(g)
    while coming:
        coming.pop(0)[1].wait()
    return acc


def tile_first_kernel(cuts, coef, image_ids, text_ids, near, *refs):
    texts, (grad, yb, stats, xb, prods, sem) = refs[: len(cuts)], refs[len(cuts) :]
    coming = load(texts, yb, sem, 0, 0, cuts) + load([near], xb, sem, len(cuts))
    for _, copy in coming:
        copy.wait()
    acc = tile_steps(coef, image_ids, text_ids, None, xb, yb, grad, prods, [0], [])
    for i in range(3):
        stats[i] = acc[i]


def tile_rest_kernel(n, coef, image_ids, text_ids, before, yb, *refs):
    blocks, (grad, stats, xb, prods, sem) = refs[:n], refs[n + 2 :]
    coming = load(blocks, xb, sem, 0, xb.shape[0] - n * blocks[0].shape[0])
    steps = range(1, xb.shape[0] // 256)
    acc = tile_steps(coef, image_ids, text_ids, before, xb, yb, grad, prods, steps, coming)
    for i in range(3):
        stats[i] = acc[i]


def tile_late_kernel(cuts, coef, image_ids, text_ids, before, xb, *refs):
    texts, (grad, yb, stats, prods, sem) = refs[: len(cuts)], refs[len(cuts) :]
    for _, copy in load(texts, yb, sem, 0, 0, cuts):
        copy.wait()
    steps = range(xb.shape[0] // 256)
    acc = tile_steps(coef, image_ids, text_ids, before, xb, yb, grad, prods, steps, [])
    for i in range(3):
        stats[pl.ds(i, 1)] = jnp.full((1, 128), jnp.sum(acc[i]))


def tile_early(coef, image_ids, text_ids, images, texts, cuts):
    cols, rows = image_ids.shape[1], text_ids.shape[0]
    d = images[0].shape[1]
    n = len(texts)
    grad = jax.ShapeDtypeStruct((rows, cols), BF16)
    yb = jax.ShapeDtypeStruct((rows, d), BF16)
    stats = jax.ShapeDtypeStruct((3, 8, 128), F32)
    xb = jax.ShapeDtypeStruct((cols, d), BF16)
    prods = pltpu.VMEM((2, rows, 256), F32)
    g, y, part, x = pl.pallas_call(
        functools.partial(tile_first_kernel, cuts),
        out_shape=(grad, yb, stats, xb),
        in_specs=[SMEM, VMEM, VMEM] + [ANY] * (1 + n),
        out_specs=(VMEM,) * 4,
        scratch_shapes=[prods, pltpu.SemaphoreType.DMA((1 + n,))],
        name="tile_first",
        cost_estimate=pl.CostEstimate(
            flops=2 * rows * 256 * d, bytes_accessed=4 * rows * d, transcendentals=3 * rows * 256
        ),
        compiler_params=BIG,
    )(coef, image_ids, text_ids, images[0], *texts)
    n = len(images) - 1
    g, part, x = pl.pallas_call(
        functools.partial(tile_rest_kernel, n),
        out_shape=(grad, stats, xb),
        in_specs=[SMEM] + [VMEM] * 4 + [ANY] * n + [VMEM] * 2,
        out_specs=(VMEM,) * 3,
        scratch_shapes=[prods, pltpu.SemaphoreType.DMA((n,))],
        input_output_aliases={5 + n: 0, 6 + n: 2},
        name="tile_rest",
        cost_estimate=pl.CostEstimate(
            flops=2 * rows * cols * d, bytes_accessed=4 * cols * d, transcendentals=3 * rows * cols
        ),
        compiler_params=BIG,
    )(coef, image_ids, text_ids, part, y, *images[1:], g, x)
    return g, y, part, x


def tile_late(coef, image_ids, text_ids, before, xb, texts, cuts):
    cols, rows = image_ids.shape[1], text_ids.shape[0]
    d = xb.shape[1]
    n = len(texts)
    return pl.pallas_call(
        functools.partial(tile_late_kernel, cuts),
        out_shape=(
            jax.ShapeDtypeStruct((rows, cols), BF16),
            jax.ShapeDtypeStruct((rows, d), BF16),
            jax.ShapeDtypeStruct((3, 128), F32),
        ),
        in_specs=[SMEM] + [VMEM] * 4 + [ANY] * n,
        out_specs=(VMEM,) * 3,
        scratch_shapes=[pltpu.VMEM((2, rows, 256), F32), pltpu.SemaphoreType.DMA((n,))],
        name="tile_late",
        cost_estimate=pl.CostEstimate(
            flops=2 * rows * cols * d, bytes_accessed=4 * cols * d, transcendentals=3 * rows * cols
        ),
        compiler_params=BIG,
    )(coef, image_ids, text_ids, before, xb, *texts)


def text_side_kernel(lower, ge, gl, xb, *refs):
    out, at = refs[-1], 0
    for g in (ge, gl):
        half = g.shape[0] // 2
        first = half if lower else 0
        out[at : at + half] = jnp.dot(
            g[first : first + half], xb[...], preferred_element_type=F32
        )
        at += half


def text_side(grads, xb, lower, after=()):
    rows = sum(g.shape[0] for g in grads) // 2
    d = xb.shape[1]
    return pl.pallas_call(
        functools.partial(text_side_kernel, lower),
        out_shape=jax.ShapeDtypeStruct((rows, d), F32),
        in_specs=[VMEM] * 3 + [ANY] * len(after),
        out_specs=VMEM,
        name="text_side",
        compiler_params=BIG,
    )(*grads, xb, *after)


def image_side_kernel(blocks, with_stats, ge, gl, ye, yl, *refs):
    outs = refs[len(refs) - len(blocks) :]
    if with_stats:
        outs, sums = refs[len(refs) - len(blocks) - 1 : -1], refs[-1]
        sums[...] = refs[0][...] + refs[1][...]
    rows = outs[0].shape[0]
    for i, out in zip(blocks, outs):
        at = slice(i * rows, (i + 1) * rows)
        out[...] = (dot_a(ge[:, at], ye[...]) + dot_a(gl[:, at], yl[...])).astype(out.dtype)


def image_side(grads, texts, blocks, stats=(), after=()):
    d, cols = texts[0].shape[1], grads[0].shape[1]
    size = cols // 4
    return pl.pallas_call(
        functools.partial(image_side_kernel, blocks, bool(stats)),
        out_shape=tuple(jax.ShapeDtypeStruct((size, d), BF16 if i else F32) for i in blocks)
        + tuple(jax.ShapeDtypeStruct(s.shape, F32) for s in stats[:1]),
        in_specs=[VMEM] * (4 + len(stats)) + [ANY] * len(after),
        out_specs=(VMEM,) * (len(blocks) + len(stats[:1])),
        name="image_side",
        compiler_params=BIG,
    )(*grads, *texts, *stats, *after)


def total_four(own, parts):
    return (own + parts[1]) + (parts[0] + parts[2])


def image_add_kernel(own, a, b, c, stats, other, keep, out1, out2, out3, total):
    rows = keep.shape[0]
    v = stats[...] + other[...]
    total[...] = v
    sums = [v[i : i + 1, :1] for i in range(3)]
    for i, out in enumerate((keep, out1, out2, out3)):
        at = pl.ds(i * rows, rows)
        out[pl.ds(0, rows)] = (
            own[at] + a[at].astype(F32) + b[at].astype(F32) + c[at].astype(F32)
        ).astype(out.dtype)
        if i:
            put_stats(sums, out.at[pl.ds(rows, STAT_ROWS)], out.shape[1])


def image_add(own, parts, stats, other):
    rows, d = own.shape[0] // 4, own.shape[1]
    sent = jax.ShapeDtypeStruct((rows + STAT_ROWS, d), BF16)
    return pl.pallas_call(
        image_add_kernel,
        out_shape=(jax.ShapeDtypeStruct((rows, d), F32), sent, sent, sent)
        + (jax.ShapeDtypeStruct(stats.shape, F32),),
        in_specs=[VMEM] * 6,
        out_specs=(VMEM,) * 5,
        name="image_add",
        compiler_params=SMALL,
    )(own, *parts, stats, other)


def text_add_kernel(runs, own, other, stats, came, *refs):
    outs, sums = refs[len(refs) - len(runs) - 1 : -1], refs[-1]
    for (at_own, at_other, rows, _), out in zip(runs, outs):
        out[...] = (own[pl.ds(at_own, rows)] + other[pl.ds(at_other, rows)]).astype(out.dtype)
    sums[...] = stats[...] + came[...]


def text_add(own, other, runs, stats, came, after):
    d = own.shape[1]
    return pl.pallas_call(
        functools.partial(text_add_kernel, runs),
        out_shape=tuple(jax.ShapeDtypeStruct((rows, d), t) for _, _, rows, t in runs)
        + (jax.ShapeDtypeStruct(stats.shape, F32),),
        in_specs=[VMEM] * 4 + [ANY] * len(after),
        out_specs=(VMEM,) * (len(runs) + 1),
        name="text_add",
        compiler_params=SMALL,
    )(own, other, stats, came, *after)


def step_add_kernel(with_stats, a, b, *refs):
    out = refs[-2] if with_stats else refs[-1]
    came = b.shape[0]
    out[0:came] = (a[0:came] + b[...].astype(F32)).astype(out.dtype)
    if came < a.shape[0]:
        out[came:] = a[came:].astype(out.dtype)
    if with_stats:
        refs[-1][...] = refs[0][...] + refs[1][...]


def step_add(a, b, stats, after, dtype=BF16):
    return pl.pallas_call(
        functools.partial(step_add_kernel, bool(stats)),
        out_shape=(jax.ShapeDtypeStruct(a.shape, dtype),)
        + tuple(jax.ShapeDtypeStruct(s.shape, F32) for s in stats[:1]),
        in_specs=[VMEM] * (2 + len(stats)) + [ANY] * len(after),
        out_specs=(VMEM,) * (1 + len(stats[:1])),
        name="step_add",
        compiler_params=SMALL,
    )(a, b, *stats, *after)


def lower_kernel(a, *refs):
    refs[-1][...] = a[pl.ds(a.shape[0] // 2, a.shape[0] // 2)]


def lower(a, after):
    return pl.pallas_call(
        lower_kernel,
        out_shape=jax.ShapeDtypeStruct((a.shape[0] // 2, a.shape[1]), a.dtype),
        in_specs=[VMEM, ANY],
        out_specs=VMEM,
        name="lower",
        compiler_params=SMALL,
    )(a, after)


def finish_kernel(starts, scale, *refs):
    refs = list(refs)
    outs, mark = refs[-3:-1], refs[-1]
    mark[...] = jnp.zeros(mark.shape, F32)
    for at_list, out in zip(starts, outs):
        raw = refs.pop(0)
        parts = [refs.pop(0) for _ in at_list]
        rows = raw[...].astype(F32)
        inv = inverse_norm(rows)
        unit = rows * inv
        owned = raw.shape[0]
        g = scale[0] * sum(p[pl.ds(at, owned)].astype(F32) for p, at in zip(parts, at_list))
        out[...] = (inv * (g - unit * jnp.sum(unit * g, axis=1, keepdims=True))).astype(BF16)


def finish(scale, *sides):
    starts = [tuple(at for _, at in parts) for _, parts in sides]
    refs = [r for raw, parts in sides for r in [raw] + [p for p, _ in parts]]
    return pl.pallas_call(
        functools.partial(finish_kernel, starts),
        out_shape=tuple(jax.ShapeDtypeStruct(raw.shape, BF16) for raw, _ in sides)
        + (jax.ShapeDtypeStruct((8, 128), F32),),
        in_specs=[SMEM] + [VMEM] * len(refs),
        out_specs=(VMEM,) * (len(sides) + 1),
        name="finish",
        compiler_params=SMALL,
    )(scale, *refs)


def stats_kernel(mine, a, b, c, out):
    tail = pl.ds(a.shape[0] - STAT_ROWS, STAT_ROWS)
    out[...] = total_four(mine[...], [get_stats(p.at[tail])[:, :128] for p in (a, b, c)])


def stats_sum(mine, parts):
    return pl.pallas_call(
        stats_kernel,
        out_shape=jax.ShapeDtypeStruct((3, 128), F32),
        in_specs=[VMEM] * 4,
        out_specs=VMEM,
        name="stats_sum",
        compiler_params=SMALL,
    )(mine, *parts)


def scalars_kernel(batch, scale, a, b, after, out):
    v = (a[...] + b[...]) * (1.0 / batch)
    for i, factor in enumerate((1 / LOG2E, scale[0], 1.0)):
        out[i] = jnp.max(v[i : i + 1]) * factor


def scalars(scale, a, b, batch, after):
    return pl.pallas_call(
        functools.partial(scalars_kernel, batch),
        out_shape=jax.ShapeDtypeStruct((3,), F32),
        in_specs=[SMEM] + [VMEM] * 2 + [ANY],
        out_specs=SMEM,
        name="scalars",
        compiler_params=SMALL,
    )(scale, a, b, after)


def labels(image_ids, text_ids, x, y, z, c, owned):
    split = (NY, 2, NX, NZ // 2, NC, owned)
    img = image_ids.reshape(split)[:, z % 2, :, z // 2, c].reshape(NY * NX, owned)
    txt = text_ids.reshape(split)[y, :, x].transpose(1, 0, 2, 3).reshape(NZ * NC, owned)
    first, second = jnp.where(c, y, x), jnp.where(c, x, y)
    at = []
    for j in range(4):
        for k in range(4):
            f, s = (first - k) % 4, (second - j) % 4
            at.append(jnp.where(c, f * NX + s, s * NX + f))
    img = img[jnp.stack(at)].reshape(1, -1)
    up = 1 - 2 * c
    sides = ((c, up), (1 - c, -up))
    at = []
    for core, sign in sides:
        order = [(0, core), (1, core), (1, 1 - core)]
        at += [(z - sign * k) % NZ * NC + d for k, d in order]
    for core, sign in sides:
        order = [(k, d) for k in (2, 3) for d in (core, 1 - core)]
        order.insert(4 if core is c else 0, (4, core))
        at += [(z - sign * k) % NZ * NC + d for k, d in order]
    txt = txt[jnp.stack(at)].reshape(-1, 1)
    return img, txt


def shards(images, texts, image_ids, text_ids, temp_log, bias):
    owned = images.shape[0]
    batch_all = owned * NX * NY * NZ * NC
    row, col = lax.axis_index("row"), lax.axis_index("col")
    x, y, z, c = row % NX, row // (2 * NX), 2 * (col // NC) + row // NX % 2, col % NC
    scale = jnp.exp(temp_log)
    coef = jnp.concatenate([scale, bias])
    img_ids, txt_ids = labels(image_ids, text_ids, x, y, z, c, owned)

    yn = normalize(texts)
    xn = normalize(images, [yn])
    sibling = hop_core(yn)
    line = [hop_first(xn, k) for k in (1, 2, 3)]
    near = join([xn] + line)
    ring = [join([yn, sibling])]
    ring.append(join([hop_z(ring[0], 1)], [near]))
    for _ in range(3):
        ring.append(hop_z(ring[-1], 1))
    image_blocks = [near] + [hop_second(near, k) for k in (1, 2, 3)]
    two = 2 * owned
    early = [yn, ring[1], sibling, hop_core(ring[1])]
    late = [ring[2], ring[3], ring[4], hop_core(ring[2]), hop_core(ring[3])]
    early_cuts = ((0, owned), (0, two), (0, owned), (0, two))
    late_cuts = ((0, two),) * 5

    cut = 6 * owned
    g_early, t_early, part, xb = tile_early(
        coef, img_ids, txt_ids[:cut], image_blocks, early, early_cuts
    )
    g_late, t_late, stats = tile_late(
        coef, img_ids, txt_ids[cut:], part, xb, late, late_cuts
    )
    grads, rows = [g_early, g_late], [t_early, t_late]

    send = text_side(grads, xb, True)
    keep = text_side(grads, xb, False, [send])
    sent1, sent3, stats = image_side(
        grads, rows, (1, 3), [stats, exchange(stats, 6, 3)], [keep]
    )
    (sent2,) = image_side(grads, rows, (2,), (), [sent1])
    runs = (
        (0, 0, owned, F32),
        (owned, owned, 2 * owned, F32),
        (3 * owned, 4 * owned, 2 * owned, F32),
        (5 * owned, 6 * owned, 2 * owned, F32),
        (7 * owned, 3 * owned, owned, BF16),
    )
    gy, gy1, gy2, gy3, far, stats = text_add(
        keep, hop_core(send), runs, stats, exchange(stats, 5, 5), [sent2]
    )
    parts = [hop_second(g, -k) for k, g in zip((1, 2, 3), (sent1, sent2, sent3))]
    step, stats = step_add(gy3, hop_z(far, -1), [stats, exchange(stats, 1, 1)], [])
    (own,) = image_side(grads, rows, (0,), (), [step])
    step, stats = step_add(gy2, hop_z(step, -1), [stats, exchange(stats, 2, 2)], [own])
    keep, g1, g2, g3, stats = image_add(own, parts, stats, exchange(stats, 7, 4))
    (step,) = step_add(gy1, hop_z(step, -1), [], [keep])
    around = hop_z(step, -1)
    parts = [hop_first(g, -k) for k, g in ((1, g1), (2, g2), (3, g3))]
    text_parts = [(gy, 0), (around, 0), (hop_core(lower(around, parts[2])), 0)]

    stats = stats_sum(stats, parts)
    image_grad, text_grad, mark = finish(
        scale, (images, [(p, 0) for p in [keep] + parts]), (texts, text_parts)
    )
    total = scalars(scale, stats, exchange(stats, 0, 0), batch_all, mark)
    return image_grad, text_grad, total


def solution(mesh):
    spread = P(("row", "col"), None)
    return jax.shard_map(
        shards,
        mesh=mesh,
        in_specs=(spread, spread, P(), P(), P(), P()),
        out_specs=(spread, spread, P()),
        check_vma=False,
    )
```

```python
import functools
import itertools
import jax
import jax.numpy as jnp
from jax import lax
from jax.experimental import pallas as pl
from jax.experimental.pallas import tpu as pltpu
from jax.sharding import PartitionSpec as P

NX, NY, NZ, NC = 4, 4, 8, 2
LOG2E = 1.4426950408889634
F32, BF16 = jnp.float32, jnp.bfloat16
ANY = pl.BlockSpec(memory_space=pl.ANY)
STAT_ROWS = 16
VMEM = pl.BlockSpec(memory_space=pltpu.VMEM)
SMEM = pl.BlockSpec(memory_space=pltpu.SMEM)
BIG = pltpu.CompilerParams(vmem_limit_bytes=24 * 2**20)
SMALL = pltpu.CompilerParams(vmem_limit_bytes=12 * 2**20)


def linear(x, y, z, c):
    return (((y * 2 + z % 2) * NX + x) * (NZ // 2) + z // 2) * NC + c


def hop(a, move):
    pairs = []
    for x, y, z, c in itertools.product(range(NX), range(NY), range(NZ), range(NC)):
        dx, dy, dz, dc = move(c)
        to = linear((x + dx) % NX, (y + dy) % NY, (z + dz) % NZ, (c + dc) % NC)
        pairs.append((linear(x, y, z, c), to))
    return lax.ppermute(a, ("row", "col"), pairs)


def hop_first(a, k):
    return hop(a, lambda c: (0, k, 0, 0) if c else (k, 0, 0, 0))


def hop_second(a, k):
    return hop(a, lambda c: (k, 0, 0, 0) if c else (0, k, 0, 0))


def hop_z(a, k):
    return hop(a, lambda c: (0, 0, -k if c else k, 0))


def hop_core(a):
    return hop(a, lambda c: (0, 0, 0, 1))


def exchange(a, bit0, bit1):
    pairs = [(i, i ^ (1 << (bit1 if i % 2 else bit0))) for i in range(256)]
    return lax.ppermute(a, ("row", "col"), pairs)


def dot_t(a, b):
    return lax.dot_general(a, b, (((1,), (1,)), ((), ())), preferred_element_type=F32)


def dot_a(a, b):
    return lax.dot_general(a, b, (((0,), (0,)), ((), ())), preferred_element_type=F32)


def inverse_norm(rows):
    return lax.rsqrt(jnp.sum(rows * rows, axis=1, keepdims=True) + 1e-06)


def norm_kernel(raw, *refs):
    rows = raw[...].astype(F32)
    refs[-1][...] = (rows * inverse_norm(rows)).astype(BF16)


def normalize(raw, after=()):
    return pl.pallas_call(
        norm_kernel,
        out_shape=jax.ShapeDtypeStruct(raw.shape, BF16),
        in_specs=[VMEM] + [ANY] * len(after),
        out_specs=VMEM,
        name="normalize",
        compiler_params=SMALL,
    )(raw, *after)


def join_kernel(n, *refs):
    out, at = refs[-1], 0
    for part in refs[:n]:
        rows = part.shape[0]
        out[at : at + rows] = part[...]
        at += rows


def join(parts, after=()):
    rows = sum(p.shape[0] for p in parts)
    return pl.pallas_call(
        functools.partial(join_kernel, len(parts)),
        out_shape=jax.ShapeDtypeStruct((rows, parts[0].shape[1]), parts[0].dtype),
        in_specs=[VMEM] * len(parts) + [ANY] * len(after),
        out_specs=VMEM,
        name="join",
        compiler_params=SMALL,
    )(*parts, *after)


def load(refs, dst, sem, first, at=0, cuts=None):
    out = []
    for i, ref in enumerate(refs):
        start, rows = cuts[i] if cuts else (0, ref.shape[0])
        src = ref.at[pl.ds(start, rows)]
        copy = pltpu.make_async_copy(src, dst.at[pl.ds(at, rows)], sem.at[first + i])
        copy.start()
        out.append((at, copy))
        at += rows
    return out


def fold(v):
    u = jnp.sum(v.reshape(v.shape[0] // 8, 8, v.shape[1]), axis=0)
    return sum(u[:, k : k + 128] for k in range(0, u.shape[1], 128))


def put_stats(sums, rows, width):
    row = lax.broadcasted_iota(jnp.int32, (STAT_ROWS, width), 0)
    v = jnp.where(row % 3 == 0, sums[0], jnp.where(row % 3 == 1, sums[1], sums[2]))
    high = v.astype(BF16).astype(F32)
    mid = (v - high).astype(BF16).astype(F32)
    low = v - high - mid
    v = jnp.where(row < 3, high, jnp.where(row < 6, mid, low))
    rows[...] = jnp.where(row < 9, v, 0.0).astype(BF16)


def get_stats(rows):
    v = rows[...].astype(F32)
    return (v[0:3] + v[3:6]) + v[6:9]


def tile_steps(coef, image_ids, text_ids, before, xb, yb, grad, prods, steps, coming):
    rows = yb.shape[0]
    wide = 256
    scale, shift = coef[0] * LOG2E, coef[1] * LOG2E
    acc = [jnp.zeros((8, 128), F32)] * 3 if before is None else [before[i] for i in range(3)]

    def multiply(k):
        while coming and coming[0][0] < (k + 1) * wide:
            coming.pop(0)[1].wait()
        prods[k % 2] = dot_t(yb[...], xb[k * wide : (k + 1) * wide])

    multiply(steps[0])
    for k in steps:
        if k + 1 in steps:
            multiply(k + 1)
        dots = prods[k % 2]
        match = text_ids[:, :1] == image_ids[:1, k * wide : (k + 1) * wide]
        logits = dots * scale + shift
        e = jnp.exp2(jnp.where(match, -logits, logits))
        p = 1.0 + e
        s = e / p
        g = jnp.where(match, -s, s)
        grad[:, k * wide : (k + 1) * wide] = g.astype(BF16)
        acc[0] += fold(jnp.log2(p[: rows // 2] * p[rows // 2 :]))
        acc[1] += fold(g * dots)
        acc[2] += fold(g)
    while coming:
        coming.pop(0)[1].wait()
    return acc


def tile_first_kernel(cuts, coef, image_ids, text_ids, near, *refs):
    texts, (grad, yb, stats, xb, prods, sem) = refs[: len(cuts)], refs[len(cuts) :]
    coming = load(texts, yb, sem, 0, 0, cuts) + load([near], xb, sem, len(cuts))
    for _, copy in coming:
        copy.wait()
    acc = tile_steps(coef, image_ids, text_ids, None, xb, yb, grad, prods, [0], [])
    for i in range(3):
        stats[i] = acc[i]


def tile_rest_kernel(n, coef, image_ids, text_ids, before, yb, *refs):
    blocks, (grad, stats, xb, prods, sem) = refs[:n], refs[n + 2 :]
    coming = load(blocks, xb, sem, 0, xb.shape[0] - n * blocks[0].shape[0])
    steps = range(1, xb.shape[0] // 256)
    acc = tile_steps(coef, image_ids, text_ids, before, xb, yb, grad, prods, steps, coming)
    for i in range(3):
        stats[i] = acc[i]


def tile_late_kernel(cuts, coef, image_ids, text_ids, before, xb, *refs):
    texts, (grad, yb, stats, prods, sem) = refs[: len(cuts)], refs[len(cuts) :]
    for _, copy in load(texts, yb, sem, 0, 0, cuts):
        copy.wait()
    steps = range(xb.shape[0] // 256)
    acc = tile_steps(coef, image_ids, text_ids, before, xb, yb, grad, prods, steps, [])
    for i in range(3):
        stats[pl.ds(i, 1)] = jnp.full((1, 128), jnp.sum(acc[i]))


def tile_early(coef, image_ids, text_ids, images, texts, cuts):
    cols, rows = image_ids.shape[1], text_ids.shape[0]
    d = images[0].shape[1]
    n = len(texts)
    grad = jax.ShapeDtypeStruct((rows, cols), BF16)
    yb = jax.ShapeDtypeStruct((rows, d), BF16)
    stats = jax.ShapeDtypeStruct((3, 8, 128), F32)
    xb = jax.ShapeDtypeStruct((cols, d), BF16)
    prods = pltpu.VMEM((2, rows, 256), F32)
    g, y, part, x = pl.pallas_call(
        functools.partial(tile_first_kernel, cuts),
        out_shape=(grad, yb, stats, xb),
        in_specs=[SMEM, VMEM, VMEM] + [ANY] * (1 + n),
        out_specs=(VMEM,) * 4,
        scratch_shapes=[prods, pltpu.SemaphoreType.DMA((1 + n,))],
        name="tile_first",
        cost_estimate=pl.CostEstimate(
            flops=2 * rows * 256 * d, bytes_accessed=4 * rows * d, transcendentals=3 * rows * 256
        ),
        compiler_params=BIG,
    )(coef, image_ids, text_ids, images[0], *texts)
    n = len(images) - 1
    g, part, x = pl.pallas_call(
        functools.partial(tile_rest_kernel, n),
        out_shape=(grad, stats, xb),
        in_specs=[SMEM] + [VMEM] * 4 + [ANY] * n + [VMEM] * 2,
        out_specs=(VMEM,) * 3,
        scratch_shapes=[prods, pltpu.SemaphoreType.DMA((n,))],
        input_output_aliases={5 + n: 0, 6 + n: 2},
        name="tile_rest",
        cost_estimate=pl.CostEstimate(
            flops=2 * rows * cols * d, bytes_accessed=4 * cols * d, transcendentals=3 * rows * cols
        ),
        compiler_params=BIG,
    )(coef, image_ids, text_ids, part, y, *images[1:], g, x)
    return g, y, part, x


def tile_late(coef, image_ids, text_ids, before, xb, texts, cuts):
    cols, rows = image_ids.shape[1], text_ids.shape[0]
    d = xb.shape[1]
    n = len(texts)
    return pl.pallas_call(
        functools.partial(tile_late_kernel, cuts),
        out_shape=(
            jax.ShapeDtypeStruct((rows, cols), BF16),
            jax.ShapeDtypeStruct((rows, d), BF16),
            jax.ShapeDtypeStruct((3, 128), F32),
        ),
        in_specs=[SMEM] + [VMEM] * 4 + [ANY] * n,
        out_specs=(VMEM,) * 3,
        scratch_shapes=[pltpu.VMEM((2, rows, 256), F32), pltpu.SemaphoreType.DMA((n,))],
        name="tile_late",
        cost_estimate=pl.CostEstimate(
            flops=2 * rows * cols * d, bytes_accessed=4 * cols * d, transcendentals=3 * rows * cols
        ),
        compiler_params=BIG,
    )(coef, image_ids, text_ids, before, xb, *texts)


def text_side_kernel(lower, ge, gl, xb, *refs):
    out, at = refs[-1], 0
    for g in (ge, gl):
        half = g.shape[0] // 2
        first = half if lower else 0
        out[at : at + half] = jnp.dot(
            g[first : first + half], xb[...], preferred_element_type=F32
        )
        at += half


def text_side(grads, xb, lower, after=()):
    rows = sum(g.shape[0] for g in grads) // 2
    d = xb.shape[1]
    return pl.pallas_call(
        functools.partial(text_side_kernel, lower),
        out_shape=jax.ShapeDtypeStruct((rows, d), F32),
        in_specs=[VMEM] * 3 + [ANY] * len(after),
        out_specs=VMEM,
        name="text_side",
        compiler_params=BIG,
    )(*grads, xb, *after)


def image_side_kernel(blocks, with_stats, ge, gl, ye, yl, *refs):
    outs = refs[len(refs) - len(blocks) :]
    if with_stats:
        outs, sums = refs[len(refs) - len(blocks) - 1 : -1], refs[-1]
        sums[...] = refs[0][...] + refs[1][...]
    rows = outs[0].shape[0]
    for i, out in zip(blocks, outs):
        at = slice(i * rows, (i + 1) * rows)
        out[...] = (dot_a(ge[:, at], ye[...]) + dot_a(gl[:, at], yl[...])).astype(out.dtype)


def image_side(grads, texts, blocks, stats=(), after=()):
    d, cols = texts[0].shape[1], grads[0].shape[1]
    size = cols // 4
    return pl.pallas_call(
        functools.partial(image_side_kernel, blocks, bool(stats)),
        out_shape=tuple(jax.ShapeDtypeStruct((size, d), BF16 if i else F32) for i in blocks)
        + tuple(jax.ShapeDtypeStruct(s.shape, F32) for s in stats[:1]),
        in_specs=[VMEM] * (4 + len(stats)) + [ANY] * len(after),
        out_specs=(VMEM,) * (len(blocks) + len(stats[:1])),
        name="image_side",
        compiler_params=BIG,
    )(*grads, *texts, *stats, *after)


def total_four(own, parts):
    return (own + parts[1]) + (parts[0] + parts[2])


def image_add_kernel(own, a, b, c, stats, other, keep, out1, out2, out3, total):
    rows = keep.shape[0]
    v = stats[...] + other[...]
    total[...] = v
    sums = [v[i : i + 1, :1] for i in range(3)]
    for i, out in enumerate((keep, out1, out2, out3)):
        at = pl.ds(i * rows, rows)
        out[pl.ds(0, rows)] = (
            own[at] + a[at].astype(F32) + b[at].astype(F32) + c[at].astype(F32)
        ).astype(out.dtype)
        if i:
            put_stats(sums, out.at[pl.ds(rows, STAT_ROWS)], out.shape[1])


def image_add(own, parts, stats, other):
    rows, d = own.shape[0] // 4, own.shape[1]
    sent = jax.ShapeDtypeStruct((rows + STAT_ROWS, d), BF16)
    return pl.pallas_call(
        image_add_kernel,
        out_shape=(jax.ShapeDtypeStruct((rows, d), F32), sent, sent, sent)
        + (jax.ShapeDtypeStruct(stats.shape, F32),),
        in_specs=[VMEM] * 6,
        out_specs=(VMEM,) * 5,
        name="image_add",
        compiler_params=SMALL,
    )(own, *parts, stats, other)


def text_add_kernel(runs, own, other, stats, came, *refs):
    outs, sums = refs[len(refs) - len(runs) - 1 : -1], refs[-1]
    for (at_own, at_other, rows, _), out in zip(runs, outs):
        out[...] = (own[pl.ds(at_own, rows)] + other[pl.ds(at_other, rows)]).astype(out.dtype)
    sums[...] = stats[...] + came[...]


def text_add(own, other, runs, stats, came, after):
    d = own.shape[1]
    return pl.pallas_call(
        functools.partial(text_add_kernel, runs),
        out_shape=tuple(jax.ShapeDtypeStruct((rows, d), t) for _, _, rows, t in runs)
        + (jax.ShapeDtypeStruct(stats.shape, F32),),
        in_specs=[VMEM] * 4 + [ANY] * len(after),
        out_specs=(VMEM,) * (len(runs) + 1),
        name="text_add",
        compiler_params=SMALL,
    )(own, other, stats, came, *after)


def step_add_kernel(with_stats, a, b, *refs):
    out = refs[-2] if with_stats else refs[-1]
    came = b.shape[0]
    out[0:came] = (a[0:came] + b[...].astype(F32)).astype(out.dtype)
    if came < a.shape[0]:
        out[came:] = a[came:].astype(out.dtype)
    if with_stats:
        refs[-1][...] = refs[0][...] + refs[1][...]


def step_add(a, b, stats, after, dtype=BF16):
    return pl.pallas_call(
        functools.partial(step_add_kernel, bool(stats)),
        out_shape=(jax.ShapeDtypeStruct(a.shape, dtype),)
        + tuple(jax.ShapeDtypeStruct(s.shape, F32) for s in stats[:1]),
        in_specs=[VMEM] * (2 + len(stats)) + [ANY] * len(after),
        out_specs=(VMEM,) * (1 + len(stats[:1])),
        name="step_add",
        compiler_params=SMALL,
    )(a, b, *stats, *after)


def lower_kernel(a, *refs):
    refs[-1][...] = a[pl.ds(a.shape[0] // 2, a.shape[0] // 2)]


def lower(a, after):
    return pl.pallas_call(
        lower_kernel,
        out_shape=jax.ShapeDtypeStruct((a.shape[0] // 2, a.shape[1]), a.dtype),
        in_specs=[VMEM, ANY],
        out_specs=VMEM,
        name="lower",
        compiler_params=SMALL,
    )(a, after)


def finish_kernel(starts, scale, *refs):
    refs = list(refs)
    outs, mark = refs[-3:-1], refs[-1]
    mark[...] = jnp.zeros(mark.shape, F32)
    for at_list, out in zip(starts, outs):
        raw = refs.pop(0)
        parts = [refs.pop(0) for _ in at_list]
        rows = raw[...].astype(F32)
        inv = inverse_norm(rows)
        unit = rows * inv
        owned = raw.shape[0]
        g = scale[0] * sum(p[pl.ds(at, owned)].astype(F32) for p, at in zip(parts, at_list))
        out[...] = (inv * (g - unit * jnp.sum(unit * g, axis=1, keepdims=True))).astype(BF16)


def finish(scale, *sides):
    starts = [tuple(at for _, at in parts) for _, parts in sides]
    refs = [r for raw, parts in sides for r in [raw] + [p for p, _ in parts]]
    return pl.pallas_call(
        functools.partial(finish_kernel, starts),
        out_shape=tuple(jax.ShapeDtypeStruct(raw.shape, BF16) for raw, _ in sides)
        + (jax.ShapeDtypeStruct((8, 128), F32),),
        in_specs=[SMEM] + [VMEM] * len(refs),
        out_specs=(VMEM,) * (len(sides) + 1),
        name="finish",
        compiler_params=SMALL,
    )(scale, *refs)


def stats_kernel(mine, a, b, c, out):
    tail = pl.ds(a.shape[0] - STAT_ROWS, STAT_ROWS)
    out[...] = total_four(mine[...], [get_stats(p.at[tail])[:, :128] for p in (a, b, c)])


def stats_sum(mine, parts):
    return pl.pallas_call(
        stats_kernel,
        out_shape=jax.ShapeDtypeStruct((3, 128), F32),
        in_specs=[VMEM] * 4,
        out_specs=VMEM,
        name="stats_sum",
        compiler_params=SMALL,
    )(mine, *parts)


def scalars_kernel(batch, scale, a, b, after, out):
    v = (a[...] + b[...]) * (1.0 / batch)
    for i, factor in enumerate((1 / LOG2E, scale[0], 1.0)):
        out[i] = jnp.max(v[i : i + 1]) * factor


def scalars(scale, a, b, batch, after):
    return pl.pallas_call(
        functools.partial(scalars_kernel, batch),
        out_shape=jax.ShapeDtypeStruct((3,), F32),
        in_specs=[SMEM] + [VMEM] * 2 + [ANY],
        out_specs=SMEM,
        name="scalars",
        compiler_params=SMALL,
    )(scale, a, b, after)


def labels(image_ids, text_ids, x, y, z, c, owned):
    split = (NY, 2, NX, NZ // 2, NC, owned)
    img = image_ids.reshape(split)[:, z % 2, :, z // 2, c].reshape(NY * NX, owned)
    txt = text_ids.reshape(split)[y, :, x].transpose(1, 0, 2, 3).reshape(NZ * NC, owned)
    first, second = jnp.where(c, y, x), jnp.where(c, x, y)
    at = []
    for j in range(4):
        for k in range(4):
            f, s = (first - k) % 4, (second - j) % 4
            at.append(jnp.where(c, f * NX + s, s * NX + f))
    img = img[jnp.stack(at)].reshape(1, -1)
    up = 1 - 2 * c
    sides = ((c, up), (1 - c, -up))
    at = []
    for core, sign in sides:
        order = [(0, core), (1, core), (1, 1 - core)]
        at += [(z - sign * k) % NZ * NC + d for k, d in order]
    for core, sign in sides:
        order = [(k, d) for k in (2, 3) for d in (core, 1 - core)]
        order.insert(4 if core is c else 0, (4, core))
        at += [(z - sign * k) % NZ * NC + d for k, d in order]
    txt = txt[jnp.stack(at)].reshape(-1, 1)
    return img, txt


def shards(images, texts, image_ids, text_ids, temp_log, bias):
    owned = images.shape[0]
    batch_all = owned * NX * NY * NZ * NC
    row, col = lax.axis_index("row"), lax.axis_index("col")
    x, y, z, c = row % NX, row // (2 * NX), 2 * (col // NC) + row // NX % 2, col % NC
    scale = jnp.exp(temp_log)
    coef = jnp.concatenate([scale, bias])
    img_ids, txt_ids = labels(image_ids, text_ids, x, y, z, c, owned)

    yn = normalize(texts)
    xn = normalize(images, [yn])
    sibling = hop_core(yn)
    line = [hop_first(xn, k) for k in (1, 2, 3)]
    near = join([xn] + line)
    ring = [join([yn, sibling])]
    ring.append(join([hop_z(ring[0], 1)], [near]))
    for _ in range(3):
        ring.append(hop_z(ring[-1], 1))
    image_blocks = [near] + [hop_second(near, k) for k in (1, 2, 3)]
    two = 2 * owned
    early = [yn, ring[1], sibling, hop_core(ring[1])]
    late = [ring[2], ring[3], ring[4], hop_core(ring[2]), hop_core(ring[3])]
    early_cuts = ((0, owned), (0, two), (0, owned), (0, two))
    late_cuts = ((0, two),) * 5

    cut = 6 * owned
    g_early, t_early, part, xb = tile_early(
        coef, img_ids, txt_ids[:cut], image_blocks, early, early_cuts
    )
    g_late, t_late, stats = tile_late(
        coef, img_ids, txt_ids[cut:], part, xb, late, late_cuts
    )
    grads, rows = [g_early, g_late], [t_early, t_late]

    send = text_side(grads, xb, True)
    keep = text_side(grads, xb, False, [send])
    sent1, sent3, stats = image_side(
        grads, rows, (1, 3), [stats, exchange(stats, 6, 3)], [keep]
    )
    (sent2,) = image_side(grads, rows, (2,), (), [sent1])
    runs = (
        (0, 0, owned, F32),
        (owned, owned, 2 * owned, F32),
        (3 * owned, 4 * owned, 2 * owned, F32),
        (5 * owned, 6 * owned, 2 * owned, F32),
        (7 * owned, 3 * owned, owned, BF16),
    )
    gy, gy1, gy2, gy3, far, stats = text_add(
        keep, hop_core(send), runs, stats, exchange(stats, 5, 5), [sent2]
    )
    parts = [hop_second(g, -k) for k, g in zip((1, 2, 3), (sent1, sent2, sent3))]
    step, stats = step_add(gy3, hop_z(far, -1), [stats, exchange(stats, 1, 1)], [])
    (own,) = image_side(grads, rows, (0,), (), [step])
    step, stats = step_add(gy2, hop_z(step, -1), [stats, exchange(stats, 2, 2)], [own, parts[0], parts[2]])
    keep, g1, g2, g3, stats = image_add(own, parts, stats, exchange(stats, 7, 4))
    (step,) = step_add(gy1, hop_z(step, -1), [], [keep])
    around = hop_z(step, -1)
    parts = [hop_first(g, -k) for k, g in ((1, g1), (2, g2), (3, g3))]
    text_parts = [(gy, 0), (around, 0), (hop_core(lower(around, parts[2])), 0)]

    stats = stats_sum(stats, parts)
    image_grad, text_grad, mark = finish(
        scale, (images, [(p, 0) for p in [keep] + parts]), (texts, text_parts)
    )
    total = scalars(scale, stats, exchange(stats, 0, 0), batch_all, mark)
    return image_grad, text_grad, total


def solution(mesh):
    spread = P(("row", "col"), None)
    return jax.shard_map(
        shards,
        mesh=mesh,
        in_specs=(spread, spread, P(), P(), P(), P()),
        out_specs=(spread, spread, P()),
        check_vma=False,
    )
```

```python
import functools
import itertools
import jax
import jax.numpy as jnp
from jax import lax
from jax.experimental import pallas as pl
from jax.experimental.pallas import tpu as pltpu
from jax.sharding import PartitionSpec as P

NX, NY, NZ, NC = 4, 4, 8, 2
LOG2E = 1.4426950408889634
F32, BF16 = jnp.float32, jnp.bfloat16
ANY = pl.BlockSpec(memory_space=pl.ANY)
STAT_ROWS = 16
VMEM = pl.BlockSpec(memory_space=pltpu.VMEM)
SMEM = pl.BlockSpec(memory_space=pltpu.SMEM)
BIG = pltpu.CompilerParams(vmem_limit_bytes=24 * 2**20)
SMALL = pltpu.CompilerParams(vmem_limit_bytes=12 * 2**20)


def linear(x, y, z, c):
    return (((y * 2 + z % 2) * NX + x) * (NZ // 2) + z // 2) * NC + c


def hop(a, move):
    pairs = []
    for x, y, z, c in itertools.product(range(NX), range(NY), range(NZ), range(NC)):
        dx, dy, dz, dc = move(c)
        to = linear((x + dx) % NX, (y + dy) % NY, (z + dz) % NZ, (c + dc) % NC)
        pairs.append((linear(x, y, z, c), to))
    return lax.ppermute(a, ("row", "col"), pairs)


def hop_first(a, k):
    return hop(a, lambda c: (0, k, 0, 0) if c else (k, 0, 0, 0))


def hop_second(a, k):
    return hop(a, lambda c: (k, 0, 0, 0) if c else (0, k, 0, 0))


def hop_z(a, k):
    return hop(a, lambda c: (0, 0, -k if c else k, 0))


def hop_core(a):
    return hop(a, lambda c: (0, 0, 0, 1))


def exchange(a, bit0, bit1):
    pairs = [(i, i ^ (1 << (bit1 if i % 2 else bit0))) for i in range(256)]
    return lax.ppermute(a, ("row", "col"), pairs)


def dot_t(a, b):
    return lax.dot_general(a, b, (((1,), (1,)), ((), ())), preferred_element_type=F32)


def dot_a(a, b):
    return lax.dot_general(a, b, (((0,), (0,)), ((), ())), preferred_element_type=F32)


def inverse_norm(rows):
    return lax.rsqrt(jnp.sum(rows * rows, axis=1, keepdims=True) + 1e-06)


def norm_kernel(raw, *refs):
    rows = raw[...].astype(F32)
    refs[-1][...] = (rows * inverse_norm(rows)).astype(BF16)


def normalize(raw, after=()):
    return pl.pallas_call(
        norm_kernel,
        out_shape=jax.ShapeDtypeStruct(raw.shape, BF16),
        in_specs=[VMEM] + [ANY] * len(after),
        out_specs=VMEM,
        name="normalize",
        compiler_params=SMALL,
    )(raw, *after)


def join_kernel(n, *refs):
    out, at = refs[-1], 0
    for part in refs[:n]:
        rows = part.shape[0]
        out[at : at + rows] = part[...]
        at += rows


def join(parts, after=()):
    rows = sum(p.shape[0] for p in parts)
    return pl.pallas_call(
        functools.partial(join_kernel, len(parts)),
        out_shape=jax.ShapeDtypeStruct((rows, parts[0].shape[1]), parts[0].dtype),
        in_specs=[VMEM] * len(parts) + [ANY] * len(after),
        out_specs=VMEM,
        name="join",
        compiler_params=SMALL,
    )(*parts, *after)


def load(refs, dst, sem, first, at=0, cuts=None):
    out = []
    for i, ref in enumerate(refs):
        start, rows = cuts[i] if cuts else (0, ref.shape[0])
        src = ref.at[pl.ds(start, rows)]
        copy = pltpu.make_async_copy(src, dst.at[pl.ds(at, rows)], sem.at[first + i])
        copy.start()
        out.append((at, copy))
        at += rows
    return out


def fold(v):
    u = jnp.sum(v.reshape(v.shape[0] // 8, 8, v.shape[1]), axis=0)
    return sum(u[:, k : k + 128] for k in range(0, u.shape[1], 128))


def put_stats(sums, rows, width):
    row = lax.broadcasted_iota(jnp.int32, (STAT_ROWS, width), 0)
    v = jnp.where(row % 3 == 0, sums[0], jnp.where(row % 3 == 1, sums[1], sums[2]))
    high = v.astype(BF16).astype(F32)
    mid = (v - high).astype(BF16).astype(F32)
    low = v - high - mid
    v = jnp.where(row < 3, high, jnp.where(row < 6, mid, low))
    rows[...] = jnp.where(row < 9, v, 0.0).astype(BF16)


def get_stats(rows):
    v = rows[...].astype(F32)
    return (v[0:3] + v[3:6]) + v[6:9]


def tile_steps(coef, image_ids, text_ids, before, xb, yb, grad, prods, steps, coming):
    rows = yb.shape[0]
    wide = 256
    scale, shift = coef[0] * LOG2E, coef[1] * LOG2E
    acc = [jnp.zeros((8, 128), F32)] * 3 if before is None else [before[i] for i in range(3)]

    def multiply(k):
        while coming and coming[0][0] < (k + 1) * wide:
            coming.pop(0)[1].wait()
        prods[k % 2] = dot_t(yb[...], xb[k * wide : (k + 1) * wide])

    multiply(steps[0])
    for k in steps:
        if k + 1 in steps:
            multiply(k + 1)
        dots = prods[k % 2]
        match = text_ids[:, :1] == image_ids[:1, k * wide : (k + 1) * wide]
        logits = dots * scale + shift
        e = jnp.exp2(jnp.where(match, -logits, logits))
        p = 1.0 + e
        s = e / p
        g = jnp.where(match, -s, s)
        grad[:, k * wide : (k + 1) * wide] = g.astype(BF16)
        acc[0] += fold(jnp.log2(p[: rows // 2] * p[rows // 2 :]))
        acc[1] += fold(g * dots)
        acc[2] += fold(g)
    while coming:
        coming.pop(0)[1].wait()
    return acc


def tile_first_kernel(cuts, coef, image_ids, text_ids, near, *refs):
    texts, (grad, yb, stats, xb, prods, sem) = refs[: len(cuts)], refs[len(cuts) :]
    coming = load(texts, yb, sem, 0, 0, cuts) + load([near], xb, sem, len(cuts))
    for _, copy in coming:
        copy.wait()
    acc = tile_steps(coef, image_ids, text_ids, None, xb, yb, grad, prods, [0], [])
    for i in range(3):
        stats[i] = acc[i]


def tile_rest_kernel(n, coef, image_ids, text_ids, before, yb, *refs):
    blocks, (grad, stats, xb, prods, sem) = refs[:n], refs[n + 2 :]
    coming = load(blocks, xb, sem, 0, xb.shape[0] - n * blocks[0].shape[0])
    steps = range(1, xb.shape[0] // 256)
    acc = tile_steps(coef, image_ids, text_ids, before, xb, yb, grad, prods, steps, coming)
    for i in range(3):
        stats[i] = acc[i]


def tile_late_kernel(cuts, coef, image_ids, text_ids, before, xb, *refs):
    texts, (grad, yb, stats, prods, sem) = refs[: len(cuts)], refs[len(cuts) :]
    for _, copy in load(texts, yb, sem, 0, 0, cuts):
        copy.wait()
    steps = range(xb.shape[0] // 256)
    acc = tile_steps(coef, image_ids, text_ids, before, xb, yb, grad, prods, steps, [])
    for i in range(3):
        stats[pl.ds(i, 1)] = jnp.full((1, 128), jnp.sum(acc[i]))


def tile_early(coef, image_ids, text_ids, images, texts, cuts):
    cols, rows = image_ids.shape[1], text_ids.shape[0]
    d = images[0].shape[1]
    n = len(texts)
    grad = jax.ShapeDtypeStruct((rows, cols), BF16)
    yb = jax.ShapeDtypeStruct((rows, d), BF16)
    stats = jax.ShapeDtypeStruct((3, 8, 128), F32)
    xb = jax.ShapeDtypeStruct((cols, d), BF16)
    prods = pltpu.VMEM((2, rows, 256), F32)
    g, y, part, x = pl.pallas_call(
        functools.partial(tile_first_kernel, cuts),
        out_shape=(grad, yb, stats, xb),
        in_specs=[SMEM, VMEM, VMEM] + [ANY] * (1 + n),
        out_specs=(VMEM,) * 4,
        scratch_shapes=[prods, pltpu.SemaphoreType.DMA((1 + n,))],
        name="tile_first",
        cost_estimate=pl.CostEstimate(
            flops=2 * rows * 256 * d, bytes_accessed=4 * rows * d, transcendentals=3 * rows * 256
        ),
        compiler_params=BIG,
    )(coef, image_ids, text_ids, images[0], *texts)
    n = len(images) - 1
    mark = part
    g, part, x = pl.pallas_call(
        functools.partial(tile_rest_kernel, n),
        out_shape=(grad, stats, xb),
        in_specs=[SMEM] + [VMEM] * 4 + [ANY] * n + [VMEM] * 2,
        out_specs=(VMEM,) * 3,
        scratch_shapes=[prods, pltpu.SemaphoreType.DMA((n,))],
        input_output_aliases={5 + n: 0, 6 + n: 2},
        name="tile_rest",
        cost_estimate=pl.CostEstimate(
            flops=2 * rows * cols * d, bytes_accessed=4 * cols * d, transcendentals=3 * rows * cols
        ),
        compiler_params=BIG,
    )(coef, image_ids, text_ids, part, y, *images[1:], g, x)
    return g, y, part, x, mark


def tile_late(coef, image_ids, text_ids, before, xb, texts, cuts):
    cols, rows = image_ids.shape[1], text_ids.shape[0]
    d = xb.shape[1]
    n = len(texts)
    return pl.pallas_call(
        functools.partial(tile_late_kernel, cuts),
        out_shape=(
            jax.ShapeDtypeStruct((rows, cols), BF16),
            jax.ShapeDtypeStruct((rows, d), BF16),
            jax.ShapeDtypeStruct((3, 128), F32),
        ),
        in_specs=[SMEM] + [VMEM] * 4 + [ANY] * n,
        out_specs=(VMEM,) * 3,
        scratch_shapes=[pltpu.VMEM((2, rows, 256), F32), pltpu.SemaphoreType.DMA((n,))],
        name="tile_late",
        cost_estimate=pl.CostEstimate(
            flops=2 * rows * cols * d, bytes_accessed=4 * cols * d, transcendentals=3 * rows * cols
        ),
        compiler_params=BIG,
    )(coef, image_ids, text_ids, before, xb, *texts)


def text_side_kernel(lower, ge, gl, xb, *refs):
    out, at = refs[-1], 0
    for g in (ge, gl):
        half = g.shape[0] // 2
        first = half if lower else 0
        out[at : at + half] = jnp.dot(
            g[first : first + half], xb[...], preferred_element_type=F32
        )
        at += half


def text_side(grads, xb, lower, after=()):
    rows = sum(g.shape[0] for g in grads) // 2
    d = xb.shape[1]
    return pl.pallas_call(
        functools.partial(text_side_kernel, lower),
        out_shape=jax.ShapeDtypeStruct((rows, d), F32),
        in_specs=[VMEM] * 3 + [ANY] * len(after),
        out_specs=VMEM,
        name="text_side",
        compiler_params=BIG,
    )(*grads, xb, *after)


def image_side_kernel(blocks, with_stats, ge, gl, ye, yl, *refs):
    outs = refs[len(refs) - len(blocks) :]
    if with_stats:
        outs, sums = refs[len(refs) - len(blocks) - 1 : -1], refs[-1]
        sums[...] = refs[0][...] + refs[1][...]
    rows = outs[0].shape[0]
    for i, out in zip(blocks, outs):
        at = slice(i * rows, (i + 1) * rows)
        out[...] = (dot_a(ge[:, at], ye[...]) + dot_a(gl[:, at], yl[...])).astype(out.dtype)


def image_side(grads, texts, blocks, stats=(), after=()):
    d, cols = texts[0].shape[1], grads[0].shape[1]
    size = cols // 4
    return pl.pallas_call(
        functools.partial(image_side_kernel, blocks, bool(stats)),
        out_shape=tuple(jax.ShapeDtypeStruct((size, d), BF16 if i else F32) for i in blocks)
        + tuple(jax.ShapeDtypeStruct(s.shape, F32) for s in stats[:1]),
        in_specs=[VMEM] * (4 + len(stats)) + [ANY] * len(after),
        out_specs=(VMEM,) * (len(blocks) + len(stats[:1])),
        name="image_side",
        compiler_params=BIG,
    )(*grads, *texts, *stats, *after)


def total_four(own, parts):
    return (own + parts[1]) + (parts[0] + parts[2])


def image_add_kernel(own, a, b, c, stats, other, keep, out1, out2, out3, total):
    rows = keep.shape[0]
    v = stats[...] + other[...]
    total[...] = v
    sums = [v[i : i + 1, :1] for i in range(3)]
    for i, out in enumerate((keep, out1, out2, out3)):
        at = pl.ds(i * rows, rows)
        out[pl.ds(0, rows)] = (
            own[at] + a[at].astype(F32) + b[at].astype(F32) + c[at].astype(F32)
        ).astype(out.dtype)
        if i:
            put_stats(sums, out.at[pl.ds(rows, STAT_ROWS)], out.shape[1])


def image_add(own, parts, stats, other):
    rows, d = own.shape[0] // 4, own.shape[1]
    sent = jax.ShapeDtypeStruct((rows + STAT_ROWS, d), BF16)
    return pl.pallas_call(
        image_add_kernel,
        out_shape=(jax.ShapeDtypeStruct((rows, d), F32), sent, sent, sent)
        + (jax.ShapeDtypeStruct(stats.shape, F32),),
        in_specs=[VMEM] * 6,
        out_specs=(VMEM,) * 5,
        name="image_add",
        compiler_params=SMALL,
    )(own, *parts, stats, other)


def text_add_kernel(runs, own, other, stats, came, *refs):
    outs, sums = refs[len(refs) - len(runs) - 1 : -1], refs[-1]
    for (at_own, at_other, rows, _), out in zip(runs, outs):
        out[...] = (own[pl.ds(at_own, rows)] + other[pl.ds(at_other, rows)]).astype(out.dtype)
    sums[...] = stats[...] + came[...]


def text_add(own, other, runs, stats, came, after):
    d = own.shape[1]
    return pl.pallas_call(
        functools.partial(text_add_kernel, runs),
        out_shape=tuple(jax.ShapeDtypeStruct((rows, d), t) for _, _, rows, t in runs)
        + (jax.ShapeDtypeStruct(stats.shape, F32),),
        in_specs=[VMEM] * 4 + [ANY] * len(after),
        out_specs=(VMEM,) * (len(runs) + 1),
        name="text_add",
        compiler_params=SMALL,
    )(own, other, stats, came, *after)


def step_add_kernel(with_stats, a, b, *refs):
    out = refs[-2] if with_stats else refs[-1]
    came = b.shape[0]
    out[0:came] = (a[0:came] + b[...].astype(F32)).astype(out.dtype)
    if came < a.shape[0]:
        out[came:] = a[came:].astype(out.dtype)
    if with_stats:
        refs[-1][...] = refs[0][...] + refs[1][...]


def step_add(a, b, stats, after, dtype=BF16):
    return pl.pallas_call(
        functools.partial(step_add_kernel, bool(stats)),
        out_shape=(jax.ShapeDtypeStruct(a.shape, dtype),)
        + tuple(jax.ShapeDtypeStruct(s.shape, F32) for s in stats[:1]),
        in_specs=[VMEM] * (2 + len(stats)) + [ANY] * len(after),
        out_specs=(VMEM,) * (1 + len(stats[:1])),
        name="step_add",
        compiler_params=SMALL,
    )(a, b, *stats, *after)


def lower_kernel(a, *refs):
    refs[-1][...] = a[pl.ds(a.shape[0] // 2, a.shape[0] // 2)]


def lower(a, after):
    return pl.pallas_call(
        lower_kernel,
        out_shape=jax.ShapeDtypeStruct((a.shape[0] // 2, a.shape[1]), a.dtype),
        in_specs=[VMEM, ANY],
        out_specs=VMEM,
        name="lower",
        compiler_params=SMALL,
    )(a, after)


def finish_kernel(starts, scale, *refs):
    refs = list(refs)
    outs, mark = refs[-3:-1], refs[-1]
    mark[...] = jnp.zeros(mark.shape, F32)
    for at_list, out in zip(starts, outs):
        raw = refs.pop(0)
        parts = [refs.pop(0) for _ in at_list]
        rows = raw[...].astype(F32)
        inv = inverse_norm(rows)
        unit = rows * inv
        owned = raw.shape[0]
        g = scale[0] * sum(p[pl.ds(at, owned)].astype(F32) for p, at in zip(parts, at_list))
        out[...] = (inv * (g - unit * jnp.sum(unit * g, axis=1, keepdims=True))).astype(BF16)


def finish(scale, *sides):
    starts = [tuple(at for _, at in parts) for _, parts in sides]
    refs = [r for raw, parts in sides for r in [raw] + [p for p, _ in parts]]
    return pl.pallas_call(
        functools.partial(finish_kernel, starts),
        out_shape=tuple(jax.ShapeDtypeStruct(raw.shape, BF16) for raw, _ in sides)
        + (jax.ShapeDtypeStruct((8, 128), F32),),
        in_specs=[SMEM] + [VMEM] * len(refs),
        out_specs=(VMEM,) * (len(sides) + 1),
        name="finish",
        compiler_params=SMALL,
    )(scale, *refs)


def stats_kernel(mine, a, b, c, out):
    tail = pl.ds(a.shape[0] - STAT_ROWS, STAT_ROWS)
    out[...] = total_four(mine[...], [get_stats(p.at[tail])[:, :128] for p in (a, b, c)])


def stats_sum(mine, parts):
    return pl.pallas_call(
        stats_kernel,
        out_shape=jax.ShapeDtypeStruct((3, 128), F32),
        in_specs=[VMEM] * 4,
        out_specs=VMEM,
        name="stats_sum",
        compiler_params=SMALL,
    )(mine, *parts)


def scalars_kernel(batch, scale, a, b, after, out):
    v = (a[...] + b[...]) * (1.0 / batch)
    for i, factor in enumerate((1 / LOG2E, scale[0], 1.0)):
        out[i] = jnp.max(v[i : i + 1]) * factor


def scalars(scale, a, b, batch, after):
    return pl.pallas_call(
        functools.partial(scalars_kernel, batch),
        out_shape=jax.ShapeDtypeStruct((3,), F32),
        in_specs=[SMEM] + [VMEM] * 2 + [ANY],
        out_specs=SMEM,
        name="scalars",
        compiler_params=SMALL,
    )(scale, a, b, after)


def labels(image_ids, text_ids, x, y, z, c, owned):
    split = (NY, 2, NX, NZ // 2, NC, owned)
    img = image_ids.reshape(split)[:, z % 2, :, z // 2, c].reshape(NY * NX, owned)
    txt = text_ids.reshape(split)[y, :, x].transpose(1, 0, 2, 3).reshape(NZ * NC, owned)
    first, second = jnp.where(c, y, x), jnp.where(c, x, y)
    at = []
    for j in range(4):
        for k in range(4):
            f, s = (first - k) % 4, (second - j) % 4
            at.append(jnp.where(c, f * NX + s, s * NX + f))
    img = img[jnp.stack(at)].reshape(1, -1)
    up = 1 - 2 * c
    sides = ((c, up), (1 - c, -up))
    at = []
    for core, sign in sides:
        order = [(0, core), (1, core), (1, 1 - core)]
        at += [(z - sign * k) % NZ * NC + d for k, d in order]
    for core, sign in sides:
        order = [(k, d) for k in (2, 3) for d in (core, 1 - core)]
        order.insert(4 if core is c else 0, (4, core))
        at += [(z - sign * k) % NZ * NC + d for k, d in order]
    txt = txt[jnp.stack(at)].reshape(-1, 1)
    return img, txt


def shards(images, texts, image_ids, text_ids, temp_log, bias):
    owned = images.shape[0]
    batch_all = owned * NX * NY * NZ * NC
    row, col = lax.axis_index("row"), lax.axis_index("col")
    x, y, z, c = row % NX, row // (2 * NX), 2 * (col // NC) + row // NX % 2, col % NC
    scale = jnp.exp(temp_log)
    coef = jnp.concatenate([scale, bias])
    img_ids, txt_ids = labels(image_ids, text_ids, x, y, z, c, owned)

    yn = normalize(texts)
    xn = normalize(images, [yn])
    sibling = hop_core(yn)
    line = [hop_first(xn, k) for k in (1, 2, 3)]
    near = join([xn] + line)
    ring = [join([yn, sibling])]
    ring.append(join([hop_z(ring[0], 1)], [near]))
    for _ in range(2):
        ring.append(hop_z(ring[-1], 1))
    image_blocks = [near] + [hop_second(near, k) for k in (1, 2, 3)]
    two = 2 * owned
    early = [yn, ring[1], sibling, hop_core(ring[1])]
    early_cuts = ((0, owned), (0, two), (0, owned), (0, two))
    late_cuts = ((0, two),) * 5

    cut = 6 * owned
    g_early, t_early, part, xb, mark = tile_early(
        coef, img_ids, txt_ids[:cut], image_blocks, early, early_cuts
    )
    ring.append(hop_z(join([ring[3]], [mark]), 1))
    late = [ring[2], ring[3], ring[4], hop_core(ring[2]), hop_core(ring[3])]
    g_late, t_late, stats = tile_late(
        coef, img_ids, txt_ids[cut:], part, xb, late, late_cuts
    )
    grads, rows = [g_early, g_late], [t_early, t_late]

    send = text_side(grads, xb, True)
    keep = text_side(grads, xb, False, [send])
    sent1, sent3, stats = image_side(
        grads, rows, (1, 3), [stats, exchange(stats, 6, 3)], [keep]
    )
    (sent2,) = image_side(grads, rows, (2,), (), [sent1])
    runs = (
        (0, 0, owned, F32),
        (owned, owned, 2 * owned, F32),
        (3 * owned, 4 * owned, 2 * owned, F32),
        (5 * owned, 6 * owned, 2 * owned, F32),
        (7 * owned, 3 * owned, owned, BF16),
    )
    gy, gy1, gy2, gy3, far, stats = text_add(
        keep, hop_core(send), runs, stats, exchange(stats, 5, 5), [sent2]
    )
    parts = [hop_second(g, -k) for k, g in zip((1, 2, 3), (sent1, sent2, sent3))]
    step, stats = step_add(gy3, hop_z(far, -1), [stats, exchange(stats, 1, 1)], [])
    (own,) = image_side(grads, rows, (0,), (), [step])
    step, stats = step_add(gy2, hop_z(step, -1), [stats, exchange(stats, 2, 2)], [own])
    keep, g1, g2, g3, stats = image_add(own, parts, stats, exchange(stats, 7, 4))
    (step,) = step_add(gy1, hop_z(step, -1), [], [keep])
    around = hop_z(step, -1)
    parts = [hop_first(g, -k) for k, g in ((1, g1), (2, g2), (3, g3))]
    text_parts = [(gy, 0), (around, 0), (hop_core(lower(around, parts[2])), 0)]

    stats = stats_sum(stats, parts)
    image_grad, text_grad, mark = finish(
        scale, (images, [(p, 0) for p in [keep] + parts]), (texts, text_parts)
    )
    total = scalars(scale, stats, exchange(stats, 0, 0), batch_all, mark)
    return image_grad, text_grad, total


def solution(mesh):
    spread = P(("row", "col"), None)
    return jax.shard_map(
        shards,
        mesh=mesh,
        in_specs=(spread, spread, P(), P(), P(), P()),
        out_specs=(spread, spread, P()),
        check_vma=False,
    )
```
